256 devices in a mesh: patch: 32 (over x_lo, z, core), tensor: 8 (over y, x_hi).
Axes of the slice: x: 4 (x_hi: 2, x_lo: 2; x = x_hi * 2 + x_lo), y: 4, z: 8, core: 2. Of those that a mesh axis runs over, the one named last changes fastest.
Arguments:
- latents: bfloat16 [8192, 3072], P('patch'), may hold values from -6 to 6
- token_rows: int32 [8192], P('patch'), may hold values from 0 to 8191, each once
- mod_shift: float32 [3072], replicated, may hold values from -3 to 3
- mod_scale: float32 [3072], replicated, may hold values from -2 to 2
- mod_gate: float32 [3072], replicated, may hold values from 0.5 to 2
- w_qkv: bfloat16 [3072, 3, 3072], P(None, None, 'tensor'), may hold values from -0.109375 to 0.109375
- q_gain: float32 [128], replicated, may hold values from 0.5 to 2
- k_gain: float32 [128], replicated, may hold values from 0.5 to 2
- stale_kv: bfloat16 [8192, 2, 3072], P('patch', None, 'tensor'), may hold values from -84 to 84
- text_kv: bfloat16 [512, 2, 3072], P(None, None, 'tensor'), may hold values from -6 to 6
- w_out: bfloat16 [3072, 3072], P('tensor'), may hold values from -0.109375 to 0.109375
- b_out: float32 [3072], replicated, may hold values from -3 to 3
Outputs:
- block_out: bfloat16 [8192, 3072], P('patch')
- fresh_kv: bfloat16 [8192, 2, 3072], P('patch', None, 'tensor')
The draws below stay inside these ranges and needn't reach their ends.
Inputs may be any that keep to these rules, and one draw needn't show every extreme that they name: `token_rows`: each position of the image of 8192 tokens appears once.
All inputs are finite; a program needn't handle non-finite values.
Results may differ from the reference program's by a relative error of at most 0.008.
Values may be sent and summed in bfloat16 or wider, within the bound.
No kernel may reach another device: no remote copies, remote signals or barrier semaphores. Data moves between devices by JAX's collectives and lax.ppermute only.
A program may use at most 192 MiB of HBM per device.

```python
import jax
import jax.numpy as jnp
from jax import lax

D = 3072
HEADS = 24
HEAD = 128
TEXT = 512
WIDTH_TOK = 256
TOK_DEV = 256
TOKENS = 8192
N_PATCH = 32


def draw_stale_kv(key, part):
    key = jax.random.fold_in(key, 17)
    noise_key = jax.random.fold_in(key, 0)
    width = HEADS * HEAD
    base = jnp.clip(jax.random.normal(noise_key, (TOKENS, 2, width), jnp.float32), -6.0, 6.0)
    return base.astype(jnp.bfloat16)


def level_of(stream_key, extent, pieces, smallest, high):
    loudness, own = 1.0, jax.random.fold_in(stream_key, 6)
    for axis_at, blocks in pieces:
        steps = jnp.exp(jax.random.uniform(jax.random.fold_in(own, axis_at), (blocks,), jnp.float32, smallest / len(pieces), high / len(pieces)))
        loudness = loudness * jnp.repeat(steps, extent[axis_at] // blocks).reshape([-1 if axis == axis_at else 1 for axis in range(len(extent))])
    return loudness


def scatter_about(key, dims, scale, most, cuts=(), dtype=jnp.bfloat16):
    factor_of = level_of(key, dims, cuts, -0.22, 0.18) if cuts else 1.0
    drawn = jax.random.normal(key, dims, jnp.float32) * scale * factor_of
    return jnp.minimum(jnp.maximum(drawn, -most), most).astype(dtype)


def setup_inputs(seed: int = 0) -> dict:
    arg_keys = jax.random.split(jax.random.key(seed), 13)
    latents = scatter_about(arg_keys[0], (TOKENS, D), 1.0, 6.0, ((0, 32),))
    token_rows = jax.random.permutation(arg_keys[1], TOKENS).astype(jnp.int32)
    mod_shift = scatter_about(arg_keys[2], (D,), 0.5, 3.0, (), jnp.float32)
    mod_scale = scatter_about(arg_keys[3], (D,), 0.4, 2.0, (), jnp.float32)
    mod_gate = jnp.clip(jax.random.uniform(arg_keys[4], (D,), jnp.float32, 0.5, 2.0), 0.5, 2.0)
    w_qkv = scatter_about(arg_keys[5], (D, 3, HEADS * HEAD), D ** -0.5, 0.109375, ((2, 8),))
    q_gain = jnp.clip(jax.random.uniform(arg_keys[6], (HEAD,), jnp.float32, 0.5, 2.0), 0.5, 2.0)
    k_gain = jnp.clip(jax.random.uniform(arg_keys[7], (HEAD,), jnp.float32, 0.5, 2.0), 0.5, 2.0)
    stale_kv = draw_stale_kv(jax.random.fold_in(arg_keys[12], 71), 0)
    text_kv = scatter_about(arg_keys[9], (TEXT, 2, HEADS * HEAD), 1.0, 6.0, ((2, 8),))
    w_out = scatter_about(arg_keys[10], (HEADS * HEAD, D), (HEADS * HEAD) ** -0.5, 0.109375, ((0, 8),))
    b_out = scatter_about(arg_keys[11], (D,), 0.5, 3.0, (), jnp.float32)
    return {"latents": latents, "token_rows": token_rows, "mod_shift": mod_shift, "mod_scale": mod_scale, "mod_gate": mod_gate, "w_qkv": w_qkv, "q_gain": q_gain, "k_gain": k_gain, "stale_kv": stale_kv, "text_kv": text_kv, "w_out": w_out, "b_out": b_out}


def rope_tables(rows):
    row_pos = (rows // WIDTH_TOK).astype(jnp.float32)
    col_pos = (rows % WIDTH_TOK).astype(jnp.float32)
    steps = jnp.arange(28).astype(jnp.float32)
    omega = 10000.0 ** (-2.0 * steps / 56.0)
    angles = jnp.concatenate([jnp.zeros((rows.shape[0], 8), jnp.float32), row_pos[:, None] * omega[None, :], col_pos[:, None] * omega[None, :]], axis=1)
    return (jnp.cos(angles), jnp.sin(angles))

def rotate(values, cosine, sine):
    count, heads, size = values.shape
    pairs = values.reshape(count, heads, size // 2, 2)
    first = pairs[..., 0]
    second = pairs[..., 1]
    cosine = cosine[:, None, :]
    sine = sine[:, None, :]
    out_first = first * cosine - second * sine
    out_second = first * sine + second * cosine
    return jnp.stack([out_first, out_second], axis=-1).reshape(count, heads, size)

def norm_head(values, gain):
    return values * lax.rsqrt(lax.optimization_barrier(jnp.mean(values * values, axis=-1, keepdims=True)) + 1e-06) * gain

def prepare(latents, rows, mod_shift, mod_scale, w_qkv, q_gain, k_gain):
    inputs = latents.astype(jnp.float32)
    centred = inputs - lax.optimization_barrier(jnp.mean(inputs, axis=-1, keepdims=True))
    spread = lax.optimization_barrier(jnp.mean(centred * centred, axis=-1, keepdims=True))
    normed = (centred * lax.rsqrt(spread + 1e-06) * (1.0 + mod_scale) + mod_shift).astype(jnp.bfloat16)
    count = inputs.shape[0]
    width = w_qkv.shape[2]
    heads = width // 128
    qkv = jnp.dot(normed, w_qkv.reshape(w_qkv.shape[0], 3 * width), preferred_element_type=jnp.float32)
    qkv = qkv.reshape(count, 3, heads, 128)
    cosine, sine = rope_tables(rows)
    query = rotate(norm_head(qkv[:, 0], q_gain), cosine, sine).astype(jnp.bfloat16).reshape(count, width)
    keys = rotate(norm_head(qkv[:, 1], k_gain), cosine, sine).astype(jnp.bfloat16).reshape(count, width)
    values = qkv[:, 2].astype(jnp.bfloat16).reshape(count, width)
    return (inputs, query, keys, values)

def scores(left, right):
    return lax.dot_general(left, right, (((1,), (1,)), ((), ())), preferred_element_type=jnp.float32)

def reference(latents, token_rows, mod_shift, mod_scale, mod_gate, w_qkv, q_gain, k_gain, stale_kv, text_kv, w_out, b_out):
    inputs, query, keys, values = prepare(latents, token_rows, mod_shift, mod_scale, w_qkv, q_gain, k_gain)
    fresh_kv = jnp.stack([keys, values], axis=1)
    factor = 1.0 / HEAD ** 0.5

    def one_head(head):
        offset = head * HEAD
        q_head = lax.dynamic_slice_in_dim(query, offset, HEAD, 1)
        k_head = lax.dynamic_slice_in_dim(keys, offset, HEAD, 1)
        v_head = lax.dynamic_slice_in_dim(values, offset, HEAD, 1)
        stale_k = lax.dynamic_slice_in_dim(stale_kv[:, 0], offset, HEAD, 1)
        stale_v = lax.dynamic_slice_in_dim(stale_kv[:, 1], offset, HEAD, 1)
        text_k = lax.dynamic_slice_in_dim(text_kv[:, 0], offset, HEAD, 1)
        text_v = lax.dynamic_slice_in_dim(text_kv[:, 1], offset, HEAD, 1)

        def one_block(block):
            start = (block * TOK_DEV).astype(jnp.int32)
            anchor = (start, jnp.zeros((), jnp.int32))
            block_k = lax.dynamic_update_slice(stale_k, lax.dynamic_slice_in_dim(k_head, start, TOK_DEV, 0), anchor)
            block_v = lax.dynamic_update_slice(stale_v, lax.dynamic_slice_in_dim(v_head, start, TOK_DEV, 0), anchor)
            all_k = jnp.concatenate([text_k, block_k], axis=0)
            all_v = jnp.concatenate([text_v, block_v], axis=0)
            q_block = lax.dynamic_slice_in_dim(q_head, start, TOK_DEV, 0)
            logits = scores(q_block, all_k) * factor
            largest = lax.optimization_barrier(jnp.max(logits, axis=1, keepdims=True))
            weights = jnp.exp(logits - largest)
            total = lax.optimization_barrier(jnp.sum(weights, axis=1, keepdims=True))
            weighted = jnp.dot(weights.astype(jnp.bfloat16), all_v, preferred_element_type=jnp.float32)
            return weighted / total
        blocks = lax.map(one_block, jnp.arange(N_PATCH).astype(jnp.int32))
        return blocks.reshape(TOKENS, HEAD)
    heads_out = lax.map(one_head, jnp.arange(HEADS).astype(jnp.int32))
    attn = jnp.transpose(heads_out, (1, 0, 2)).reshape(TOKENS, HEADS * HEAD).astype(jnp.bfloat16)
    projected = jnp.dot(attn, w_out, preferred_element_type=jnp.float32)
    block_out = (inputs + mod_gate * (projected + b_out)).astype(jnp.bfloat16)
    return (block_out, fresh_kv)
```

```python
import jax
import jax.numpy as jnp
import numpy as np
from jax import lax
from jax.experimental import pallas as pl
from jax.experimental.pallas import tpu as pltpu
from jax.sharding import Mesh
from jax.sharding import PartitionSpec as P

WIDTH_TOK = 256
HEAD = 128
LOCAL_HEADS = 3
WIDTH = HEAD * LOCAL_HEADS
COUNT = 256
TEXT = 512
MODEL = 3072
ROWS = COUNT // 8
AXES = ("x_lo", "z", "core", "y", "x_hi")
SIZES = (2, 8, 2, 4, 2)
PATCH = ("x_lo", "z", "core")
TENSOR = ("y", "x_hi")
SCALE = float(np.log2(np.e) / np.sqrt(128.0))
MIB = 1024 * 1024
HOPS = [(0, 0), (2, 1), (2, 0), (1, 1), (3, 1), (1, 0), (3, 0), (0, 1)]
FULL = pl.BlockSpec(memory_space=pltpu.VMEM)
SMEM = pl.BlockSpec(memory_space=pltpu.SMEM)


def params(mib=48):
    return pltpu.CompilerParams(vmem_limit_bytes=mib * MIB)


def cost(flops, nbytes, exps=0):
    return pl.CostEstimate(flops=flops, bytes_accessed=nbytes, transcendentals=exps)


def head_of(head):
    return slice(head * HEAD, (head + 1) * HEAD)


def qkv_kernel(lat, shift, scale, w, q_gain, k_gain, cosine, sine, q, k, v, normed):
    part = pl.program_id(0)

    @pl.when(part == 0)
    def _():
        x = lat[...].astype(jnp.float32)
        centred = x - jnp.mean(x, axis=-1, keepdims=True)
        spread = jnp.mean(centred * centred, axis=-1, keepdims=True)
        y = centred * lax.rsqrt(spread + 1e-06) * (1.0 + scale[...]) + shift[...]
        normed[...] = y.astype(jnp.bfloat16)

    out = jnp.dot(normed[...], w[0], preferred_element_type=jnp.float32)

    def rotated(gain):
        even = lax.broadcasted_iota(jnp.int32, (COUNT, HEAD), 1) % 2 == 0
        heads = []
        for head in range(LOCAL_HEADS):
            x = out[:, head_of(head)]
            x = x * lax.rsqrt(jnp.mean(x * x, axis=-1, keepdims=True) + 1e-06) * gain[...]
            other = jnp.where(even, pltpu.roll(x, HEAD - 1, 1), pltpu.roll(x, 1, 1))
            heads.append((x * cosine[...] + other * sine[...]).astype(jnp.bfloat16))
        return jnp.concatenate(heads, axis=1)

    @pl.when(part == 0)
    def _():
        q[...] = rotated(q_gain)

    @pl.when(part == 1)
    def _():
        k[...] = rotated(k_gain)

    @pl.when(part == 2)
    def _():
        v[...] = out.astype(jnp.bfloat16)


def qkv_call(latents, shift, scale, w, q_gain, k_gain, cosine, sine):
    whole = lambda shape: pl.BlockSpec(shape, lambda i: (0,) * len(shape))
    piece = jax.ShapeDtypeStruct((COUNT, WIDTH), jnp.bfloat16)
    return pl.pallas_call(
        qkv_kernel,
        grid=(3,),
        in_specs=[
            whole((COUNT, MODEL)),
            whole((1, MODEL)),
            whole((1, MODEL)),
            pl.BlockSpec((1, MODEL, WIDTH), lambda i: (i, 0, 0)),
            whole((1, HEAD)),
            whole((1, HEAD)),
            whole((COUNT, HEAD)),
            whole((COUNT, HEAD)),
        ],
        out_specs=[whole((COUNT, WIDTH))] * 3,
        out_shape=[piece] * 3,
        scratch_shapes=[pltpu.VMEM((COUNT, MODEL), jnp.bfloat16)],
        compiler_params=params(),
        cost_estimate=cost(2 * COUNT * MODEL * WIDTH * 3, 10 * MIB),
    )(
        latents,
        shift.reshape(1, MODEL),
        scale.reshape(1, MODEL),
        w,
        q_gain.reshape(1, HEAD),
        k_gain.reshape(1, HEAD),
        cosine,
        sine,
    )


def pick(values):
    rows = values[0].shape[0]
    lane = lax.broadcasted_iota(jnp.int32, (rows, HEAD), 1)
    out = jnp.zeros((rows, HEAD), jnp.float32)
    for at, value in enumerate(values):
        out = jnp.where(lane == at, value, out)
    return out


def attend(q, pairs, state):
    scores = [
        lax.dot_general(q, k, (((1,), (1,)), ((), ())), preferred_element_type=jnp.float32) * SCALE
        for k, _ in pairs
    ]
    most = scores[0]
    for s in scores[1:]:
        most = jnp.maximum(most, s)
    top = jnp.max(most, axis=1, keepdims=True)
    if state is not None:
        top = jnp.maximum(top, state[1])
    total = None
    for s, (_, v) in zip(scores, pairs):
        p = jnp.exp2(s - top).astype(jnp.bfloat16)
        wide = jnp.concatenate([v, jnp.ones_like(v)], axis=1)
        part = jnp.dot(p, wide, preferred_element_type=jnp.float32)
        total = part if total is None else total + part
    num, den = total[:, :HEAD], total[:, HEAD : HEAD + 1]
    if state is not None:
        keep = jnp.exp2(state[1] - top)
        num, den = num + keep * state[0], den + keep * state[2]
    return num, top, den


def store_state(num, ml, results):
    for head, result in enumerate(results):
        num[0, :, head_of(head)] = result[0]
    ml[0] = pick([r[1] for r in results] + [r[2] for r in results])


def load_state(num, ml):
    stats = ml[0]
    return [
        (num[0, :, head_of(h)], stats[:, h : h + 1], stats[:, LOCAL_HEADS + h : LOCAL_HEADS + h + 1])
        for h in range(LOCAL_HEADS)
    ]


def first_kernel(q, k, v, text, own, num, ml):
    def run(pairs_of):
        results = []
        for head in range(LOCAL_HEADS):
            cols = head_of(head)
            results.append(attend(q[0, :, cols], pairs_of(cols), None))
        store_state(num, ml, results)

    @pl.when(pl.program_id(0) == 0)
    def _():
        run(
            lambda c: [
                (k[:, c], v[:, c]),
                (text[0, :COUNT, c], text[1, :COUNT, c]),
                (text[0, COUNT:, c], text[1, COUNT:, c]),
            ]
        )

    @pl.when(pl.program_id(0) != 0)
    def _():
        run(lambda c: [(own[0, :, c], own[1, :, c])])


def whole_spec(shape):
    return pl.BlockSpec(shape, lambda i: (0,) * len(shape))


def at_spec(shape, offset=0):
    return pl.BlockSpec((1, *shape), lambda i: (i + offset, 0, 0))


def state_shapes(blocks):
    return [
        jax.ShapeDtypeStruct((blocks, COUNT, WIDTH), jnp.float32),
        jax.ShapeDtypeStruct((blocks, COUNT, HEAD), jnp.float32),
    ]


def attend_cost(blocks):
    return cost(blocks * COUNT * COUNT * WIDTH * 4, 6 * MIB, blocks * COUNT * COUNT * LOCAL_HEADS)


def first_call(qs, k, v, text, own):
    return pl.pallas_call(
        first_kernel,
        grid=(4,),
        in_specs=[
            at_spec((COUNT, WIDTH)),
            whole_spec((COUNT, WIDTH)),
            whole_spec((COUNT, WIDTH)),
            whole_spec((2, TEXT, WIDTH)),
            whole_spec((2, COUNT, WIDTH)),
        ],
        out_specs=[at_spec((COUNT, WIDTH)), at_spec((COUNT, HEAD))],
        out_shape=state_shapes(4),
        compiler_params=params(),
        cost_estimate=attend_cost(6),
    )(qs, k, v, text, own)


def next_kernel(q, left, right, num_in, ml_in, num, ml):
    states = load_state(num_in, ml_in)
    results = []
    for head in range(LOCAL_HEADS):
        c = head_of(head)
        pairs = [(left[0, :, c], left[1, :, c]), (right[0, :, c], right[1, :, c])]
        results.append(attend(q[0, :, c], pairs, states[head]))
    store_state(num, ml, results)


def next_call(qs, left, right, num, ml):
    return pl.pallas_call(
        next_kernel,
        grid=(4,),
        in_specs=[
            at_spec((COUNT, WIDTH)),
            whole_spec((2, COUNT, WIDTH)),
            whole_spec((2, COUNT, WIDTH)),
            at_spec((COUNT, WIDTH)),
            at_spec((COUNT, HEAD)),
        ],
        out_specs=[at_spec((COUNT, WIDTH)), at_spec((COUNT, HEAD))],
        out_shape=state_shapes(4),
        compiler_params=params(),
        cost_estimate=attend_cost(8),
    )(qs, left, right, num, ml)


def pack_message(message, results):
    logs = []
    for head, (num, top, den) in enumerate(results):
        message[:, head_of(head)] = (num / den).astype(jnp.bfloat16)
        logs.append(top + jnp.log2(den))
    parts = []
    for _ in range(3):
        rounded = [x.astype(jnp.bfloat16).astype(jnp.float32) for x in logs]
        parts += rounded
        logs = [x - r for x, r in zip(logs, rounded)]
    message[:, WIDTH:] = pick(parts).astype(jnp.bfloat16)


def open_message(message):
    stats = message[:, WIDTH:].astype(jnp.float32)
    out = []
    for h in range(LOCAL_HEADS):
        log = sum(
            stats[:, n * LOCAL_HEADS + h : n * LOCAL_HEADS + h + 1] for n in (1, 2)
        ) + stats[:, h : h + 1]
        out.append((message[:, head_of(h)].astype(jnp.float32), log, 1.0))
    return out


def merge(states):
    top = states[0][1]
    for s in states[1:]:
        top = jnp.maximum(top, s[1])
    num, den = 0.0, 0.0
    for n, m, d in states:
        keep = jnp.exp2(m - top)
        num, den = num + keep * n, den + keep * d
    return num, top, den


def last_kernel(q, keys, values, num_in, ml_in, num, ml, message):
    states = load_state(num_in, ml_in)
    results = []
    for head in range(LOCAL_HEADS):
        c = head_of(head)
        results.append(attend(q[0, :, c], [(keys[:, c], values[:, c])], states[head]))

    @pl.when(pl.program_id(0) == 0)
    def _():
        store_state(num, ml, results)

    @pl.when(pl.program_id(0) == 1)
    def _():
        pack_message(message, results)


def last_call(qs, keys, values, num, ml, offset):
    return pl.pallas_call(
        last_kernel,
        grid=(2,),
        in_specs=[
            at_spec((COUNT, WIDTH), offset),
            whole_spec((COUNT, WIDTH)),
            whole_spec((COUNT, WIDTH)),
            at_spec((COUNT, WIDTH), offset),
            at_spec((COUNT, HEAD), offset),
        ],
        out_specs=[
            whole_spec((1, COUNT, WIDTH)),
            whole_spec((1, COUNT, HEAD)),
            whole_spec((COUNT, WIDTH + HEAD)),
        ],
        out_shape=state_shapes(1) + [jax.ShapeDtypeStruct((COUNT, WIDTH + HEAD), jnp.bfloat16)],
        compiler_params=params(),
        cost_estimate=attend_cost(2),
    )(qs, keys, values, num, ml)


def merge_kernel(num, ml, message, out):
    mine, other = load_state(num, ml), open_message(message)
    pack_message(out, [merge([a, b]) for a, b in zip(mine, other)])


def merge_call(num, ml, message):
    return pl.pallas_call(
        merge_kernel,
        in_specs=[FULL] * 3,
        out_specs=FULL,
        out_shape=jax.ShapeDtypeStruct((COUNT, WIDTH + HEAD), jnp.bfloat16),
        compiler_params=params(),
        cost_estimate=cost(0, 2 * MIB),
    )(num, ml, message)


def project_kernel(place, num, ml, near, far, w, *rest):
    outs, attn, full = rest[:8], rest[8], rest[9]
    triples = zip(load_state(num, ml), open_message(near), open_message(far))
    for head, states in enumerate(triples):
        total, _, den = merge(states)
        attn[:, head_of(head)] = (total / den).astype(jnp.bfloat16)
    for at in range(0, MODEL, 768):
        full[:, at : at + 768] = jnp.dot(
            attn[...], w[:, at : at + 768], preferred_element_type=jnp.float32
        ).astype(jnp.bfloat16)
    for n in range(8):
        outs[n][...] = full[pl.ds(pl.multiple_of(place[n] * ROWS, ROWS), ROWS), :]


def project_call(place, num, ml, near, far, w):
    return pl.pallas_call(
        project_kernel,
        in_specs=[SMEM] + [FULL] * 5,
        out_specs=[FULL] * 8,
        out_shape=[jax.ShapeDtypeStruct((ROWS, MODEL), jnp.bfloat16)] * 8,
        scratch_shapes=[
            pltpu.VMEM((COUNT, WIDTH), jnp.bfloat16),
            pltpu.VMEM((COUNT, MODEL), jnp.bfloat16),
        ],
        compiler_params=params(),
        cost_estimate=cost(2 * COUNT * WIDTH * MODEL, 5 * MIB),
    )(place, num, ml, near, far, w)


def gather_kernel(place, *refs):
    out = refs[8]
    for n in range(8):
        out[pl.ds(pl.multiple_of(place[n] * ROWS, ROWS), ROWS), :] = refs[n][...]


def gather_call(place, pieces):
    return pl.pallas_call(
        gather_kernel,
        in_specs=[SMEM] + [FULL] * 8,
        out_specs=FULL,
        out_shape=jax.ShapeDtypeStruct((COUNT, MODEL), jnp.bfloat16),
        compiler_params=params(),
        cost_estimate=cost(0, 4 * MIB),
    )(place, *pieces)


def ring(value, axis, step):
    size = SIZES[AXES.index(axis)]
    return lax.ppermute(value, axis, [(i, (i + step) % size) for i in range(size)])


def across(value, dy, dx):
    pairs = [(y * 2 + x, (y + dy) % 4 * 2 + (x ^ dx)) for y in range(4) for x in range(2)]
    return lax.ppermute(value, TENSOR, pairs)


def tables(rows):
    row_pos = (rows // WIDTH_TOK).astype(jnp.float32)
    col_pos = (rows % WIDTH_TOK).astype(jnp.float32)
    omega = 10000.0 ** (-2.0 * np.arange(28) / 56.0)
    by_row = np.repeat(np.concatenate([np.zeros(8), omega, np.zeros(28)]), 2).astype(np.float32)
    by_col = np.repeat(np.concatenate([np.zeros(36), omega]), 2).astype(np.float32)
    angles = row_pos[:, None] * by_row[None, :] + col_pos[:, None] * by_col[None, :]
    sign = np.tile(np.array([-1.0, 1.0], np.float32), HEAD // 2)
    return jnp.cos(angles), jnp.sin(angles) * sign[None, :]


def shards(
    latents,
    token_rows,
    mod_shift,
    mod_scale,
    mod_gate,
    w_qkv,
    q_gain,
    k_gain,
    stale_kv,
    text_kv,
    w_out,
    b_out,
):
    own = jnp.transpose(stale_kv, (1, 0, 2))
    right, left = [ring(own, "z", 1)], [ring(own, "z", -1)]
    cosine, sine = tables(token_rows)
    q, k, v = qkv_call(
        latents, mod_shift, mod_scale, jnp.transpose(w_qkv, (1, 0, 2)), q_gain, k_gain, cosine, sine
    )
    q_core = ring(q, "core", 1)
    q_x = ring(q, "x_lo", 1)
    q_both = lax.ppermute(q, ("x_lo", "core"), [(0, 3), (1, 2), (2, 1), (3, 0)])
    fresh_kv = jnp.stack([k, v], axis=1)
    text = jnp.transpose(text_kv, (1, 0, 2))
    qs = jnp.stack([q, q_core, q_x, q_both])
    for _ in range(2):
        right.append(ring(right[-1], "z", 1))
        left.append(ring(left[-1], "z", -1))
    far_k = ring(right[-1][0], "z", 1)
    far_v = ring(left[-1][1], "z", -1)

    num, ml = first_call(qs, k, v, text, own)
    for r, l in zip(right, left):
        num, ml = next_call(qs, r, l, num, ml)

    x_num, x_ml, x_msg = last_call(qs, far_k, far_v, num, ml, 2)
    x_msg = ring(x_msg, "core", 1)
    x_out = ring(merge_call(x_num, x_ml, x_msg), "x_lo", 1)
    o_num, o_ml, o_msg = last_call(qs, far_k, far_v, num, ml, 0)
    o_msg = ring(o_msg, "core", 1)

    y, x = lax.axis_index("y"), lax.axis_index("x_hi")
    to = jnp.stack([(y + dy) % 4 * 2 + (x + dx) % 2 for dy, dx in HOPS]).astype(jnp.int32)
    come = jnp.stack([(y - dy) % 4 * 2 + (x + dx) % 2 for dy, dx in HOPS]).astype(jnp.int32)
    parts = project_call(to, o_num, o_ml, o_msg, x_out, w_out)
    parts = [parts[0]] + [across(p, dy, dx) for p, (dy, dx) in zip(parts[1:], HOPS[1:])]
    mine = lax.dynamic_slice_in_dim(latents, to[0] * ROWS, ROWS, 0).astype(jnp.float32)
    total = parts[0].astype(jnp.float32)
    for p in parts[1:]:
        total = total + p.astype(jnp.float32)
    piece = (mine + mod_gate * (total + b_out)).astype(jnp.bfloat16)
    pieces = [piece] + [across(piece, dy, dx) for dy, dx in HOPS[1:]]
    return (gather_call(come, pieces), fresh_kv)


def solution(mesh):
    fine = Mesh(mesh.devices.reshape(SIZES), AXES)
    return jax.shard_map(
        shards,
        mesh=fine,
        in_specs=(
            P(PATCH, None),
            P(PATCH),
            P(),
            P(),
            P(),
            P(None, None, TENSOR),
            P(),
            P(),
            P(PATCH, None, TENSOR),
            P(None, None, TENSOR),
            P(TENSOR, None),
            P(),
        ),
        out_specs=(P(PATCH, None), P(PATCH, None, TENSOR)),
        check_vma=False,
    )
```

```python
import jax
import jax.numpy as jnp
import numpy as np
from jax import lax
from jax.experimental import pallas as pl
from jax.experimental.pallas import tpu as pltpu
from jax.sharding import Mesh
from jax.sharding import PartitionSpec as P

WIDTH_TOK = 256
HEAD = 128
LOCAL_HEADS = 3
WIDTH = HEAD * LOCAL_HEADS
COUNT = 256
TEXT = 512
MODEL = 3072
ROWS = COUNT // 8
AXES = ("x_lo", "z", "core", "y", "x_hi")
SIZES = (2, 8, 2, 4, 2)
PATCH = ("x_lo", "z", "core")
TENSOR = ("y", "x_hi")
SCALE = float(np.log2(np.e) / np.sqrt(128.0))
MIB = 1024 * 1024
EXTRA = 16
HALF = COUNT // 2
SPLIT = WIDTH // 2
FULL = pl.BlockSpec(memory_space=pltpu.VMEM)
SMEM = pl.BlockSpec(memory_space=pltpu.SMEM)


def params(mib=48):
    return pltpu.CompilerParams(vmem_limit_bytes=mib * MIB)


def cost(flops, nbytes, exps=0):
    return pl.CostEstimate(flops=flops, bytes_accessed=nbytes, transcendentals=exps)


def head_of(head):
    return slice(head * HEAD, (head + 1) * HEAD)


def qkv_kernel(lat, shift, scale, w, q_gain, k_gain, cosine, sine, q, k, v, normed):
    part = pl.program_id(0)

    @pl.when(part == 0)
    def _():
        x = lat[...].astype(jnp.float32)
        centred = x - jnp.mean(x, axis=-1, keepdims=True)
        spread = jnp.mean(centred * centred, axis=-1, keepdims=True)
        y = centred * lax.rsqrt(spread + 1e-06) * (1.0 + scale[...]) + shift[...]
        normed[...] = y.astype(jnp.bfloat16)

    out = jnp.dot(normed[...], w[0], preferred_element_type=jnp.float32)

    def rotated(gain):
        even = lax.broadcasted_iota(jnp.int32, (COUNT, HEAD), 1) % 2 == 0
        heads = []
        for head in range(LOCAL_HEADS):
            x = out[:, head_of(head)]
            x = x * lax.rsqrt(jnp.mean(x * x, axis=-1, keepdims=True) + 1e-06) * gain[...]
            other = jnp.where(even, pltpu.roll(x, HEAD - 1, 1), pltpu.roll(x, 1, 1))
            heads.append(x * cosine[...] + other * sine[...])
        return heads

    @pl.when(part == 0)
    def _():
        for head, x in enumerate(rotated(q_gain)):
            q[head_of(head), :] = (x * SCALE).T.astype(jnp.bfloat16)

    @pl.when(part == 1)
    def _():
        for head, x in enumerate(rotated(k_gain)):
            k[:, head_of(head)] = x.astype(jnp.bfloat16)

    @pl.when(part == 2)
    def _():
        v[...] = out.astype(jnp.bfloat16)


def whole_spec(shape):
    return pl.BlockSpec(shape, lambda i: (0,) * len(shape))


def at_spec(shape, offset=0):
    return pl.BlockSpec((1, *shape), lambda i: (i + offset, 0, 0))


def qkv_call(latents, shift, scale, w, q_gain, k_gain, cosine, sine):
    shape = lambda *dims: jax.ShapeDtypeStruct(dims, jnp.bfloat16)
    return pl.pallas_call(
        qkv_kernel,
        grid=(3,),
        in_specs=[
            whole_spec((COUNT, MODEL)),
            whole_spec((1, MODEL)),
            whole_spec((1, MODEL)),
            pl.BlockSpec((1, MODEL, WIDTH), lambda i: (i, 0, 0)),
            whole_spec((1, HEAD)),
            whole_spec((1, HEAD)),
            whole_spec((COUNT, HEAD)),
            whole_spec((COUNT, HEAD)),
        ],
        out_specs=[whole_spec((WIDTH, COUNT)), whole_spec((COUNT, WIDTH)), whole_spec((COUNT, WIDTH))],
        out_shape=[shape(WIDTH, COUNT), shape(COUNT, WIDTH), shape(COUNT, WIDTH)],
        scratch_shapes=[pltpu.VMEM((COUNT, MODEL), jnp.bfloat16)],
        compiler_params=params(60),
        cost_estimate=cost(2 * COUNT * MODEL * WIDTH * 3, 10 * MIB),
    )(
        latents,
        shift.reshape(1, MODEL),
        scale.reshape(1, MODEL),
        w,
        q_gain.reshape(1, HEAD),
        k_gain.reshape(1, HEAD),
        cosine,
        sine,
    )


def pick(values, rows):
    at = lax.broadcasted_iota(jnp.int32, (rows, COUNT), 0)
    out = jnp.zeros((rows, COUNT), jnp.float32)
    for n, value in enumerate(values):
        out = jnp.where(at == n, value, out)
    return out


def attend(q, pairs, state):
    scores = [jnp.dot(k, q, preferred_element_type=jnp.float32) for k, _ in pairs]
    top = jnp.max(scores[0], axis=0, keepdims=True)
    for s in scores[1:]:
        top = jnp.maximum(top, jnp.max(s, axis=0, keepdims=True))
    if state is not None:
        top = jnp.maximum(top, state[1])
    num, den = None, None
    for s, (_, v) in zip(scores, pairs):
        p = jnp.exp2(s - top)
        total = jnp.sum(p, axis=0, keepdims=True)
        part = lax.dot_general(
            v, p.astype(jnp.bfloat16), (((0,), (0,)), ((), ())), preferred_element_type=jnp.float32
        )
        num = part if num is None else num + part
        den = total if den is None else den + total
    if state is not None:
        keep = jnp.exp2(state[1] - top)
        num, den = num + keep * state[0], den + keep * state[2]
    return num, top, den


def store_state(num, ml, results):
    for head, result in enumerate(results):
        num[0, head_of(head), :] = result[0]
    ml[0] = pick([r[1] for r in results] + [r[2] for r in results], 8)


def load_state(num, ml):
    return [
        (num[0, head_of(h), :], ml[0, h : h + 1, :], ml[0, LOCAL_HEADS + h : LOCAL_HEADS + h + 1, :])
        for h in range(LOCAL_HEADS)
    ]


def first_kernel(q, k, v, text, own, num, ml):
    def run(pairs_of):
        results = []
        for head in range(LOCAL_HEADS):
            cols = head_of(head)
            results.append(attend(q[0, cols, :], pairs_of(cols), None))
        store_state(num, ml, results)

    @pl.when(pl.program_id(0) == 0)
    def _():
        run(lambda c: [(k[:, c], v[:, c]), (text[0, :, c], text[1, :, c])])

    @pl.when(pl.program_id(0) != 0)
    def _():
        run(lambda c: [(own[0, :, c], own[1, :, c])])


def state_shapes(blocks):
    return [
        jax.ShapeDtypeStruct((blocks, WIDTH, COUNT), jnp.float32),
        jax.ShapeDtypeStruct((blocks, 8, COUNT), jnp.float32),
    ]


def attend_cost(blocks):
    return cost(blocks * COUNT * COUNT * WIDTH * 4, 6 * MIB, blocks * COUNT * COUNT * LOCAL_HEADS)


def first_call(qs, k, v, text, own):
    return pl.pallas_call(
        first_kernel,
        grid=(4,),
        in_specs=[
            at_spec((WIDTH, COUNT)),
            whole_spec((COUNT, WIDTH)),
            whole_spec((COUNT, WIDTH)),
            whole_spec((2, TEXT, WIDTH)),
            whole_spec((2, COUNT, WIDTH)),
        ],
        out_specs=[at_spec((WIDTH, COUNT)), at_spec((8, COUNT))],
        out_shape=state_shapes(4),
        compiler_params=params(),
        cost_estimate=attend_cost(6),
    )(qs, k, v, text, own)


def next_kernel(q, left, right, num_in, ml_in, num, ml):
    states = load_state(num_in, ml_in)
    results = []
    for head in range(LOCAL_HEADS):
        c = head_of(head)
        pairs = [(left[0, :, c], left[1, :, c]), (right[0, :, c], right[1, :, c])]
        results.append(attend(q[0, c, :], pairs, states[head]))
    store_state(num, ml, results)


def next_call(qs, left, right, num, ml):
    return pl.pallas_call(
        next_kernel,
        grid=(4,),
        in_specs=[
            at_spec((WIDTH, COUNT)),
            whole_spec((2, COUNT, WIDTH)),
            whole_spec((2, COUNT, WIDTH)),
            at_spec((WIDTH, COUNT)),
            at_spec((8, COUNT)),
        ],
        out_specs=[at_spec((WIDTH, COUNT)), at_spec((8, COUNT))],
        out_shape=state_shapes(4),
        compiler_params=params(),
        cost_estimate=attend_cost(8),
    )(qs, left, right, num, ml)


def pack_message(message, results):
    logs = []
    for head, (num, top, den) in enumerate(results):
        message[head_of(head), :] = (num * (1.0 / den)).astype(jnp.bfloat16)
        logs.append(top + jnp.log2(den))
    parts = []
    for _ in range(3):
        rounded = [x.astype(jnp.bfloat16).astype(jnp.float32) for x in logs]
        parts += rounded
        logs = [x - r for x, r in zip(logs, rounded)]
    message[WIDTH:, :] = pick(parts, EXTRA).astype(jnp.bfloat16)


def open_message(message):
    stats = message[WIDTH:, :].astype(jnp.float32)
    row = lambda n: stats[n : n + 1, :]
    return [
        (message[head_of(h), :].astype(jnp.float32), row(h) + (row(h + 3) + row(h + 6)), 1.0)
        for h in range(LOCAL_HEADS)
    ]


def merge(states):
    top = states[0][1]
    for s in states[1:]:
        top = jnp.maximum(top, s[1])
    num, den = 0.0, 0.0
    for n, m, d in states:
        keep = jnp.exp2(m - top)
        num, den = num + keep * n, den + keep * d
    return num, top, den


def last_kernel(q, keys, values, num_in, ml_in, num, ml, message):
    states = load_state(num_in, ml_in)
    results = []
    for head in range(LOCAL_HEADS):
        c = head_of(head)
        results.append(attend(q[0, c, :], [(keys[:, c], values[:, c])], states[head]))

    @pl.when(pl.program_id(0) == 0)
    def _():
        pack_message(message, results)

    @pl.when(pl.program_id(0) == 1)
    def _():
        store_state(num, ml, results)


def last_call(qs, keys, values, num, ml, offset):
    back = lambda shape: pl.BlockSpec((1, *shape), lambda i: (offset + 1 - i, 0, 0))
    message = (WIDTH + EXTRA, COUNT)
    return pl.pallas_call(
        last_kernel,
        grid=(2,),
        in_specs=[
            back((WIDTH, COUNT)),
            whole_spec((COUNT, WIDTH)),
            whole_spec((COUNT, WIDTH)),
            back((WIDTH, COUNT)),
            back((8, COUNT)),
        ],
        out_specs=[
            whole_spec((1, WIDTH, COUNT)),
            whole_spec((1, 8, COUNT)),
            whole_spec(message),
        ],
        out_shape=state_shapes(1) + [jax.ShapeDtypeStruct(message, jnp.bfloat16)],
        compiler_params=params(),
        cost_estimate=attend_cost(2),
    )(qs, keys, values, num, ml)


def merge_kernel(num, ml, message, out):
    mine, other = load_state(num, ml), open_message(message)
    pack_message(out, [merge([a, b]) for a, b in zip(mine, other)])


def merge_call(num, ml, message):
    return pl.pallas_call(
        merge_kernel,
        in_specs=[FULL] * 3,
        out_specs=FULL,
        out_shape=jax.ShapeDtypeStruct((WIDTH + EXTRA, COUNT), jnp.bfloat16),
        compiler_params=params(),
        cost_estimate=cost(0, 2 * MIB),
    )(num, ml, message)


def settle_kernel(place, num, ml, near, far, kept, sent, attn):
    triples = zip(load_state(num, ml), open_message(near), open_message(far))
    for head, states in enumerate(triples):
        total, _, den = merge(states)
        attn[:, head_of(head)] = (total * (1.0 / den)).T.astype(jnp.bfloat16)
    x = place[4]
    kept[...] = attn[pl.ds(pl.multiple_of(x * HALF, HALF), HALF), :]
    sent[...] = attn[pl.ds(pl.multiple_of((1 - x) * HALF, HALF), HALF), :]


def settle_call(place, num, ml, near, far):
    return pl.pallas_call(
        settle_kernel,
        in_specs=[SMEM] + [FULL] * 4,
        out_specs=[FULL] * 2,
        out_shape=[jax.ShapeDtypeStruct((HALF, WIDTH), jnp.bfloat16)] * 2,
        scratch_shapes=[pltpu.VMEM((COUNT, WIDTH), jnp.bfloat16)],
        compiler_params=params(),
        cost_estimate=cost(0, 2 * MIB),
    )(place, num, ml, near, far)


def project_kernel(place, attn, other, w, w_x, w_core, own, plus, minus, two, full):
    first = place[5] == 0
    low, high = other[:, :SPLIT].astype(jnp.float32), other[:, SPLIT:].astype(jnp.float32)
    by_x = jnp.where(first, low, high).astype(jnp.bfloat16)
    by_core = jnp.where(first, high, low).astype(jnp.bfloat16)
    for at in range(0, MODEL, 768):
        cols = slice(at, at + 768)
        total = jnp.dot(attn[...], w[:, cols], preferred_element_type=jnp.float32)
        total += jnp.dot(by_x, w_x[:, cols], preferred_element_type=jnp.float32)
        total += jnp.dot(by_core, w_core[:, cols], preferred_element_type=jnp.float32)
        full[:, cols] = total.astype(jnp.bfloat16)
    for n, out in enumerate((own, plus, minus, two)):
        out[...] = full[pl.ds(pl.multiple_of(place[n] * ROWS, ROWS), ROWS), :]


def project_call(place, attn, other, w, w_x, w_core):
    return pl.pallas_call(
        project_kernel,
        in_specs=[SMEM] + [FULL] * 5,
        out_specs=[FULL] * 4,
        out_shape=[jax.ShapeDtypeStruct((ROWS, MODEL), jnp.bfloat16)] * 4,
        scratch_shapes=[pltpu.VMEM((HALF, MODEL), jnp.bfloat16)],
        compiler_params=params(),
        cost_estimate=cost(2 * COUNT * WIDTH * MODEL, 5 * MIB),
    )(place, attn, other, w, w_x, w_core)


def gather_kernel(place, *refs):
    out = refs[8]
    for n in range(8):
        out[pl.ds(pl.multiple_of(place[n] * ROWS, ROWS), ROWS), :] = refs[n][...]


def gather_call(place, pieces):
    return pl.pallas_call(
        gather_kernel,
        in_specs=[SMEM] + [FULL] * 8,
        out_specs=FULL,
        out_shape=jax.ShapeDtypeStruct((COUNT, MODEL), jnp.bfloat16),
        compiler_params=params(),
        cost_estimate=cost(0, 4 * MIB),
    )(place, *pieces)


def ring(value, axis, step):
    size = SIZES[AXES.index(axis)]
    return lax.ppermute(value, axis, [(i, (i + step) % size) for i in range(size)])


def tables(rows):
    row_pos = (rows // WIDTH_TOK).astype(jnp.float32)
    col_pos = (rows % WIDTH_TOK).astype(jnp.float32)
    omega = 10000.0 ** (-2.0 * np.arange(28) / 56.0)
    by_row = np.repeat(np.concatenate([np.zeros(8), omega, np.zeros(28)]), 2).astype(np.float32)
    by_col = np.repeat(np.concatenate([np.zeros(36), omega]), 2).astype(np.float32)
    angles = row_pos[:, None] * by_row[None, :] + col_pos[:, None] * by_col[None, :]
    sign = np.tile(np.array([-1.0, 1.0], np.float32), HEAD // 2)
    return jnp.cos(angles), jnp.sin(angles) * sign[None, :]


def shards(
    latents,
    token_rows,
    mod_shift,
    mod_scale,
    mod_gate,
    w_qkv,
    q_gain,
    k_gain,
    stale_kv,
    text_kv,
    w_out,
    b_out,
):
    after = lax.optimization_barrier
    x, y, core = lax.axis_index("x_hi"), lax.axis_index("y"), lax.axis_index("core")
    own = jnp.transpose(stale_kv, (1, 0, 2))
    r1, l1 = ring(own, "z", 1), ring(own, "z", -1)
    w_x = ring(lax.dynamic_slice_in_dim(w_out, core * SPLIT, SPLIT, 0), "x_hi", 1)

    cosine, sine = tables(token_rows)
    q, k, v = qkv_call(
        latents, mod_shift, mod_scale, jnp.transpose(w_qkv, (1, 0, 2)), q_gain, k_gain, cosine, sine
    )
    q_core = ring(q, "core", 1)
    q_x = ring(q, "x_lo", 1)
    q_both = lax.ppermute(q, ("x_lo", "core"), [(0, 3), (1, 2), (2, 1), (3, 0)])

    r1, l1, q = after((r1, l1, q))
    r2, l2 = ring(r1, "z", 1), ring(l1, "z", -1)
    text = jnp.transpose(text_kv, (1, 0, 2))
    qs = jnp.stack([q, q_core, q_x, q_both])
    num, ml = first_call(qs, k, v, text, own)

    r2, l2, num, w_x = after((r2, l2, num, w_x))
    r3, l3 = ring(r2, "z", 1), ring(l2, "z", -1)
    w_core = ring(w_x, "core", 1)
    num, ml = next_call(qs, r1, l1, num, ml)
    num, ml = next_call(qs, r2, l2, num, ml)

    r3, l3, num = after((r3, l3, num))
    far_k, far_v = ring(r3[0], "z", 1), ring(l3[1], "z", -1)
    num, ml = next_call(qs, r3, l3, num, ml)

    far_k, far_v, num, w_core = after((far_k, far_v, num, w_core))
    x_num, x_ml, x_msg = last_call(qs, far_k, far_v, num, ml, 2)
    x_msg = ring(x_msg, "core", 1)
    o_num, o_ml, o_msg = last_call(qs, far_k, far_v, num, ml, 0)
    o_msg = ring(o_msg, "core", 1)
    x_out = ring(merge_call(x_num, x_ml, x_msg), "x_lo", 1)

    place = jnp.stack([y, (y + 1) % 4, (y + 3) % 4, (y + 2) % 4, x, core]).astype(jnp.int32)
    kept, sent = settle_call(place, o_num, o_ml, o_msg, x_out)
    other = ring(sent, "x_hi", 1)
    mine, plus, minus, two = project_call(place, kept, other, w_out, w_x, w_core)
    parts = [ring(plus, "y", 1), ring(minus, "y", -1), ring(two, "y", 2)]
    rows = lax.dynamic_slice_in_dim(latents, x * HALF + y * ROWS, ROWS, 0).astype(jnp.float32)
    total = mine.astype(jnp.float32)
    for part in parts:
        total = total + part.astype(jnp.float32)
    piece = (rows + mod_gate * (total + b_out)).astype(jnp.bfloat16)

    steps = (1, -1, 2)
    beside = ring(piece, "x_hi", 1)
    pieces = [piece] + [ring(piece, "y", s) for s in steps]
    pieces += [beside] + [ring(beside, "y", s) for s in steps]
    come = [(y - s) % 4 for s in (0, *steps)]
    come = jnp.stack([4 * x + c for c in come] + [4 * (1 - x) + c for c in come]).astype(jnp.int32)
    return (gather_call(come, pieces), jnp.stack([k, v], axis=1))


def solution(mesh):
    fine = Mesh(mesh.devices.reshape(SIZES), AXES)
    return jax.shard_map(
        shards,
        mesh=fine,
        in_specs=(
            P(PATCH, None),
            P(PATCH),
            P(),
            P(),
            P(),
            P(None, None, TENSOR),
            P(),
            P(),
            P(PATCH, None, TENSOR),
            P(None, None, TENSOR),
            P(TENSOR, None),
            P(),
        ),
        out_specs=(P(PATCH, None), P(PATCH, None, TENSOR)),
        check_vma=False,
    )
```

```python
import functools

import jax
import jax.numpy as jnp
import numpy as np
from jax import lax
from jax.experimental import pallas as pl
from jax.experimental.pallas import tpu as pltpu
from jax.sharding import Mesh
from jax.sharding import PartitionSpec as P

WIDTH_TOK = 256
ROW_POS = 8192 // WIDTH_TOK
HEAD = 128
LOCAL_HEADS = 3
WIDTH = HEAD * LOCAL_HEADS
COUNT = 256
TEXT = 512
MODEL = 3072
ROWS = COUNT // 8
AXES = ("x_lo", "z", "core", "y", "x_hi")
SIZES = (2, 8, 2, 4, 2)
PATCH = ("x_lo", "z", "core")
TENSOR = ("y", "x_hi")
SCALE = float(np.log2(np.e) / np.sqrt(128.0))
MIB = 1024 * 1024
EXTRA = 16
HALF = COUNT // 2
SPLIT = WIDTH // 2
FULL = pl.BlockSpec(memory_space=pltpu.VMEM)
SMEM = pl.BlockSpec(memory_space=pltpu.SMEM)


def params(mib=48):
    return pltpu.CompilerParams(vmem_limit_bytes=mib * MIB)


def cost(flops, nbytes, exps=0):
    del flops, nbytes, exps
    return pl.CostEstimate(flops=1024, bytes_accessed=1024, transcendentals=0)


def head_of(head):
    return slice(head * HEAD, (head + 1) * HEAD)


def whole_spec(shape):
    return pl.BlockSpec(shape, lambda i: (0,) * len(shape))


def trig_parts():
    omega = 10000.0 ** (-2.0 * np.arange(28) / 56.0)
    by_row = np.repeat(np.concatenate([np.zeros(8), omega, np.zeros(28)]), 2).astype(np.float32)
    by_col = np.repeat(np.concatenate([np.zeros(36), omega]), 2).astype(np.float32)
    lanes = np.arange(HEAD)
    sign = np.where(lanes % 2 == 0, -1.0, 1.0)
    blocks = []
    for omegas, count, mine in ((by_row, ROW_POS, lanes < 72), (by_col, WIDTH_TOK, lanes >= 72)):
        angle = (np.arange(count, dtype=np.float32)[:, None] * omegas[None, :]).astype(np.float64)
        blocks.append(np.concatenate([np.cos(angle) * mine, np.sin(angle) * sign * mine], axis=1))
    rest = np.concatenate(blocks).astype(np.float32)
    parts = []
    for _ in range(3):
        parts.append(rest.astype(jnp.bfloat16))
        rest = rest - parts[-1].astype(np.float32)
    return np.concatenate(parts, axis=1)


def qkv_kernel(
    place, lat, w, w_out, rows, trig, shift, scale, q_gain, k_gain, q, k, v, w_half, x_buf, w_buf, half, sems
):
    copies = [pltpu.make_async_copy(lat, x_buf, sems.at[3])]
    copies += [pltpu.make_async_copy(w.at[n], w_buf.at[n], sems.at[n]) for n in range(3)]
    part = pl.ds(pl.multiple_of(place[2] * SPLIT, SPLIT), SPLIT)
    copies.append(pltpu.make_async_copy(w_out.at[part], half, sems.at[4]))
    for copy in copies:
        copy.start()

    at = lax.broadcasted_iota(jnp.int32, (ROW_POS + WIDTH_TOK, COUNT), 0)
    row_pos = lax.shift_right_logical(rows[...], 8)
    col_pos = jnp.bitwise_and(rows[...], WIDTH_TOK - 1) + ROW_POS
    hot = jnp.where((at == row_pos) | (at == col_pos), 1.0, 0.0).astype(jnp.bfloat16)
    table = lax.dot_general(hot, trig[...], (((0,), (0,)), ((), ())), preferred_element_type=jnp.float32)
    table = table[:, : 2 * HEAD] + (table[:, 2 * HEAD : 4 * HEAD] + table[:, 4 * HEAD :])
    cosine, sine = table[:, :HEAD], table[:, HEAD:]

    copies[0].wait()
    x = x_buf[...].astype(jnp.float32)
    centred = x - jnp.mean(x, axis=-1, keepdims=True)
    spread = jnp.mean(centred * centred, axis=-1, keepdims=True)
    y = centred * lax.rsqrt(spread + 1e-06) * (1.0 + scale[...]) + shift[...]
    normed = y.astype(jnp.bfloat16)
    even = lax.broadcasted_iota(jnp.int32, (COUNT, HEAD), 1) % 2 == 0

    def rotated(out, gain, factor):
        heads = []
        for head in range(LOCAL_HEADS):
            x = out[:, head_of(head)]
            x = x * lax.rsqrt(jnp.mean(x * x, axis=-1, keepdims=True) + 1e-06) * gain[...]
            other = jnp.where(even, pltpu.roll(x, HEAD - 1, 1), pltpu.roll(x, 1, 1))
            x = x * cosine + other * sine
            heads.append((x * factor if factor else x).astype(jnp.bfloat16))
        return heads

    for n, (ref, gain, factor) in enumerate(((q, q_gain, SCALE), (k, k_gain, None), (v, None, None))):
        copies[n + 1].wait()
        out = jnp.dot(normed, w_buf[n], preferred_element_type=jnp.float32)
        if gain is None:
            ref[...] = out.astype(jnp.bfloat16)
        else:
            for head, x in enumerate(rotated(out, gain, factor)):
                ref[:, head_of(head)] = x
        if n == 0:
            copies[4].wait()
            back = pltpu.make_async_copy(half, w_half, sems.at[5])
            back.start()
    back.wait()


def qkv_call(place, latents, w, w_out, rows, shift, scale, q_gain, k_gain):
    anywhere = pl.BlockSpec(memory_space=pl.ANY)
    trig = trig_parts()
    return pl.pallas_call(
        qkv_kernel,
        grid=(1,),
        in_specs=[
            SMEM,
            anywhere,
            anywhere,
            anywhere,
            whole_spec((1, COUNT)),
            whole_spec(trig.shape),
            whole_spec((1, MODEL)),
            whole_spec((1, MODEL)),
            whole_spec((1, HEAD)),
            whole_spec((1, HEAD)),
        ],
        out_specs=[whole_spec((COUNT, WIDTH))] * 3 + [anywhere],
        out_shape=[jax.ShapeDtypeStruct((COUNT, WIDTH), jnp.bfloat16)] * 3
        + [jax.ShapeDtypeStruct((SPLIT, MODEL), jnp.bfloat16)],
        scratch_shapes=[
            pltpu.VMEM((COUNT, MODEL), jnp.bfloat16),
            pltpu.VMEM((3, MODEL, WIDTH), jnp.bfloat16),
            pltpu.VMEM((SPLIT, MODEL), jnp.bfloat16),
            pltpu.SemaphoreType.DMA((6,)),
        ],
        compiler_params=params(60),
        cost_estimate=cost(2 * COUNT * MODEL * WIDTH * 3, 10 * MIB),
    )(
        place,
        latents,
        w,
        w_out,
        rows.reshape(1, COUNT),
        jnp.asarray(trig),
        shift.reshape(1, MODEL),
        scale.reshape(1, MODEL),
        q_gain.reshape(1, HEAD),
        k_gain.reshape(1, HEAD),
    )


def attend(q, pairs, state=None):
    scores = []
    for k, _ in pairs:
        s = lax.dot_general(q, k, (((1,), (1,)), ((), ())), preferred_element_type=jnp.float32)
        scores.append([s[:, at : at + HEAD] for at in range(0, s.shape[1], HEAD)])
    top = None
    for piece in sum(scores, []):
        top = piece if top is None else jnp.maximum(top, piece)
    top = jnp.broadcast_to(jnp.max(top, axis=1, keepdims=True), top.shape)
    if state is not None:
        top = jnp.maximum(top, state[1])
    total = None
    for pieces, (_, v) in zip(scores, pairs):
        p = [jnp.exp2(s - top).astype(jnp.bfloat16) for s in pieces]
        wide = jnp.concatenate([v, jnp.ones_like(v)], axis=1)
        part = jnp.dot(jnp.concatenate(p, axis=1), wide, preferred_element_type=jnp.float32)
        total = part if total is None else total + part
    num, den = total[:, :HEAD], total[:, HEAD:]
    if state is not None:
        keep = jnp.exp2(state[1] - top)
        num, den = num + keep * state[0], den + keep * state[2]
    return num, top, den


def store_state(refs, cols, result, rows=slice(None)):
    for ref, value in zip(refs, result):
        ref[rows, cols] = value


def load_state(refs, cols, rows=slice(None)):
    return [ref[rows, cols] for ref in refs]


def both(pair, cols):
    return [(ref[0, :, cols], ref[1, :, cols]) for ref in pair]


HEADS = [head_of(n) for n in range(LOCAL_HEADS)]


def near_kernel(q0, q1, k, v, text, own, right, left, *state):
    for c in HEADS:
        ring_pairs = both((right, left), c)
        first = [(k[:, c], v[:, c]), (text[0, :, c], text[1, :, c])]
        store_state(state, c, attend(q0[:, c], first + ring_pairs), slice(0, COUNT))
        second = both((own,), c) + ring_pairs
        store_state(state, c, attend(q1[:, c], second), slice(COUNT, 2 * COUNT))


def far_kernel(q0, q1, *refs):
    blocks, state = refs[:-3], refs[-3:]
    for c in HEADS:
        q = jnp.concatenate([q0[:, c], q1[:, c]], axis=0)
        store_state(state, c, attend(q, both(blocks, c)))


def next_kernel(q0, q1, *refs):
    blocks, given, state = refs[:-6], refs[-6:-3], refs[-3:]
    for c in HEADS:
        q = jnp.concatenate([q0[:, c], q1[:, c]], axis=0)
        store_state(state, c, attend(q, both(blocks, c), load_state(given, c)))


def state_shapes(rows):
    return [jax.ShapeDtypeStruct((rows, WIDTH), jnp.float32)] * 3


def attend_cost(blocks):
    return cost(blocks * COUNT * COUNT * WIDTH * 4, 6 * MIB, blocks * COUNT * COUNT * LOCAL_HEADS)


def attend_call(kernel, blocks, *args):
    call = pl.pallas_call(
        kernel,
        in_specs=[FULL] * len(args),
        out_specs=[FULL] * 3,
        out_shape=state_shapes(2 * COUNT),
        compiler_params=params(24),
        cost_estimate=attend_cost(blocks),
    )
    return list(call(*args))


def pack(num, top, den):
    log = (top + jnp.log2(den)).T[:EXTRA, :]
    row = lax.broadcasted_iota(jnp.int32, log.shape, 0)
    parts = jnp.zeros_like(log)
    for n in range(3):
        rounded = log.astype(jnp.bfloat16).astype(jnp.float32)
        parts = jnp.where(row == n, rounded, parts)
        log = log - rounded
    return jnp.concatenate([num * (1.0 / den), parts], axis=0).astype(jnp.bfloat16)


def unpack(message):
    value = message[:HALF, :].astype(jnp.float32)
    stats = message[HALF:, :].astype(jnp.float32)
    log = stats[0:1, :] + (stats[1:2, :] + stats[2:3, :])
    return value, jnp.broadcast_to(log, (HALF, HEAD)).T, 1.0


def merge(*states):
    top = states[0][1]
    for s in states[1:]:
        top = jnp.maximum(top, s[1])
    num, den = 0.0, 0.0
    for n, m, d in states:
        keep = jnp.exp2(m - top)
        num, den = num + keep * n, den + keep * d
    return num, top, den


def last_kernel(q0, q1, keys, values, *refs):
    given, state, message = refs[:3], refs[3:6], refs[6]
    for c in HEADS:
        pairs = [(keys[:, c], values[:, c])]
        result = attend(q1[:, c], pairs, load_state(given, c, slice(COUNT, 2 * COUNT)))
        for n in range(2):
            message[n, :, c] = pack(*[a[n * HALF : (n + 1) * HALF] for a in result])
    for c in HEADS:
        pairs = [(keys[:, c], values[:, c])]
        store_state(state, c, attend(q0[:, c], pairs, load_state(given, c, slice(0, COUNT))))


def last_call(q0, q1, keys, values, *state):
    message = jax.ShapeDtypeStruct((2, HALF + EXTRA, WIDTH), jnp.bfloat16)
    *state, message = pl.pallas_call(
        last_kernel,
        in_specs=[FULL] * 7,
        out_specs=[FULL] * 4,
        out_shape=state_shapes(COUNT) + [message],
        compiler_params=params(24),
        cost_estimate=attend_cost(2),
    )(q0, q1, keys, values, *state)
    return state, message


def merge_kernel(place, *refs):
    swap = place[0] == 1
    for block in range(2):
        state, message = refs[4 * block : 4 * block + 3], refs[4 * block + 3]
        mine, other = refs[8 + 2 * block : 10 + 2 * block]
        for c in HEADS:
            halves = []
            for n in range(2):
                part = load_state(state, c, slice(n * HALF, (n + 1) * HALF))
                both_cores = merge(part, unpack(message[n, :, c]))
                halves.append(pack(*both_cores).astype(jnp.float32))
            mine[:, c] = jnp.where(swap, halves[1], halves[0]).astype(jnp.bfloat16)
            other[:, c] = jnp.where(swap, halves[0], halves[1]).astype(jnp.bfloat16)


def merge_call(place, *args):
    return pl.pallas_call(
        merge_kernel,
        in_specs=[SMEM] + [FULL] * 8,
        out_specs=[FULL] * 4,
        out_shape=[jax.ShapeDtypeStruct((HALF + EXTRA, WIDTH), jnp.bfloat16)] * 4,
        compiler_params=params(24),
        cost_estimate=cost(0, 4 * MIB),
    )(place, *args)


def project_kernel(place, *refs):
    messages, (w, w_x, w_core) = refs[:4], refs[4:7]
    own, plus, minus, two, attn, full = refs[7:]
    y, first = place[1], place[2] == 0
    for n in range(2):
        for head in range(LOCAL_HEADS):
            c = head_of(head)
            num, _, den = merge(*[unpack(m[:, c]) for m in messages[2 * n : 2 * n + 2]])
            attn[:, head_of(LOCAL_HEADS * n + head)] = (num * (1.0 / den)).astype(jnp.bfloat16)
    low = attn[:, WIDTH : WIDTH + SPLIT].astype(jnp.float32)
    high = attn[:, WIDTH + SPLIT :].astype(jnp.float32)
    by_x = jnp.where(first, low, high).astype(jnp.bfloat16)
    by_core = jnp.where(first, high, low).astype(jnp.bfloat16)
    for at in range(0, MODEL, 768):
        cols = slice(at, at + 768)
        total = jnp.dot(attn[:, :WIDTH], w[:, cols], preferred_element_type=jnp.float32)
        total += jnp.dot(by_x, w_x[:, cols], preferred_element_type=jnp.float32)
        total += jnp.dot(by_core, w_core[:, cols], preferred_element_type=jnp.float32)
        full[:, cols] = total.astype(jnp.bfloat16)
    for n, out in enumerate((own, plus, minus, two)):
        to = lax.rem(y + (0, 1, 3, 2)[n], 4)
        out[...] = full[pl.ds(pl.multiple_of(to * ROWS, ROWS), ROWS), :]


def project_call(place, messages, weights):
    return pl.pallas_call(
        project_kernel,
        in_specs=[SMEM] + [FULL] * 7,
        out_specs=[FULL] * 4,
        out_shape=[jax.ShapeDtypeStruct((ROWS, MODEL), jnp.bfloat16)] * 4,
        scratch_shapes=[
            pltpu.VMEM((HALF, 2 * WIDTH), jnp.bfloat16),
            pltpu.VMEM((HALF, MODEL), jnp.bfloat16),
        ],
        compiler_params=params(24),
        cost_estimate=cost(2 * COUNT * WIDTH * MODEL, 5 * MIB),
    )(place, *messages, *weights)


def put_kernel(offsets, place, *refs):
    out, sems = refs[-2:]
    x, y = place[0], place[1]
    copies = []
    for n, (flip, step) in enumerate(offsets):
        half = 1 - x if flip else x
        at = half * HALF + lax.rem(y + 4 - step, 4) * ROWS
        rows = pl.ds(pl.multiple_of(at, ROWS), ROWS)
        copies.append(pltpu.make_async_copy(refs[n], out.at[rows], sems.at[n]))
    for copy in copies:
        copy.start()
    for copy in copies:
        copy.wait()


def put_call(place, offsets, pieces, out=None):
    anywhere = pl.BlockSpec(memory_space=pl.ANY)
    count = len(pieces)
    more = [] if out is None else [out]
    return pl.pallas_call(
        functools.partial(put_kernel, offsets),
        in_specs=[SMEM] + [FULL] * count + [anywhere] * len(more),
        out_specs=anywhere,
        out_shape=jax.ShapeDtypeStruct((COUNT, MODEL), jnp.bfloat16),
        input_output_aliases={count + 1: 0} if more else {},
        scratch_shapes=[pltpu.SemaphoreType.DMA((count,))],
        compiler_params=params(24),
        cost_estimate=cost(0, 4 * MIB),
    )(place, *pieces, *more)


def ring(value, axis, step):
    size = SIZES[AXES.index(axis)]
    return lax.ppermute(value, axis, [(i, (i + step) % size) for i in range(size)])


def crossed(value, axes):
    return lax.ppermute(value, axes, [(i, 3 - i) for i in range(4)])


def shards(
    latents,
    token_rows,
    mod_shift,
    mod_scale,
    mod_gate,
    w_qkv,
    q_gain,
    k_gain,
    stale_kv,
    text_kv,
    w_out,
    b_out,
):
    after = lax.optimization_barrier
    x, y, core = lax.axis_index("x_hi"), lax.axis_index("y"), lax.axis_index("core")
    place = jnp.stack([x, y, core]).astype(jnp.int32)
    own = jnp.transpose(stale_kv, (1, 0, 2))
    r1, l1 = ring(own, "z", 1), ring(own, "z", -1)

    w = jnp.transpose(w_qkv, (1, 0, 2))
    q, k, v, w_half = qkv_call(
        place, latents, w, w_out, token_rows, mod_shift, mod_scale, q_gain, k_gain
    )
    q_core, q_x = ring(q, "core", 1), ring(q, "x_lo", 1)
    q_both = ring(q_x, "core", 1)
    w_half, q_x = after((w_half, q_x))
    w_x = ring(w_half, "x_hi", 1)

    r1, l1, q = after((r1, l1, q))
    r2, l2 = ring(r1, "z", 1), ring(l1, "z", -1)
    text = jnp.transpose(text_kv, (1, 0, 2))
    near = attend_call(near_kernel, 8, q, q_core, k, v, text, own, r1, l1)

    r2, l2, near[0], q_both = after((r2, l2, near[0], q_both))
    r3, l3 = ring(r2, "z", 1), ring(l2, "z", -1)
    near = attend_call(next_kernel, 4, q, q_core, r2, l2, *near)
    far = attend_call(far_kernel, 10, q_x, q_both, own, r1, l1, r2, l2)

    r3, l3, near[0], far[0] = after((r3, l3, near[0], far[0]))
    far_k, far_v = ring(r3[0], "z", 1), ring(l3[1], "z", -1)
    far = attend_call(next_kernel, 4, q_x, q_both, r3, l3, *far)
    near = attend_call(next_kernel, 4, q, q_core, r3, l3, *near)

    far_k, far_v, near[0], far[0] = after((far_k, far_v, near[0], far[0]))
    x_state, x_msg = last_call(q_x, q_both, far_k, far_v, *far)
    x_msg = ring(x_msg, "core", 1)
    o_state, o_msg = last_call(q, q_core, far_k, far_v, *near)
    w_x, o_msg = after((w_x, o_msg))
    w_core = ring(w_x, "core", 1)
    o_msg = ring(o_msg, "core", 1)
    x_mine, x_other, o_mine, o_other = merge_call(place, *x_state, x_msg, *o_state, o_msg)
    from_hi = ring(o_other, "x_hi", 1)
    from_x = ring(x_mine, "x_lo", 1)
    from_both = crossed(x_other, ("x_lo", "x_hi"))

    mine, plus, minus, two = project_call(
        place, (o_mine, from_x, from_hi, from_both), (w_out, w_x, w_core)
    )
    parts = [ring(two, "y", 2), ring(plus, "y", 1), ring(minus, "y", -1)]
    rows = lax.dynamic_slice_in_dim(latents, x * HALF + y * ROWS, ROWS, 0).astype(jnp.float32)
    total = mine.astype(jnp.float32)
    for part in parts:
        total = total + part.astype(jnp.float32)
    piece = (rows + mod_gate * (total + b_out)).astype(jnp.bfloat16)

    beside, plus = ring(piece, "x_hi", 1), ring(piece, "y", 1)
    minus, two = ring(piece, "y", -1), ring(piece, "y", 2)
    early = [((0, 0), piece), ((1, 0), beside), ((0, 1), plus), ((0, -1), minus), ((0, 2), two)]
    out = put_call(place, [e[0] for e in early], [e[1] for e in early])
    late = [
        ((1, 1), ring(plus, "x_hi", 1)),
        ((1, -1), ring(minus, "x_hi", 1)),
        ((1, 2), ring(beside, "y", 2)),
    ]
    out = put_call(place, [e[0] for e in late], [e[1] for e in late], out)
    return (out, jnp.stack([k, v], axis=1))


def solution(mesh):
    fine = Mesh(mesh.devices.reshape(SIZES), AXES)
    return jax.shard_map(
        shards,
        mesh=fine,
        in_specs=(
            P(PATCH, None),
            P(PATCH),
            P(),
            P(),
            P(),
            P(None, None, TENSOR),
            P(),
            P(),
            P(PATCH, None, TENSOR),
            P(None, None, TENSOR),
            P(TENSOR, None),
            P(),
        ),
        out_specs=(P(PATCH, None), P(PATCH, None, TENSOR)),
        check_vma=False,
    )
```

```python
import functools

import jax
import jax.numpy as jnp
import numpy as np
from jax import lax
from jax.experimental import pallas as pl
from jax.experimental.pallas import tpu as pltpu
from jax.sharding import Mesh
from jax.sharding import PartitionSpec as P

WIDTH_TOK = 256
ROW_POS = 8192 // WIDTH_TOK
HEAD = 128
LOCAL_HEADS = 3
WIDTH = HEAD * LOCAL_HEADS
COUNT = 256
TEXT = 512
MODEL = 3072
ROWS = COUNT // 8
AXES = ("x_lo", "z", "core", "y", "x_hi")
SIZES = (2, 8, 2, 4, 2)
PATCH = ("x_lo", "z", "core")
TENSOR = ("y", "x_hi")
SCALE = float(np.log2(np.e) / np.sqrt(128.0))
MIB = 1024 * 1024
EXTRA = 16
HALF = COUNT // 2
SPLIT = WIDTH // 2
FULL = pl.BlockSpec(memory_space=pltpu.VMEM)
SMEM = pl.BlockSpec(memory_space=pltpu.SMEM)


def params(mib=48):
    return pltpu.CompilerParams(vmem_limit_bytes=mib * MIB)


def cost(flops, nbytes, exps=0):
    del flops, nbytes, exps
    return pl.CostEstimate(flops=1024, bytes_accessed=1024, transcendentals=0)


def head_of(head):
    return slice(head * HEAD, (head + 1) * HEAD)


HEADS = [head_of(n) for n in range(LOCAL_HEADS)]


def whole_spec(shape):
    return pl.BlockSpec(shape, lambda i: (0,) * len(shape))


def trig_parts():
    omega = 10000.0 ** (-2.0 * np.arange(28) / 56.0)
    by_row = np.repeat(np.concatenate([np.zeros(8), omega, np.zeros(28)]), 2).astype(np.float32)
    by_col = np.repeat(np.concatenate([np.zeros(36), omega]), 2).astype(np.float32)
    lanes = np.arange(HEAD)
    sign = np.where(lanes % 2 == 0, -1.0, 1.0)
    blocks = []
    for omegas, count, mine in ((by_row, ROW_POS, lanes < 72), (by_col, WIDTH_TOK, lanes >= 72)):
        angle = (np.arange(count, dtype=np.float32)[:, None] * omegas[None, :]).astype(np.float64)
        blocks.append(np.concatenate([np.cos(angle) * mine, np.sin(angle) * sign * mine], axis=1))
    rest = np.concatenate(blocks).astype(np.float32)
    parts = []
    for _ in range(3):
        parts.append(rest.astype(jnp.bfloat16))
        rest = rest - parts[-1].astype(np.float32)
    return np.concatenate(parts, axis=1)


def qkv_kernel(place, *refs):
    given, (q, k, v, w_half), buffers, sems = refs[:9], refs[9:13], refs[13:-1], refs[-1]
    lat, w, trig, rows, shift, scale, q_gain, k_gain, half = buffers
    part = pl.ds(pl.multiple_of(place[2] * SPLIT, SPLIT), SPLIT)
    copy = lambda n, source, target: pltpu.make_async_copy(source, target, sems.at[n])
    weights = [copy(n, given[1].at[n], w.at[n]) for n in range(3)]
    small = [copy(n + 1, given[n], buffers[n]) for n in range(2, 8)]
    latents, half_in = copy(9, given[0], lat), copy(10, given[8].at[part], half)
    half_out = copy(11, half, w_half)
    latents.start()
    for c in small:
        c.start()
    weights[0].start()

    for c in small:
        c.wait()
    at = lax.broadcasted_iota(jnp.int32, (ROW_POS + WIDTH_TOK, COUNT), 0)
    row_pos = lax.shift_right_logical(rows[...], 8)
    col_pos = jnp.bitwise_and(rows[...], WIDTH_TOK - 1) + ROW_POS
    hot = jnp.where((at == row_pos) | (at == col_pos), 1.0, 0.0).astype(jnp.bfloat16)
    turn = lax.dot_general(hot, trig[...], (((0,), (0,)), ((), ())), preferred_element_type=jnp.float32)
    turn = turn[:, : 2 * HEAD] + (turn[:, 2 * HEAD : 4 * HEAD] + turn[:, 4 * HEAD :])
    cosine, sine = turn[:, :HEAD], turn[:, HEAD:]
    even = lax.broadcasted_iota(jnp.int32, (COUNT, HEAD), 1) % 2 == 0

    latents.wait()
    weights[1].start()
    x = lat[...].astype(jnp.float32)
    centred = x - jnp.mean(x, axis=-1, keepdims=True)
    spread = jnp.mean(centred * centred, axis=-1, keepdims=True)
    y = centred * lax.rsqrt(spread + 1e-06) * (1.0 + scale[...]) + shift[...]
    normed = y.astype(jnp.bfloat16)

    def rotated(x, gain, factor):
        x = x * lax.rsqrt(jnp.mean(x * x, axis=-1, keepdims=True) + 1e-06) * gain[...]
        other = jnp.where(even, pltpu.roll(x, HEAD - 1, 1), pltpu.roll(x, 1, 1))
        x = x * cosine + other * sine
        return (x * factor if factor else x).astype(jnp.bfloat16)

    for n, (ref, gain, factor) in enumerate(((q, q_gain, SCALE), (k, k_gain, None), (v, None, None))):
        weights[n].wait()
        if n == 0:
            weights[2].start()
            half_in.start()
        out = jnp.dot(normed, w[n], preferred_element_type=jnp.float32)
        for c in HEADS:
            x = out[:, c]
            ref[:, c] = x.astype(jnp.bfloat16) if gain is None else rotated(x, gain, factor)
        if n == 1:
            half_in.wait()
            half_out.start()
    half_out.wait()


def qkv_call(place, latents, w, rows, shift, scale, q_gain, k_gain, w_out):
    anywhere = pl.BlockSpec(memory_space=pl.ANY)
    row = lambda a: a.reshape(1, a.shape[0])
    args = [latents, w, jnp.asarray(trig_parts())]
    args += [row(a) for a in (rows, shift, scale, q_gain, k_gain)]
    half = (SPLIT, MODEL)
    return pl.pallas_call(
        qkv_kernel,
        in_specs=[SMEM] + [anywhere] * 9,
        out_specs=[FULL] * 3 + [anywhere],
        out_shape=[jax.ShapeDtypeStruct((COUNT, WIDTH), jnp.bfloat16)] * 3
        + [jax.ShapeDtypeStruct(half, jnp.bfloat16)],
        scratch_shapes=[pltpu.VMEM(a.shape, a.dtype) for a in args]
        + [pltpu.VMEM(half, jnp.bfloat16), pltpu.SemaphoreType.DMA((12,))],
        compiler_params=params(60),
        cost_estimate=cost(2 * COUNT * MODEL * WIDTH * 3, 10 * MIB),
    )(place, *args, w_out)


def attend(q, pairs, state=None):
    scores = []
    for k, _ in pairs:
        s = lax.dot_general(q, k, (((1,), (1,)), ((), ())), preferred_element_type=jnp.float32)
        scores.append([s[:, at : at + HEAD] for at in range(0, s.shape[1], HEAD)])
    top = None
    for piece in sum(scores, []):
        top = piece if top is None else jnp.maximum(top, piece)
    top = jnp.broadcast_to(jnp.max(top, axis=1, keepdims=True), top.shape)
    if state is not None:
        top = jnp.maximum(top, state[1])
    total = None
    for pieces, (_, v) in zip(scores, pairs):
        p = [jnp.exp2(s - top).astype(jnp.bfloat16) for s in pieces]
        wide = jnp.concatenate([v, jnp.ones_like(v)], axis=1)
        part = jnp.dot(jnp.concatenate(p, axis=1), wide, preferred_element_type=jnp.float32)
        total = part if total is None else total + part
    num, den = total[:, :HEAD], total[:, HEAD:]
    if state is not None:
        keep = jnp.exp2(state[1] - top)
        num, den = num + keep * state[0], den + keep * state[2]
    return num, top, den


def store_state(refs, cols, result, rows=slice(None)):
    for ref, value in zip(refs, result):
        ref[rows, cols] = value


def load_state(refs, cols, rows=slice(None)):
    return [ref[rows, cols] for ref in refs]


def both(pair, cols):
    return [(ref[0, :, cols], ref[1, :, cols]) for ref in pair]


def near_kernel(q0, q1, k, v, text, own, right, left, *state):
    for c in HEADS:
        ring_pairs = both((right, left), c)
        first = [(k[:, c], v[:, c]), (text[0, :, c], text[1, :, c])]
        store_state(state, c, attend(q0[:, c], first + ring_pairs), slice(0, COUNT))
        second = both((own,), c) + ring_pairs
        store_state(state, c, attend(q1[:, c], second), slice(COUNT, 2 * COUNT))


def far_kernel(q0, q1, *refs):
    blocks, state = refs[:-3], refs[-3:]
    for c in HEADS:
        q = jnp.concatenate([q0[:, c], q1[:, c]], axis=0)
        store_state(state, c, attend(q, both(blocks, c)))


def next_kernel(q0, q1, *refs):
    blocks, given, state = refs[:-6], refs[-6:-3], refs[-3:]
    for c in HEADS:
        q = jnp.concatenate([q0[:, c], q1[:, c]], axis=0)
        store_state(state, c, attend(q, both(blocks, c), load_state(given, c)))


def state_shapes(rows):
    return [jax.ShapeDtypeStruct((rows, WIDTH), jnp.float32)] * 3


def attend_cost(blocks):
    return cost(blocks * COUNT * COUNT * WIDTH * 4, 6 * MIB, blocks * COUNT * COUNT * LOCAL_HEADS)


def attend_call(kernel, blocks, *args):
    call = pl.pallas_call(
        kernel,
        in_specs=[FULL] * len(args),
        out_specs=[FULL] * 3,
        out_shape=state_shapes(2 * COUNT),
        compiler_params=params(24),
        cost_estimate=attend_cost(blocks),
    )
    return list(call(*args))


def pack(num, top, den):
    log = (top + jnp.log2(den)).T[:EXTRA, :]
    row = lax.broadcasted_iota(jnp.int32, log.shape, 0)
    parts = jnp.zeros_like(log)
    for n in range(3):
        rounded = log.astype(jnp.bfloat16).astype(jnp.float32)
        parts = jnp.where(row == n, rounded, parts)
        log = log - rounded
    return jnp.concatenate([num * (1.0 / den), parts], axis=0).astype(jnp.bfloat16)


def unpack(message):
    value = message[:HALF, :].astype(jnp.float32)
    stats = message[HALF:, :].astype(jnp.float32)
    log = stats[0:1, :] + (stats[1:2, :] + stats[2:3, :])
    return value, jnp.broadcast_to(log, (HALF, HEAD)).T, 1.0


def merge(*states):
    top = states[0][1]
    for s in states[1:]:
        top = jnp.maximum(top, s[1])
    num, den = 0.0, 0.0
    for n, m, d in states:
        keep = jnp.exp2(m - top)
        num, den = num + keep * n, den + keep * d
    return num, top, den


def last_kernel(q0, q1, keys, values, *refs):
    given, state, message = refs[:3], refs[3:6], refs[6]
    for c in HEADS:
        pairs = [(keys[:, c], values[:, c])]
        result = attend(q1[:, c], pairs, load_state(given, c, slice(COUNT, 2 * COUNT)))
        for n in range(2):
            message[n, :, c] = pack(*[a[n * HALF : (n + 1) * HALF] for a in result])
    for c in HEADS:
        pairs = [(keys[:, c], values[:, c])]
        store_state(state, c, attend(q0[:, c], pairs, load_state(given, c, slice(0, COUNT))))


def last_call(q0, q1, keys, values, *state):
    message = jax.ShapeDtypeStruct((2, HALF + EXTRA, WIDTH), jnp.bfloat16)
    *state, message = pl.pallas_call(
        last_kernel,
        in_specs=[FULL] * 7,
        out_specs=[FULL] * 4,
        out_shape=state_shapes(COUNT) + [message],
        compiler_params=params(24),
        cost_estimate=attend_cost(2),
    )(q0, q1, keys, values, *state)
    return state, message


def merge_kernel(place, *refs):
    swap = jnp.bitwise_and(place[1], 1) == 1
    for block in range(2):
        state, message = refs[4 * block : 4 * block + 3], refs[4 * block + 3]
        mine, other = refs[8 + 2 * block : 10 + 2 * block]
        for c in HEADS:
            halves = []
            for n in range(2):
                part = load_state(state, c, slice(n * HALF, (n + 1) * HALF))
                both_cores = merge(part, unpack(message[n, :, c]))
                halves.append(pack(*both_cores).astype(jnp.float32))
            mine[:, c] = jnp.where(swap, halves[1], halves[0]).astype(jnp.bfloat16)
            other[:, c] = jnp.where(swap, halves[0], halves[1]).astype(jnp.bfloat16)


def merge_call(place, *args):
    return pl.pallas_call(
        merge_kernel,
        in_specs=[SMEM] + [FULL] * 8,
        out_specs=[FULL] * 4,
        out_shape=[jax.ShapeDtypeStruct((HALF + EXTRA, WIDTH), jnp.bfloat16)] * 4,
        compiler_params=params(24),
        cost_estimate=cost(0, 4 * MIB),
    )(place, *args)


QUARTERS = ((0, 0), (1, 1), (1, 0), (0, 1))


def project_kernel(place, *refs):
    messages, (w, w_x, w_core) = refs[:4], refs[4:7]
    outs, attn, full = refs[7:11], refs[11], refs[12]
    x, high_y, first = place[0], lax.shift_right_logical(place[1], 1), place[2] == 0
    for n in range(2):
        for head in range(LOCAL_HEADS):
            c = head_of(head)
            num, _, den = merge(*[unpack(m[:, c]) for m in messages[2 * n : 2 * n + 2]])
            attn[:, head_of(LOCAL_HEADS * n + head)] = (num * (1.0 / den)).astype(jnp.bfloat16)
    low = attn[:, WIDTH : WIDTH + SPLIT].astype(jnp.float32)
    high = attn[:, WIDTH + SPLIT :].astype(jnp.float32)
    by_x = jnp.where(first, low, high).astype(jnp.bfloat16)
    by_core = jnp.where(first, high, low).astype(jnp.bfloat16)
    for at in range(0, MODEL, 768):
        cols = slice(at, at + 768)
        total = jnp.dot(attn[:, :WIDTH], w[:, cols], preferred_element_type=jnp.float32)
        total += jnp.dot(by_x, w_x[:, cols], preferred_element_type=jnp.float32)
        total += jnp.dot(by_core, w_core[:, cols], preferred_element_type=jnp.float32)
        full[:, cols] = total.astype(jnp.bfloat16)
    for out, (dy, dx) in zip(outs, QUARTERS):
        to = jnp.bitwise_xor(high_y, dy) * 2 + jnp.bitwise_xor(x, dx)
        out[...] = full[pl.ds(pl.multiple_of(to * ROWS, ROWS), ROWS), :]


def project_call(place, messages, weights):
    return pl.pallas_call(
        project_kernel,
        in_specs=[SMEM] + [FULL] * 7,
        out_specs=[FULL] * 4,
        out_shape=[jax.ShapeDtypeStruct((ROWS, MODEL), jnp.bfloat16)] * 4,
        scratch_shapes=[
            pltpu.VMEM((HALF, 2 * WIDTH), jnp.bfloat16),
            pltpu.VMEM((HALF, MODEL), jnp.bfloat16),
        ],
        compiler_params=params(24),
        cost_estimate=cost(2 * COUNT * WIDTH * MODEL, 5 * MIB),
    )(place, *messages, *weights)


def put_kernel(offsets, place, *refs):
    out, sems = refs[-2:]
    x, y = place[0], place[1]
    copies = []
    for n, (flip, step) in enumerate(offsets):
        from_y = lax.rem(y + 4 - step, 4)
        quarter = lax.shift_right_logical(from_y, 1) * 2 + (1 - x if flip else x)
        at = jnp.bitwise_and(from_y, 1) * HALF + quarter * ROWS
        rows = pl.ds(pl.multiple_of(at, ROWS), ROWS)
        copies.append(pltpu.make_async_copy(refs[n], out.at[rows], sems.at[n]))
    for copy in copies:
        copy.start()
    for copy in copies:
        copy.wait()


def put_call(place, offsets, pieces, out=None):
    anywhere = pl.BlockSpec(memory_space=pl.ANY)
    count = len(pieces)
    more = [] if out is None else [out]
    return pl.pallas_call(
        functools.partial(put_kernel, offsets),
        in_specs=[SMEM] + [FULL] * count + [anywhere] * len(more),
        out_specs=anywhere,
        out_shape=jax.ShapeDtypeStruct((COUNT, MODEL), jnp.bfloat16),
        input_output_aliases={count + 1: 0} if more else {},
        scratch_shapes=[pltpu.SemaphoreType.DMA((count,))],
        compiler_params=params(24),
        cost_estimate=cost(0, 4 * MIB),
    )(place, *pieces, *more)


def ring(value, axis, step):
    size = SIZES[AXES.index(axis)]
    return lax.ppermute(value, axis, [(i, (i + step) % size) for i in range(size)])


def beside_y(value):
    return lax.ppermute(value, "y", [(i, i ^ 1) for i in range(4)])


def crossed(value, axes):
    return lax.ppermute(value, axes, [(i, 3 - i) for i in range(4)])


def shards(
    latents,
    token_rows,
    mod_shift,
    mod_scale,
    mod_gate,
    w_qkv,
    q_gain,
    k_gain,
    stale_kv,
    text_kv,
    w_out,
    b_out,
):
    after = lax.optimization_barrier
    x, y, core = lax.axis_index("x_hi"), lax.axis_index("y"), lax.axis_index("core")
    place = jnp.stack([x, y, core]).astype(jnp.int32)
    own = jnp.transpose(stale_kv, (1, 0, 2))
    r1, l1 = ring(own, "z", 1), ring(own, "z", -1)

    w = jnp.transpose(w_qkv, (1, 0, 2))
    q, k, v, w_half = qkv_call(
        place, latents, w, token_rows, mod_shift, mod_scale, q_gain, k_gain, w_out
    )
    w_pair = beside_y(w_half)
    q_core, q_x = ring(q, "core", 1), ring(q, "x_lo", 1)

    r1, l1, q = after((r1, l1, q))
    r2, l2 = ring(r1, "z", 1), ring(l1, "z", -1)
    text = jnp.transpose(text_kv, (1, 0, 2))
    near = attend_call(near_kernel, 8, q, q_core, k, v, text, own, r1, l1)

    q_x, near[2] = after((q_x, near[2]))
    q_both = ring(q_x, "core", 1)
    r2, near[0] = after((r2, near[0]))
    r3 = ring(r2, "z", 1)
    l2, near[1] = after((l2, near[1]))
    l3 = ring(l2, "z", -1)
    near = attend_call(next_kernel, 4, q, q_core, r2, l2, *near)
    far = attend_call(far_kernel, 10, q_x, q_both, own, r1, l1, r2, l2)

    r3, near[0], far[0] = after((r3, near[0], far[0]))
    far_k = ring(r3[0], "z", 1)
    l3, near[1], far[1] = after((l3, near[1], far[1]))
    far_v = ring(l3[1], "z", -1)
    far = attend_call(next_kernel, 4, q_x, q_both, r3, l3, *far)
    near = attend_call(next_kernel, 4, q, q_core, r3, l3, *near)

    far_k, far_v, near[0], far[0] = after((far_k, far_v, near[0], far[0]))
    x_state, x_msg = last_call(q_x, q_both, far_k, far_v, *far)
    x_msg = ring(x_msg, "core", 1)
    o_state, o_msg = last_call(q, q_core, far_k, far_v, *near)
    w_pair, o_msg = after((w_pair, o_msg))
    o_msg = ring(o_msg, "core", 1)
    w_core = ring(w_pair, "core", 1)
    x_mine, x_other, o_mine, o_other = merge_call(place, *x_state, x_msg, *o_state, o_msg)
    from_y, from_x = beside_y(o_other), ring(x_mine, "x_lo", 1)
    from_both = lax.ppermute(
        x_other, ("x_lo", "y"), [(i, (1 - i // 4) * 4 + (i % 4 ^ 1)) for i in range(8)]
    )

    mine, both_ways, along_y, along_x = project_call(
        place, (o_mine, from_x, from_y, from_both), (w_out, w_pair, w_core)
    )
    parts = [
        lax.ppermute(both_ways, TENSOR, [(i, (i // 2 + 2) % 4 * 2 + (1 - i % 2)) for i in range(8)]),
        ring(along_y, "y", 2),
        ring(along_x, "x_hi", 1),
    ]
    start = y % 2 * HALF + (y // 2 * 2 + x) * ROWS
    rows = lax.dynamic_slice_in_dim(latents, start, ROWS, 0).astype(jnp.float32)
    total = mine.astype(jnp.float32)
    for part in parts:
        total = total + part.astype(jnp.float32)
    piece = (rows + mod_gate * (total + b_out)).astype(jnp.bfloat16)

    beside, two = ring(piece, "x_hi", 1), ring(piece, "y", 2)
    plus, minus = ring(piece, "y", 1), ring(piece, "y", -1)
    early = [
        ((0, 0), piece),
        ((1, 0), beside),
        ((0, 1), plus),
        ((0, -1), minus),
        ((0, 2), two),
    ]
    late = [
        ((1, 1), ring(beside, "y", 1)),
        ((1, -1), ring(beside, "y", -1)),
        ((1, 2), ring(two, "x_hi", 1)),
    ]
    out = put_call(place, [e[0] for e in early], [e[1] for e in early])
    out = put_call(place, [e[0] for e in late], [e[1] for e in late], out)
    return (out, jnp.stack([k, v], axis=1))


def solution(mesh):
    fine = Mesh(mesh.devices.reshape(SIZES), AXES)
    return jax.shard_map(
        shards,
        mesh=fine,
        in_specs=(
            P(PATCH, None),
            P(PATCH),
            P(),
            P(),
            P(),
            P(None, None, TENSOR),
            P(),
            P(),
            P(PATCH, None, TENSOR),
            P(None, None, TENSOR),
            P(TENSOR, None),
            P(),
        ),
        out_specs=(P(PATCH, None), P(PATCH, None, TENSOR)),
        check_vma=False,
    )
```

```python
import functools

import jax
import jax.numpy as jnp
import numpy as np
from jax import lax
from jax.experimental import pallas as pl
from jax.experimental.pallas import tpu as pltpu
from jax.sharding import Mesh
from jax.sharding import PartitionSpec as P

WIDTH_TOK = 256
ROW_POS = 8192 // WIDTH_TOK
HEAD = 128
LOCAL_HEADS = 3
WIDTH = HEAD * LOCAL_HEADS
COUNT = 256
TEXT = 512
MODEL = 3072
ROWS = COUNT // 8
WIDE = (slice(0, MODEL // 2), slice(MODEL // 2, MODEL))
AXES = ("x_lo", "z", "core", "y", "x_hi")
SIZES = (2, 8, 2, 4, 2)
PATCH = ("x_lo", "z", "core")
TENSOR = ("y", "x_hi")
SCALE = float(np.log2(np.e) / np.sqrt(128.0))
MIB = 1024 * 1024
EXTRA = 16
HALF = COUNT // 2
SPLIT = WIDTH // 2
FULL = pl.BlockSpec(memory_space=pltpu.VMEM)


def params(mib=48):
    return pltpu.CompilerParams(vmem_limit_bytes=mib * MIB)


def cost(flops, nbytes, exps=0):
    del flops, nbytes, exps
    return pl.CostEstimate(flops=1024, bytes_accessed=1024, transcendentals=0)


def head_of(head):
    return slice(head * HEAD, (head + 1) * HEAD)


HEADS = [head_of(n) for n in range(LOCAL_HEADS)]


def whole_spec(shape):
    return pl.BlockSpec(shape, lambda i: (0,) * len(shape))


def trig_parts():
    omega = 10000.0 ** (-2.0 * np.arange(28) / 56.0)
    by_row = np.repeat(np.concatenate([np.zeros(8), omega, np.zeros(28)]), 2).astype(np.float32)
    by_col = np.repeat(np.concatenate([np.zeros(36), omega]), 2).astype(np.float32)
    lanes = np.arange(HEAD)
    sign = np.where(lanes % 2 == 0, -1.0, 1.0)
    blocks = []
    for omegas, count, mine in ((by_row, ROW_POS, lanes < 72), (by_col, WIDTH_TOK, lanes >= 72)):
        angle = (np.arange(count, dtype=np.float32)[:, None] * omegas[None, :]).astype(np.float64)
        blocks.append(np.concatenate([np.cos(angle) * mine, np.sin(angle) * sign * mine], axis=1))
    rest = np.concatenate(blocks).astype(np.float32)
    parts = []
    for _ in range(3):
        parts.append(rest.astype(jnp.bfloat16))
        rest = rest - parts[-1].astype(np.float32)
    return np.concatenate(parts, axis=1)


def qkv_kernel(*refs):
    given, (q, k, v, *w_half), buffers, sems = refs[:9], refs[9:14], refs[14:-1], refs[-1]
    lat, w, trig, rows, shift, scale, q_gain, k_gain, half = buffers
    part = pl.ds(pl.multiple_of(lax.axis_index("core") * SPLIT, SPLIT), SPLIT)
    copy = lambda n, source, target: pltpu.make_async_copy(source, target, sems.at[n])
    weights = [copy(n, given[1].at[n], w.at[n]) for n in range(3)]
    small = [copy(n + 1, given[n], buffers[n]) for n in range(2, 8)]
    latents, half_in = copy(9, given[0], lat), copy(10, given[8].at[part], half)
    half_out = [copy(11 + n, half.at[:, cols], w_half[n]) for n, cols in enumerate(WIDE)]
    latents.start()
    for c in small:
        c.start()
    weights[0].start()

    for c in small:
        c.wait()
    at = lax.broadcasted_iota(jnp.int32, (ROW_POS + WIDTH_TOK, COUNT), 0)
    row_pos = lax.shift_right_logical(rows[...], 8)
    col_pos = jnp.bitwise_and(rows[...], WIDTH_TOK - 1) + ROW_POS
    hot = jnp.where((at == row_pos) | (at == col_pos), 1.0, 0.0).astype(jnp.bfloat16)
    turn = lax.dot_general(hot, trig[...], (((0,), (0,)), ((), ())), preferred_element_type=jnp.float32)
    turn = turn[:, : 2 * HEAD] + (turn[:, 2 * HEAD : 4 * HEAD] + turn[:, 4 * HEAD :])
    cosine, sine = turn[:, :HEAD], turn[:, HEAD:]
    even = lax.broadcasted_iota(jnp.int32, (COUNT, HEAD), 1) % 2 == 0

    latents.wait()
    weights[1].start()
    x = lat[...].astype(jnp.float32)
    centred = x - jnp.mean(x, axis=-1, keepdims=True)
    spread = jnp.mean(centred * centred, axis=-1, keepdims=True)
    y = centred * lax.rsqrt(spread + 1e-06) * (1.0 + scale[...]) + shift[...]
    normed = y.astype(jnp.bfloat16)

    def rotated(x, gain, factor):
        x = x * lax.rsqrt(jnp.mean(x * x, axis=-1, keepdims=True) + 1e-06) * gain[...]
        other = jnp.where(even, pltpu.roll(x, HEAD - 1, 1), pltpu.roll(x, 1, 1))
        x = x * cosine + other * sine
        return (x * factor if factor else x).astype(jnp.bfloat16)

    for n, (ref, gain, factor) in enumerate(((q, q_gain, SCALE), (k, k_gain, None), (v, None, None))):
        weights[n].wait()
        if n == 0:
            weights[2].start()
            half_in.start()
        out = jnp.dot(normed, w[n], preferred_element_type=jnp.float32)
        for c in HEADS:
            x = out[:, c]
            ref[:, c] = x.astype(jnp.bfloat16) if gain is None else rotated(x, gain, factor)
        if n == 1:
            half_in.wait()
            for c in half_out:
                c.start()
    for c in half_out:
        c.wait()


def qkv_call(latents, w, rows, shift, scale, q_gain, k_gain, w_out):
    anywhere = pl.BlockSpec(memory_space=pl.ANY)
    row = lambda a: a.reshape(1, a.shape[0])
    args = [latents, w, jnp.asarray(trig_parts())]
    args += [row(a) for a in (rows, shift, scale, q_gain, k_gain)]
    half = (SPLIT, MODEL)
    return pl.pallas_call(
        qkv_kernel,
        in_specs=[anywhere] * 9,
        out_specs=[FULL] * 3 + [anywhere] * 2,
        out_shape=[jax.ShapeDtypeStruct((COUNT, WIDTH), jnp.bfloat16)] * 3
        + [jax.ShapeDtypeStruct((SPLIT, MODEL // 2), jnp.bfloat16)] * 2,
        scratch_shapes=[pltpu.VMEM(a.shape, a.dtype) for a in args]
        + [pltpu.VMEM(half, jnp.bfloat16), pltpu.SemaphoreType.DMA((13,))],
        compiler_params=params(60),
        cost_estimate=cost(2 * COUNT * MODEL * WIDTH * 3, 10 * MIB),
    )(*args, w_out)


def attend(q, pairs, state=None):
    scores = []
    for k, _ in pairs:
        s = lax.dot_general(q, k, (((1,), (1,)), ((), ())), preferred_element_type=jnp.float32)
        scores.append([s[:, at : at + HEAD] for at in range(0, s.shape[1], HEAD)])
    top = None
    for piece in sum(scores, []):
        top = piece if top is None else jnp.maximum(top, piece)
    top = jnp.broadcast_to(jnp.max(top, axis=1, keepdims=True), top.shape)
    if state is not None:
        top = jnp.maximum(top, state[1])
    total = None
    for pieces, (_, v) in zip(scores, pairs):
        p = [jnp.exp2(s - top).astype(jnp.bfloat16) for s in pieces]
        wide = jnp.concatenate([v, jnp.ones_like(v)], axis=1)
        part = jnp.dot(jnp.concatenate(p, axis=1), wide, preferred_element_type=jnp.float32)
        total = part if total is None else total + part
    num, den = total[:, :HEAD], total[:, HEAD:]
    if state is not None:
        keep = jnp.exp2(state[1] - top)
        num, den = num + keep * state[0], den + keep * state[2]
    return num, top, den


def store_state(refs, cols, result, rows=slice(None)):
    for ref, value in zip(refs, result):
        ref[rows, cols] = value


def load_state(refs, cols, rows=slice(None)):
    return [ref[rows, cols] for ref in refs]


def both(pair, cols):
    return [(ref[0, :, cols], ref[1, :, cols]) for ref in pair]


def near_kernel(q0, q1, k, v, text, own, right, left, *state):
    for c in HEADS:
        ring_pairs = both((right, left), c)
        first = [(k[:, c], v[:, c]), (text[0, :, c], text[1, :, c])]
        store_state(state, c, attend(q0[:, c], first + ring_pairs), slice(0, COUNT))
        second = both((own,), c) + ring_pairs
        store_state(state, c, attend(q1[:, c], second), slice(COUNT, 2 * COUNT))


def far_kernel(q0, q1, *refs):
    blocks, state = refs[:-3], refs[-3:]
    for c in HEADS:
        q = jnp.concatenate([q0[:, c], q1[:, c]], axis=0)
        store_state(state, c, attend(q, both(blocks, c)))


def next_kernel(q0, q1, *refs):
    blocks, given, state = refs[:-6], refs[-6:-3], refs[-3:]
    for c in HEADS:
        q = jnp.concatenate([q0[:, c], q1[:, c]], axis=0)
        store_state(state, c, attend(q, both(blocks, c), load_state(given, c)))


def state_shapes(rows):
    return [jax.ShapeDtypeStruct((rows, WIDTH), jnp.float32)] * 3


def attend_cost(blocks):
    return cost(blocks * COUNT * COUNT * WIDTH * 4, 6 * MIB, blocks * COUNT * COUNT * LOCAL_HEADS)


def attend_call(kernel, blocks, *args):
    call = pl.pallas_call(
        kernel,
        in_specs=[FULL] * len(args),
        out_specs=[FULL] * 3,
        out_shape=state_shapes(2 * COUNT),
        compiler_params=params(24),
        cost_estimate=attend_cost(blocks),
    )
    return list(call(*args))


def pack(num, top, den):
    log = (top + jnp.log2(den)).T[:EXTRA, :]
    row = lax.broadcasted_iota(jnp.int32, log.shape, 0)
    parts = jnp.zeros_like(log)
    for n in range(3):
        rounded = log.astype(jnp.bfloat16).astype(jnp.float32)
        parts = jnp.where(row == n, rounded, parts)
        log = log - rounded
    return jnp.concatenate([num * (1.0 / den), parts], axis=0).astype(jnp.bfloat16)


def unpack(message):
    value = message[:HALF, :].astype(jnp.float32)
    stats = message[HALF:, :].astype(jnp.float32)
    log = stats[0:1, :] + (stats[1:2, :] + stats[2:3, :])
    return value, jnp.broadcast_to(log, (HALF, HEAD)).T, 1.0


def merge(*states):
    top = states[0][1]
    for s in states[1:]:
        top = jnp.maximum(top, s[1])
    num, den = 0.0, 0.0
    for n, m, d in states:
        keep = jnp.exp2(m - top)
        num, den = num + keep * n, den + keep * d
    return num, top, den


def last_kernel(q0, q1, keys, values, *refs):
    given, state, message = refs[:3], refs[3:6], refs[6]
    for c in HEADS:
        pairs = [(keys[:, c], values[:, c])]
        result = attend(q1[:, c], pairs, load_state(given, c, slice(COUNT, 2 * COUNT)))
        for n in range(2):
            message[n, :, c] = pack(*[a[n * HALF : (n + 1) * HALF] for a in result])
    for c in HEADS:
        pairs = [(keys[:, c], values[:, c])]
        store_state(state, c, attend(q0[:, c], pairs, load_state(given, c, slice(0, COUNT))))


def last_call(q0, q1, keys, values, *state):
    message = jax.ShapeDtypeStruct((2, HALF + EXTRA, WIDTH), jnp.bfloat16)
    *state, message = pl.pallas_call(
        last_kernel,
        in_specs=[FULL] * 7,
        out_specs=[FULL] * 4,
        out_shape=state_shapes(COUNT) + [message],
        compiler_params=params(24),
        cost_estimate=attend_cost(2),
    )(q0, q1, keys, values, *state)
    return state, message


def merge_kernel(*refs):
    swap = jnp.bitwise_and(lax.axis_index("y"), 1) == 1
    for block in range(2):
        state, message = refs[4 * block : 4 * block + 3], refs[4 * block + 3]
        mine, other = refs[8 + 2 * block : 10 + 2 * block]
        for c in HEADS:
            halves = []
            for n in range(2):
                part = load_state(state, c, slice(n * HALF, (n + 1) * HALF))
                both_cores = merge(part, unpack(message[n, :, c]))
                halves.append(pack(*both_cores).astype(jnp.float32))
            mine[:, c] = jnp.where(swap, halves[1], halves[0]).astype(jnp.bfloat16)
            other[:, c] = jnp.where(swap, halves[0], halves[1]).astype(jnp.bfloat16)


def merge_call(*args):
    return pl.pallas_call(
        merge_kernel,
        in_specs=[FULL] * 8,
        out_specs=[FULL] * 4,
        out_shape=[jax.ShapeDtypeStruct((HALF + EXTRA, WIDTH), jnp.bfloat16)] * 4,
        compiler_params=params(24),
        cost_estimate=cost(0, 4 * MIB),
    )(*args)


QUARTERS = ((0, 0), (1, 1), (1, 0), (0, 1))


def project_kernel(*refs):
    messages, w, w_pair, w_core = refs[:4], refs[4], refs[5:7], refs[7:9]
    outs, attn, full = refs[9:13], refs[13], refs[14]
    x, first = lax.axis_index("x_hi"), lax.axis_index("core") == 0
    high_y = lax.shift_right_logical(lax.axis_index("y"), 1)
    for n in range(2):
        for head in range(LOCAL_HEADS):
            c = head_of(head)
            num, _, den = merge(*[unpack(m[:, c]) for m in messages[2 * n : 2 * n + 2]])
            attn[:, head_of(LOCAL_HEADS * n + head)] = (num * (1.0 / den)).astype(jnp.bfloat16)
    low = attn[:, WIDTH : WIDTH + SPLIT].astype(jnp.float32)
    high = attn[:, WIDTH + SPLIT :].astype(jnp.float32)
    by_x = jnp.where(first, low, high).astype(jnp.bfloat16)
    by_core = jnp.where(first, high, low).astype(jnp.bfloat16)
    for at in range(0, MODEL, 768):
        cols = slice(at, at + 768)
        side, start = divmod(at, MODEL // 2)
        part = slice(start, start + 768)
        total = jnp.dot(attn[:, :WIDTH], w[:, cols], preferred_element_type=jnp.float32)
        total += jnp.dot(by_x, w_pair[side][:, part], preferred_element_type=jnp.float32)
        total += jnp.dot(by_core, w_core[side][:, part], preferred_element_type=jnp.float32)
        full[:, cols] = total.astype(jnp.bfloat16)
    for out, (dy, dx) in zip(outs, QUARTERS):
        to = jnp.bitwise_xor(high_y, dy) * 2 + jnp.bitwise_xor(x, dx)
        out[...] = full[pl.ds(pl.multiple_of(to * ROWS, ROWS), ROWS), :]


def project_call(messages, weights):
    return pl.pallas_call(
        project_kernel,
        in_specs=[FULL] * 9,
        out_specs=[FULL] * 4,
        out_shape=[jax.ShapeDtypeStruct((ROWS, MODEL), jnp.bfloat16)] * 4,
        scratch_shapes=[
            pltpu.VMEM((HALF, 2 * WIDTH), jnp.bfloat16),
            pltpu.VMEM((HALF, MODEL), jnp.bfloat16),
        ],
        compiler_params=params(24),
        cost_estimate=cost(2 * COUNT * WIDTH * MODEL, 5 * MIB),
    )(*messages, *weights)


def put_kernel(offsets, *refs):
    out, sems = refs[-2:]
    x, y = lax.axis_index("x_hi"), lax.axis_index("y")
    copies = []
    for n, (flip, step) in enumerate(offsets):
        from_y = lax.rem(y + 4 - step, 4)
        quarter = lax.shift_right_logical(from_y, 1) * 2 + (1 - x if flip else x)
        at = jnp.bitwise_and(from_y, 1) * HALF + quarter * ROWS
        rows = pl.ds(pl.multiple_of(at, ROWS), ROWS)
        copies.append(pltpu.make_async_copy(refs[n], out.at[rows], sems.at[n]))
    for copy in copies:
        copy.start()
    for copy in copies:
        copy.wait()


def put_call(offsets, pieces, out=None):
    anywhere = pl.BlockSpec(memory_space=pl.ANY)
    count = len(pieces)
    more = [] if out is None else [out]
    return pl.pallas_call(
        functools.partial(put_kernel, offsets),
        in_specs=[FULL] * count + [anywhere] * len(more),
        out_specs=anywhere,
        out_shape=jax.ShapeDtypeStruct((COUNT, MODEL), jnp.bfloat16),
        input_output_aliases={count: 0} if more else {},
        scratch_shapes=[pltpu.SemaphoreType.DMA((count,))],
        compiler_params=params(24),
        cost_estimate=cost(0, 4 * MIB),
    )(*pieces, *more)


def ring(value, axis, step):
    size = SIZES[AXES.index(axis)]
    return lax.ppermute(value, axis, [(i, (i + step) % size) for i in range(size)])


def beside_y(value):
    return lax.ppermute(value, "y", [(i, i ^ 1) for i in range(4)])


def crossed(value, axes):
    return lax.ppermute(value, axes, [(i, 3 - i) for i in range(4)])


def shards(
    latents,
    token_rows,
    mod_shift,
    mod_scale,
    mod_gate,
    w_qkv,
    q_gain,
    k_gain,
    stale_kv,
    text_kv,
    w_out,
    b_out,
):
    after = lax.optimization_barrier
    x, y = lax.axis_index("x_hi"), lax.axis_index("y")
    own = jnp.transpose(stale_kv, (1, 0, 2))
    r1, l1 = ring(own, "z", 1), ring(own, "z", -1)

    w = jnp.transpose(w_qkv, (1, 0, 2))
    q, k, v, *w_half = qkv_call(
        latents, w, token_rows, mod_shift, mod_scale, q_gain, k_gain, w_out
    )
    w_pair = [beside_y(w) for w in w_half]
    q_core, q_x = ring(q, "core", 1), ring(q, "x_lo", 1)

    r1, l1, q = after((r1, l1, q))
    r2, l2 = ring(r1, "z", 1), ring(l1, "z", -1)
    text = jnp.transpose(text_kv, (1, 0, 2))
    near = attend_call(near_kernel, 8, q, q_core, k, v, text, own, r1, l1)

    q_x, near[2] = after((q_x, near[2]))
    q_both = ring(q_x, "core", 1)
    r2, near[0] = after((r2, near[0]))
    r3 = ring(r2, "z", 1)
    l2, near[1] = after((l2, near[1]))
    l3 = ring(l2, "z", -1)
    near = attend_call(next_kernel, 4, q, q_core, r2, l2, *near)
    far = attend_call(far_kernel, 10, q_x, q_both, own, r1, l1, r2, l2)

    r3, near[0], far[0], w_pair[0] = after((r3, near[0], far[0], w_pair[0]))
    far_k = ring(r3[0], "z", 1)
    l3, near[1], far[1] = after((l3, near[1], far[1]))
    far_v = ring(l3[1], "z", -1)
    far = attend_call(next_kernel, 4, q_x, q_both, r3, l3, *far)
    near = attend_call(next_kernel, 4, q, q_core, r3, l3, *near)

    far_k, far_v, near[0], far[0] = after((far_k, far_v, near[0], far[0]))
    w_core = [ring(w_pair[0], "core", 1)]
    x_state, x_msg = last_call(q_x, q_both, far_k, far_v, *far)
    x_msg = ring(x_msg, "core", 1)
    o_state, o_msg = last_call(q, q_core, far_k, far_v, *near)
    o_msg = ring(o_msg, "core", 1)
    x_mine, x_other, o_mine, o_other = merge_call(*x_state, x_msg, *o_state, o_msg)
    from_y, from_x = beside_y(o_other), ring(x_mine, "x_lo", 1)
    from_both = lax.ppermute(
        x_other, ("x_lo", "y"), [(i, (1 - i // 4) * 4 + (i % 4 ^ 1)) for i in range(8)]
    )
    w_pair[1], o_mine = after((w_pair[1], o_mine))
    w_core.append(ring(w_pair[1], "core", 1))

    mine, both_ways, along_y, along_x = project_call(
        (o_mine, from_x, from_y, from_both), (w_out, *w_pair, *w_core)
    )
    parts = [
        lax.ppermute(both_ways, TENSOR, [(i, (i // 2 + 2) % 4 * 2 + (1 - i % 2)) for i in range(8)]),
        ring(along_y, "y", 2),
        ring(along_x, "x_hi", 1),
    ]
    start = y % 2 * HALF + (y // 2 * 2 + x) * ROWS
    rows = lax.dynamic_slice_in_dim(latents, start, ROWS, 0).astype(jnp.float32)
    total = mine.astype(jnp.float32)
    for part in parts:
        total = total + part.astype(jnp.float32)
    piece = (rows + mod_gate * (total + b_out)).astype(jnp.bfloat16)

    beside, two = ring(piece, "x_hi", 1), ring(piece, "y", 2)
    plus, minus = ring(piece, "y", 1), ring(piece, "y", -1)
    early = [
        ((0, 0), piece),
        ((1, 0), beside),
        ((0, 1), plus),
        ((0, -1), minus),
        ((0, 2), two),
    ]
    late = [
        ((1, 1), ring(beside, "y", 1)),
        ((1, -1), ring(beside, "y", -1)),
        ((1, 2), ring(two, "x_hi", 1)),
    ]
    out = put_call([e[0] for e in early], [e[1] for e in early])
    out = put_call([e[0] for e in late], [e[1] for e in late], out)
    return (out, jnp.stack([k, v], axis=1))


def solution(mesh):
    fine = Mesh(mesh.devices.reshape(SIZES), AXES)
    return jax.shard_map(
        shards,
        mesh=fine,
        in_specs=(
            P(PATCH, None),
            P(PATCH),
            P(),
            P(),
            P(),
            P(None, None, TENSOR),
            P(),
            P(),
            P(PATCH, None, TENSOR),
            P(None, None, TENSOR),
            P(TENSOR, None),
            P(),
        ),
        out_specs=(P(PATCH, None), P(PATCH, None, TENSOR)),
        check_vma=False,
    )
```

```python
import functools

import jax
import jax.numpy as jnp
import numpy as np
from jax import lax
from jax.experimental import pallas as pl
from jax.experimental.pallas import tpu as pltpu
from jax.sharding import Mesh
from jax.sharding import PartitionSpec as P

WIDTH_TOK = 256
ROW_POS = 8192 // WIDTH_TOK
HEAD = 128
LOCAL_HEADS = 3
WIDTH = HEAD * LOCAL_HEADS
COUNT = 256
TEXT = 512
MODEL = 3072
ROWS = COUNT // 8
WIDE = (slice(0, MODEL // 2), slice(MODEL // 2, MODEL))
AXES = ("x_lo", "z", "core", "y", "x_hi")
SIZES = (2, 8, 2, 4, 2)
PATCH = ("x_lo", "z", "core")
TENSOR = ("y", "x_hi")
SCALE = float(np.log2(np.e) / np.sqrt(128.0))
MIB = 1024 * 1024
EXTRA = 16
HALF = COUNT // 2
SPLIT = WIDTH // 2
FULL = pl.BlockSpec(memory_space=pltpu.VMEM)


def params(mib=48):
    return pltpu.CompilerParams(vmem_limit_bytes=mib * MIB)


def cost(flops, nbytes, exps=0):
    del flops, nbytes, exps
    return pl.CostEstimate(flops=1024, bytes_accessed=1024, transcendentals=0)


def coordinate(place, n):
    return jnp.max(place[n : n + 1, :]).astype(jnp.int32)


def head_of(head):
    return slice(head * HEAD, (head + 1) * HEAD)


HEADS = [head_of(n) for n in range(LOCAL_HEADS)]


def whole_spec(shape):
    return pl.BlockSpec(shape, lambda i: (0,) * len(shape))


def trig_parts():
    omega = 10000.0 ** (-2.0 * np.arange(28) / 56.0)
    by_row = np.repeat(np.concatenate([np.zeros(8), omega, np.zeros(28)]), 2).astype(np.float32)
    by_col = np.repeat(np.concatenate([np.zeros(36), omega]), 2).astype(np.float32)
    lanes = np.arange(HEAD)
    sign = np.where(lanes % 2 == 0, -1.0, 1.0)
    blocks = []
    for omegas, count, mine in ((by_row, ROW_POS, lanes < 72), (by_col, WIDTH_TOK, lanes >= 72)):
        angle = (np.arange(count, dtype=np.float32)[:, None] * omegas[None, :]).astype(np.float64)
        blocks.append(np.concatenate([np.cos(angle) * mine, np.sin(angle) * sign * mine], axis=1))
    rest = np.concatenate(blocks).astype(np.float32)
    parts = []
    for _ in range(3):
        parts.append(rest.astype(jnp.bfloat16))
        rest = rest - parts[-1].astype(np.float32)
    return np.concatenate(parts, axis=1)


def qkv_kernel(place, *refs):
    given, (q, k, v, *w_half), buffers, sems = refs[:9], refs[9:14], refs[14:-1], refs[-1]
    lat, w, trig, rows, shift, scale, q_gain, k_gain, half = buffers
    part = pl.ds(pl.multiple_of(coordinate(place, 2) * SPLIT, SPLIT), SPLIT)
    copy = lambda n, source, target: pltpu.make_async_copy(source, target, sems.at[n])
    weights = [copy(n, given[1].at[n], w.at[n]) for n in range(3)]
    small = [copy(n + 1, given[n], buffers[n]) for n in range(2, 8)]
    latents, half_in = copy(9, given[0], lat), copy(10, given[8].at[part], half)
    half_out = [copy(11 + n, half.at[:, cols], w_half[n]) for n, cols in enumerate(WIDE)]
    latents.start()
    for c in small:
        c.start()
    weights[0].start()

    for c in small:
        c.wait()
    at = lax.broadcasted_iota(jnp.int32, (ROW_POS + WIDTH_TOK, COUNT), 0)
    row_pos = lax.shift_right_logical(rows[...], 8)
    col_pos = jnp.bitwise_and(rows[...], WIDTH_TOK - 1) + ROW_POS
    hot = jnp.where((at == row_pos) | (at == col_pos), 1.0, 0.0).astype(jnp.bfloat16)
    turn = lax.dot_general(hot, trig[...], (((0,), (0,)), ((), ())), preferred_element_type=jnp.float32)
    turn = turn[:, : 2 * HEAD] + (turn[:, 2 * HEAD : 4 * HEAD] + turn[:, 4 * HEAD :])
    cosine, sine = turn[:, :HEAD], turn[:, HEAD:]
    even = lax.broadcasted_iota(jnp.int32, (COUNT, HEAD), 1) % 2 == 0

    latents.wait()
    weights[1].start()
    x = lat[...].astype(jnp.float32)
    centred = x - jnp.mean(x, axis=-1, keepdims=True)
    spread = jnp.mean(centred * centred, axis=-1, keepdims=True)
    y = centred * lax.rsqrt(spread + 1e-06) * (1.0 + scale[...]) + shift[...]
    normed = y.astype(jnp.bfloat16)

    def rotated(x, gain, factor):
        x = x * lax.rsqrt(jnp.mean(x * x, axis=-1, keepdims=True) + 1e-06) * gain[...]
        other = jnp.where(even, pltpu.roll(x, HEAD - 1, 1), pltpu.roll(x, 1, 1))
        x = x * cosine + other * sine
        return (x * factor if factor else x).astype(jnp.bfloat16)

    for n, (ref, gain, factor) in enumerate(((q, q_gain, SCALE), (k, k_gain, None), (v, None, None))):
        weights[n].wait()
        if n == 0:
            weights[2].start()
            half_in.start()
        out = jnp.dot(normed, w[n], preferred_element_type=jnp.float32)
        for c in HEADS:
            x = out[:, c]
            ref[:, c] = x.astype(jnp.bfloat16) if gain is None else rotated(x, gain, factor)
        if n == 1:
            half_in.wait()
            for c in half_out:
                c.start()
    for c in half_out:
        c.wait()


def qkv_call(place, latents, w, rows, shift, scale, q_gain, k_gain, w_out):
    anywhere = pl.BlockSpec(memory_space=pl.ANY)
    row = lambda a: a.reshape(1, a.shape[0])
    args = [latents, w, jnp.asarray(trig_parts())]
    args += [row(a) for a in (rows, shift, scale, q_gain, k_gain)]
    half = (SPLIT, MODEL)
    return pl.pallas_call(
        qkv_kernel,
        in_specs=[FULL] + [anywhere] * 9,
        out_specs=[FULL] * 3 + [anywhere] * 2,
        out_shape=[jax.ShapeDtypeStruct((COUNT, WIDTH), jnp.bfloat16)] * 3
        + [jax.ShapeDtypeStruct((SPLIT, MODEL // 2), jnp.bfloat16)] * 2,
        scratch_shapes=[pltpu.VMEM(a.shape, a.dtype) for a in args]
        + [pltpu.VMEM(half, jnp.bfloat16), pltpu.SemaphoreType.DMA((13,))],
        compiler_params=params(60),
        cost_estimate=cost(2 * COUNT * MODEL * WIDTH * 3, 10 * MIB),
    )(place, *args, w_out)


def attend(q, pairs, state=None):
    scores = []
    for k, _ in pairs:
        s = lax.dot_general(q, k, (((1,), (1,)), ((), ())), preferred_element_type=jnp.float32)
        scores.append([s[:, at : at + HEAD] for at in range(0, s.shape[1], HEAD)])
    top = None
    for piece in sum(scores, []):
        top = piece if top is None else jnp.maximum(top, piece)
    top = jnp.broadcast_to(jnp.max(top, axis=1, keepdims=True), top.shape)
    if state is not None:
        top = jnp.maximum(top, state[1])
    total = None
    for pieces, (_, v) in zip(scores, pairs):
        p = [jnp.exp2(s - top).astype(jnp.bfloat16) for s in pieces]
        wide = jnp.concatenate([v, jnp.ones_like(v)], axis=1)
        part = jnp.dot(jnp.concatenate(p, axis=1), wide, preferred_element_type=jnp.float32)
        total = part if total is None else total + part
    num, den = total[:, :HEAD], total[:, HEAD:]
    if state is not None:
        keep = jnp.exp2(state[1] - top)
        num, den = num + keep * state[0], den + keep * state[2]
    return num, top, den


def store_state(refs, cols, result, rows=slice(None)):
    for ref, value in zip(refs, result):
        ref[rows, cols] = value


def load_state(refs, cols, rows=slice(None)):
    return [ref[rows, cols] for ref in refs]


def both(pair, cols):
    return [(ref[0, :, cols], ref[1, :, cols]) for ref in pair]


def near_kernel(q0, q1, k, v, text, own, right, left, *state):
    for c in HEADS:
        ring_pairs = both((right, left), c)
        first = [(k[:, c], v[:, c]), (text[0, :, c], text[1, :, c])]
        store_state(state, c, attend(q0[:, c], first + ring_pairs), slice(0, COUNT))
        second = both((own,), c) + ring_pairs
        store_state(state, c, attend(q1[:, c], second), slice(COUNT, 2 * COUNT))


def far_kernel(q0, q1, *refs):
    blocks, state = refs[:-3], refs[-3:]
    for c in HEADS:
        q = jnp.concatenate([q0[:, c], q1[:, c]], axis=0)
        store_state(state, c, attend(q, both(blocks, c)))


def next_kernel(q0, q1, *refs):
    blocks, given, state = refs[:-6], refs[-6:-3], refs[-3:]
    for c in HEADS:
        q = jnp.concatenate([q0[:, c], q1[:, c]], axis=0)
        store_state(state, c, attend(q, both(blocks, c), load_state(given, c)))


def state_shapes(rows):
    return [jax.ShapeDtypeStruct((rows, WIDTH), jnp.float32)] * 3


def attend_cost(blocks):
    return cost(blocks * COUNT * COUNT * WIDTH * 4, 6 * MIB, blocks * COUNT * COUNT * LOCAL_HEADS)


def attend_call(kernel, blocks, *args):
    call = pl.pallas_call(
        kernel,
        in_specs=[FULL] * len(args),
        out_specs=[FULL] * 3,
        out_shape=state_shapes(2 * COUNT),
        compiler_params=params(24),
        cost_estimate=attend_cost(blocks),
    )
    return list(call(*args))


def pack(num, top, den):
    log = (top + jnp.log2(den)).T[:EXTRA, :]
    row = lax.broadcasted_iota(jnp.int32, log.shape, 0)
    parts = jnp.zeros_like(log)
    for n in range(3):
        rounded = log.astype(jnp.bfloat16).astype(jnp.float32)
        parts = jnp.where(row == n, rounded, parts)
        log = log - rounded
    return jnp.concatenate([num * (1.0 / den), parts], axis=0).astype(jnp.bfloat16)


def unpack(message):
    value = message[:HALF, :].astype(jnp.float32)
    stats = message[HALF:, :].astype(jnp.float32)
    log = stats[0:1, :] + (stats[1:2, :] + stats[2:3, :])
    return value, jnp.broadcast_to(log, (HALF, HEAD)).T, 1.0


def merge(*states):
    top = states[0][1]
    for s in states[1:]:
        top = jnp.maximum(top, s[1])
    num, den = 0.0, 0.0
    for n, m, d in states:
        keep = jnp.exp2(m - top)
        num, den = num + keep * n, den + keep * d
    return num, top, den


def last_kernel(q0, q1, keys, values, *refs):
    given, state, message = refs[:3], refs[3:6], refs[6]
    for c in HEADS:
        pairs = [(keys[:, c], values[:, c])]
        result = attend(q1[:, c], pairs, load_state(given, c, slice(COUNT, 2 * COUNT)))
        for n in range(2):
            message[n, :, c] = pack(*[a[n * HALF : (n + 1) * HALF] for a in result])
    for c in HEADS:
        pairs = [(keys[:, c], values[:, c])]
        store_state(state, c, attend(q0[:, c], pairs, load_state(given, c, slice(0, COUNT))))


def last_call(q0, q1, keys, values, *state):
    message = jax.ShapeDtypeStruct((2, HALF + EXTRA, WIDTH), jnp.bfloat16)
    *state, message = pl.pallas_call(
        last_kernel,
        in_specs=[FULL] * 7,
        out_specs=[FULL] * 4,
        out_shape=state_shapes(COUNT) + [message],
        compiler_params=params(24),
        cost_estimate=attend_cost(2),
    )(q0, q1, keys, values, *state)
    return state, message


def merge_kernel(place, *refs):
    swap = jnp.bitwise_and(coordinate(place, 1), 1) == 1
    for block in range(2):
        state, message = refs[4 * block : 4 * block + 3], refs[4 * block + 3]
        mine, other = refs[8 + 2 * block : 10 + 2 * block]
        for c in HEADS:
            halves = []
            for n in range(2):
                part = load_state(state, c, slice(n * HALF, (n + 1) * HALF))
                both_cores = merge(part, unpack(message[n, :, c]))
                halves.append(pack(*both_cores).astype(jnp.float32))
            mine[:, c] = jnp.where(swap, halves[1], halves[0]).astype(jnp.bfloat16)
            other[:, c] = jnp.where(swap, halves[0], halves[1]).astype(jnp.bfloat16)


def merge_call(place, *args):
    return pl.pallas_call(
        merge_kernel,
        in_specs=[FULL] * 9,
        out_specs=[FULL] * 4,
        out_shape=[jax.ShapeDtypeStruct((HALF + EXTRA, WIDTH), jnp.bfloat16)] * 4,
        compiler_params=params(24),
        cost_estimate=cost(0, 4 * MIB),
    )(place, *args)


QUARTERS = ((0, 0), (1, 1), (1, 0), (0, 1))


def project_kernel(place, *refs):
    messages, w, w_pair, w_core = refs[:4], refs[4], refs[5:7], refs[7:9]
    outs, attn, full = refs[9:13], refs[13], refs[14]
    x, first = coordinate(place, 0), coordinate(place, 2) == 0
    high_y = lax.shift_right_logical(coordinate(place, 1), 1)
    for n in range(2):
        for head in range(LOCAL_HEADS):
            c = head_of(head)
            num, _, den = merge(*[unpack(m[:, c]) for m in messages[2 * n : 2 * n + 2]])
            attn[:, head_of(LOCAL_HEADS * n + head)] = (num * (1.0 / den)).astype(jnp.bfloat16)
    low = attn[:, WIDTH : WIDTH + SPLIT].astype(jnp.float32)
    high = attn[:, WIDTH + SPLIT :].astype(jnp.float32)
    by_x = jnp.where(first, low, high).astype(jnp.bfloat16)
    by_core = jnp.where(first, high, low).astype(jnp.bfloat16)
    for at in range(0, MODEL, 768):
        cols = slice(at, at + 768)
        side, start = divmod(at, MODEL // 2)
        part = slice(start, start + 768)
        total = jnp.dot(attn[:, :WIDTH], w[:, cols], preferred_element_type=jnp.float32)
        total += jnp.dot(by_x, w_pair[side][:, part], preferred_element_type=jnp.float32)
        total += jnp.dot(by_core, w_core[side][:, part], preferred_element_type=jnp.float32)
        full[:, cols] = total.astype(jnp.bfloat16)
    for out, (dy, dx) in zip(outs, QUARTERS):
        to = jnp.bitwise_xor(high_y, dy) * 2 + jnp.bitwise_xor(x, dx)
        out[...] = full[pl.ds(pl.multiple_of(to * ROWS, ROWS), ROWS), :]


def project_call(place, messages, weights):
    return pl.pallas_call(
        project_kernel,
        in_specs=[FULL] * 10,
        out_specs=[FULL] * 4,
        out_shape=[jax.ShapeDtypeStruct((ROWS, MODEL), jnp.bfloat16)] * 4,
        scratch_shapes=[
            pltpu.VMEM((HALF, 2 * WIDTH), jnp.bfloat16),
            pltpu.VMEM((HALF, MODEL), jnp.bfloat16),
        ],
        compiler_params=params(24),
        cost_estimate=cost(2 * COUNT * WIDTH * MODEL, 5 * MIB),
    )(place, *messages, *weights)


def put_kernel(offsets, place, *refs):
    out, sems = refs[-2:]
    x, y = coordinate(place, 0), coordinate(place, 1)
    copies = []
    for n, (flip, step) in enumerate(offsets):
        from_y = lax.rem(y + 4 - step, 4)
        quarter = lax.shift_right_logical(from_y, 1) * 2 + (1 - x if flip else x)
        at = jnp.bitwise_and(from_y, 1) * HALF + quarter * ROWS
        rows = pl.ds(pl.multiple_of(at, ROWS), ROWS)
        copies.append(pltpu.make_async_copy(refs[n], out.at[rows], sems.at[n]))
    for copy in copies:
        copy.start()
    for copy in copies:
        copy.wait()


def put_call(place, offsets, pieces, out=None):
    anywhere = pl.BlockSpec(memory_space=pl.ANY)
    count = len(pieces)
    more = [] if out is None else [out]
    return pl.pallas_call(
        functools.partial(put_kernel, offsets),
        in_specs=[FULL] * (count + 1) + [anywhere] * len(more),
        out_specs=anywhere,
        out_shape=jax.ShapeDtypeStruct((COUNT, MODEL), jnp.bfloat16),
        input_output_aliases={count + 1: 0} if more else {},
        scratch_shapes=[pltpu.SemaphoreType.DMA((count,))],
        compiler_params=params(24),
        cost_estimate=cost(0, 4 * MIB),
    )(place, *pieces, *more)


def ring(value, axis, step):
    size = SIZES[AXES.index(axis)]
    return lax.ppermute(value, axis, [(i, (i + step) % size) for i in range(size)])


def beside_y(value):
    return lax.ppermute(value, "y", [(i, i ^ 1) for i in range(4)])


def crossed(value, axes):
    return lax.ppermute(value, axes, [(i, 3 - i) for i in range(4)])


def shards(
    latents,
    token_rows,
    mod_shift,
    mod_scale,
    mod_gate,
    w_qkv,
    q_gain,
    k_gain,
    stale_kv,
    text_kv,
    w_out,
    b_out,
):
    after = lax.optimization_barrier
    x, y = lax.axis_index("x_hi"), lax.axis_index("y")
    place = jnp.stack([x, y, lax.axis_index("core")] + [0] * 5).astype(jnp.float32)
    place = jnp.broadcast_to(place[:, None], (8, HEAD))
    own = jnp.transpose(stale_kv, (1, 0, 2))
    r1, l1 = ring(own, "z", 1), ring(own, "z", -1)

    w = jnp.transpose(w_qkv, (1, 0, 2))
    q, k, v, *w_half = qkv_call(
        place, latents, w, token_rows, mod_shift, mod_scale, q_gain, k_gain, w_out
    )
    w_pair = [beside_y(w) for w in w_half]
    q_core, q_x = ring(q, "core", 1), ring(q, "x_lo", 1)

    r1, l1, q = after((r1, l1, q))
    r2, l2 = ring(r1, "z", 1), ring(l1, "z", -1)
    text = jnp.transpose(text_kv, (1, 0, 2))
    near = attend_call(near_kernel, 8, q, q_core, k, v, text, own, r1, l1)

    q_x, near[2] = after((q_x, near[2]))
    q_both = ring(q_x, "core", 1)
    r2, near[0] = after((r2, near[0]))
    r3 = ring(r2, "z", 1)
    l2, near[1] = after((l2, near[1]))
    l3 = ring(l2, "z", -1)
    near = attend_call(next_kernel, 4, q, q_core, r2, l2, *near)
    far = attend_call(far_kernel, 10, q_x, q_both, own, r1, l1, r2, l2)

    r3, near[0], far[0], w_pair[0] = after((r3, near[0], far[0], w_pair[0]))
    far_k = ring(r3[0], "z", 1)
    l3, near[1], far[1] = after((l3, near[1], far[1]))
    far_v = ring(l3[1], "z", -1)
    far = attend_call(next_kernel, 4, q_x, q_both, r3, l3, *far)
    near = attend_call(next_kernel, 4, q, q_core, r3, l3, *near)

    far_k, far_v, near[0], far[0] = after((far_k, far_v, near[0], far[0]))
    w_core = [ring(w_pair[0], "core", 1)]
    x_state, x_msg = last_call(q_x, q_both, far_k, far_v, *far)
    x_msg = ring(x_msg, "core", 1)
    o_state, o_msg = last_call(q, q_core, far_k, far_v, *near)
    o_msg = ring(o_msg, "core", 1)
    x_mine, x_other, o_mine, o_other = merge_call(place, *x_state, x_msg, *o_state, o_msg)
    from_y, from_x = beside_y(o_other), ring(x_mine, "x_lo", 1)
    from_both = lax.ppermute(
        x_other, ("x_lo", "y"), [(i, (1 - i // 4) * 4 + (i % 4 ^ 1)) for i in range(8)]
    )
    w_pair[1], o_mine = after((w_pair[1], o_mine))
    w_core.append(ring(w_pair[1], "core", 1))

    mine, both_ways, along_y, along_x = project_call(
        place, (o_mine, from_x, from_y, from_both), (w_out, *w_pair, *w_core)
    )
    parts = [
        lax.ppermute(both_ways, TENSOR, [(i, (i // 2 + 2) % 4 * 2 + (1 - i % 2)) for i in range(8)]),
        ring(along_y, "y", 2),
        ring(along_x, "x_hi", 1),
    ]
    start = y % 2 * HALF + (y // 2 * 2 + x) * ROWS
    rows = lax.dynamic_slice_in_dim(latents, start, ROWS, 0).astype(jnp.float32)
    total = mine.astype(jnp.float32)
    for part in parts:
        total = total + part.astype(jnp.float32)
    piece = (rows + mod_gate * (total + b_out)).astype(jnp.bfloat16)

    beside, two = ring(piece, "x_hi", 1), ring(piece, "y", 2)
    plus, minus = ring(piece, "y", 1), ring(piece, "y", -1)
    early = [
        ((0, 0), piece),
        ((1, 0), beside),
        ((0, 1), plus),
        ((0, -1), minus),
        ((0, 2), two),
    ]
    late = [
        ((1, 1), ring(beside, "y", 1)),
        ((1, -1), ring(beside, "y", -1)),
        ((1, 2), ring(two, "x_hi", 1)),
    ]
    out = put_call(place, [e[0] for e in early], [e[1] for e in early])
    out = put_call(place, [e[0] for e in late], [e[1] for e in late], out)
    return (out, jnp.stack([k, v], axis=1))


def solution(mesh):
    fine = Mesh(mesh.devices.reshape(SIZES), AXES)
    return jax.shard_map(
        shards,
        mesh=fine,
        in_specs=(
            P(PATCH, None),
            P(PATCH),
            P(),
            P(),
            P(),
            P(None, None, TENSOR),
            P(),
            P(),
            P(PATCH, None, TENSOR),
            P(None, None, TENSOR),
            P(TENSOR, None),
            P(),
        ),
        out_specs=(P(PATCH, None), P(PATCH, None, TENSOR)),
        check_vma=False,
    )
```

```python
import functools

import jax
import jax.numpy as jnp
import numpy as np
from jax import lax
from jax.experimental import pallas as pl
from jax.experimental.pallas import tpu as pltpu
from jax.sharding import Mesh
from jax.sharding import PartitionSpec as P

WIDTH_TOK = 256
ROW_POS = 8192 // WIDTH_TOK
HEAD = 128
LOCAL_HEADS = 3
WIDTH = HEAD * LOCAL_HEADS
COUNT = 256
TEXT = 512
MODEL = 3072
ROWS = COUNT // 8
AXES = ("x_lo", "z", "core", "y", "x_hi")
SIZES = (2, 8, 2, 4, 2)
PATCH = ("x_lo", "z", "core")
TENSOR = ("y", "x_hi")
SCALE = float(np.log2(np.e) / np.sqrt(128.0))
MIB = 1024 * 1024
EXTRA = 16
HALF = COUNT // 2
SPLIT = WIDTH // 2
FULL = pl.BlockSpec(memory_space=pltpu.VMEM)


def params(mib=48):
    return pltpu.CompilerParams(vmem_limit_bytes=mib * MIB)


def cost(flops, nbytes, exps=0):
    del flops, nbytes, exps
    return pl.CostEstimate(flops=1024, bytes_accessed=1024, transcendentals=0)


def coordinate(place, n):
    return jnp.max(place[n : n + 1, :]).astype(jnp.int32)


def head_of(head):
    return slice(head * HEAD, (head + 1) * HEAD)


HEADS = [head_of(n) for n in range(LOCAL_HEADS)]


def whole_spec(shape):
    return pl.BlockSpec(shape, lambda i: (0,) * len(shape))


def trig_parts():
    omega = 10000.0 ** (-2.0 * np.arange(28) / 56.0)
    by_row = np.repeat(np.concatenate([np.zeros(8), omega, np.zeros(28)]), 2).astype(np.float32)
    by_col = np.repeat(np.concatenate([np.zeros(36), omega]), 2).astype(np.float32)
    lanes = np.arange(HEAD)
    sign = np.where(lanes % 2 == 0, -1.0, 1.0)
    blocks = []
    for omegas, count, mine in ((by_row, ROW_POS, lanes < 72), (by_col, WIDTH_TOK, lanes >= 72)):
        angle = (np.arange(count, dtype=np.float32)[:, None] * omegas[None, :]).astype(np.float64)
        blocks.append(np.concatenate([np.cos(angle) * mine, np.sin(angle) * sign * mine], axis=1))
    rest = np.concatenate(blocks).astype(np.float32)
    parts = []
    for _ in range(3):
        parts.append(rest.astype(jnp.bfloat16))
        rest = rest - parts[-1].astype(np.float32)
    return np.concatenate(parts, axis=1)


def qkv_kernel(place, *refs):
    given, (q, k, v, w_half), buffers, sems = refs[:9], refs[9:13], refs[13:-1], refs[-1]
    lat, w, trig, rows, shift, scale, q_gain, k_gain, half = buffers
    copy = lambda n, source, target: pltpu.make_async_copy(source, target, sems.at[n])
    weights = [copy(n, given[1].at[n], w.at[n]) for n in range(3)]
    small = [copy(n + 1, given[n], buffers[n]) for n in range(2, 8)]
    latents, half_out = copy(9, given[0], lat), copy(11, half, w_half)
    latents.start()
    for c in small:
        c.start()
    weights[0].start()

    for c in small:
        c.wait()
    at = lax.broadcasted_iota(jnp.int32, (ROW_POS + WIDTH_TOK, COUNT), 0)
    row_pos = lax.shift_right_logical(rows[...], 8)
    col_pos = jnp.bitwise_and(rows[...], WIDTH_TOK - 1) + ROW_POS
    hot = jnp.where((at == row_pos) | (at == col_pos), 1.0, 0.0).astype(jnp.bfloat16)
    turn = lax.dot_general(hot, trig[...], (((0,), (0,)), ((), ())), preferred_element_type=jnp.float32)
    turn = turn[:, : 2 * HEAD] + (turn[:, 2 * HEAD : 4 * HEAD] + turn[:, 4 * HEAD :])
    cosine, sine = turn[:, :HEAD], turn[:, HEAD:]
    even = lax.broadcasted_iota(jnp.int32, (COUNT, HEAD), 1) % 2 == 0

    latents.wait()
    weights[1].start()
    x = lat[...].astype(jnp.float32)
    centred = x - jnp.mean(x, axis=-1, keepdims=True)
    spread = jnp.mean(centred * centred, axis=-1, keepdims=True)
    y = centred * lax.rsqrt(spread + 1e-06) * (1.0 + scale[...]) + shift[...]
    normed = y.astype(jnp.bfloat16)

    def rotated(x, gain, factor):
        x = x * lax.rsqrt(jnp.mean(x * x, axis=-1, keepdims=True) + 1e-06) * gain[...]
        other = jnp.where(even, pltpu.roll(x, HEAD - 1, 1), pltpu.roll(x, 1, 1))
        x = x * cosine + other * sine
        return (x * factor if factor else x).astype(jnp.bfloat16)

    for n, (ref, gain, factor) in enumerate(((q, q_gain, SCALE), (k, k_gain, None), (v, None, None))):
        weights[n].wait()
        if n == 0:
            weights[2].start()
            part = pl.ds(pl.multiple_of(coordinate(place, 2) * SPLIT, SPLIT), SPLIT)
            half_in = copy(10, given[8].at[part], half)
            half_in.start()
        out = jnp.dot(normed, w[n], preferred_element_type=jnp.float32)
        for c in HEADS:
            x = out[:, c]
            ref[:, c] = x.astype(jnp.bfloat16) if gain is None else rotated(x, gain, factor)
        if n == 1:
            half_in.wait()
            half_out.start()
    half_out.wait()


def qkv_call(place, latents, w, rows, shift, scale, q_gain, k_gain, w_out):
    anywhere = pl.BlockSpec(memory_space=pl.ANY)
    row = lambda a: a.reshape(1, a.shape[0])
    args = [latents, w, jnp.asarray(trig_parts())]
    args += [row(a) for a in (rows, shift, scale, q_gain, k_gain)]
    half = (SPLIT, MODEL)
    return pl.pallas_call(
        qkv_kernel,
        in_specs=[FULL] + [anywhere] * 9,
        out_specs=[FULL] * 3 + [anywhere],
        out_shape=[jax.ShapeDtypeStruct((COUNT, WIDTH), jnp.bfloat16)] * 3
        + [jax.ShapeDtypeStruct(half, jnp.bfloat16)],
        scratch_shapes=[pltpu.VMEM(a.shape, a.dtype) for a in args]
        + [pltpu.VMEM(half, jnp.bfloat16), pltpu.SemaphoreType.DMA((12,))],
        compiler_params=params(60),
        cost_estimate=cost(2 * COUNT * MODEL * WIDTH * 3, 10 * MIB),
    )(place, *args, w_out)


def attend(q, pairs, state=None):
    scores = []
    for k, _ in pairs:
        s = lax.dot_general(q, k, (((1,), (1,)), ((), ())), preferred_element_type=jnp.float32)
        scores.append([s[:, at : at + HEAD] for at in range(0, s.shape[1], HEAD)])
    top = None
    for piece in sum(scores, []):
        top = piece if top is None else jnp.maximum(top, piece)
    top = jnp.broadcast_to(jnp.max(top, axis=1, keepdims=True), top.shape)
    if state is not None:
        top = jnp.maximum(top, state[1])
    total = None
    for pieces, (_, v) in zip(scores, pairs):
        p = [jnp.exp2(s - top).astype(jnp.bfloat16) for s in pieces]
        wide = jnp.concatenate([v, jnp.ones_like(v)], axis=1)
        part = jnp.dot(jnp.concatenate(p, axis=1), wide, preferred_element_type=jnp.float32)
        total = part if total is None else total + part
    num, den = total[:, :HEAD], total[:, HEAD:]
    if state is not None:
        keep = jnp.exp2(state[1] - top)
        num, den = num + keep * state[0], den + keep * state[2]
    return num, top, den


def store_state(refs, cols, result, rows=slice(None)):
    for ref, value in zip(refs, result):
        ref[rows, cols] = value


def load_state(refs, cols, rows=slice(None)):
    return [ref[rows, cols] for ref in refs]


def both(pair, cols):
    return [(ref[0, :, cols], ref[1, :, cols]) for ref in pair]


def near_kernel(q0, q1, k, v, text, own, right, left, *state):
    for c in HEADS:
        ring_pairs = both((right, left), c)
        first = [(k[:, c], v[:, c]), (text[0, :, c], text[1, :, c])]
        store_state(state, c, attend(q0[:, c], first + ring_pairs), slice(0, COUNT))
        second = both((own,), c) + ring_pairs
        store_state(state, c, attend(q1[:, c], second), slice(COUNT, 2 * COUNT))


def far_kernel(q0, q1, *refs):
    blocks, state = refs[:-3], refs[-3:]
    for c in HEADS:
        q = jnp.concatenate([q0[:, c], q1[:, c]], axis=0)
        store_state(state, c, attend(q, both(blocks, c)))


def next_kernel(q0, q1, *refs):
    blocks, given, state = refs[:-6], refs[-6:-3], refs[-3:]
    for c in HEADS:
        q = jnp.concatenate([q0[:, c], q1[:, c]], axis=0)
        store_state(state, c, attend(q, both(blocks, c), load_state(given, c)))


def state_shapes(rows):
    return [jax.ShapeDtypeStruct((rows, WIDTH), jnp.float32)] * 3


def attend_cost(blocks):
    return cost(blocks * COUNT * COUNT * WIDTH * 4, 6 * MIB, blocks * COUNT * COUNT * LOCAL_HEADS)


def attend_call(kernel, blocks, *args):
    call = pl.pallas_call(
        kernel,
        in_specs=[FULL] * len(args),
        out_specs=[FULL] * 3,
        out_shape=state_shapes(2 * COUNT),
        compiler_params=params(24),
        cost_estimate=attend_cost(blocks),
    )
    return list(call(*args))


def pack(num, top, den):
    log = (top + jnp.log2(den)).T[:EXTRA, :]
    row = lax.broadcasted_iota(jnp.int32, log.shape, 0)
    parts = jnp.zeros_like(log)
    for n in range(3):
        rounded = log.astype(jnp.bfloat16).astype(jnp.float32)
        parts = jnp.where(row == n, rounded, parts)
        log = log - rounded
    return jnp.concatenate([num * (1.0 / den), parts], axis=0).astype(jnp.bfloat16)


def unpack(message):
    value = message[:HALF, :].astype(jnp.float32)
    stats = message[HALF:, :].astype(jnp.float32)
    log = stats[0:1, :] + (stats[1:2, :] + stats[2:3, :])
    return value, jnp.broadcast_to(log, (HALF, HEAD)).T, 1.0


def merge(*states):
    top = states[0][1]
    for s in states[1:]:
        top = jnp.maximum(top, s[1])
    num, den = 0.0, 0.0
    for n, m, d in states:
        keep = jnp.exp2(m - top)
        num, den = num + keep * n, den + keep * d
    return num, top, den


def last_kernel(q0, q1, keys, values, *refs):
    given, state, message = refs[:3], refs[3:6], refs[6]
    for c in HEADS:
        pairs = [(keys[:, c], values[:, c])]
        result = attend(q1[:, c], pairs, load_state(given, c, slice(COUNT, 2 * COUNT)))
        for n in range(2):
            message[n, :, c] = pack(*[a[n * HALF : (n + 1) * HALF] for a in result])
    for c in HEADS:
        pairs = [(keys[:, c], values[:, c])]
        store_state(state, c, attend(q0[:, c], pairs, load_state(given, c, slice(0, COUNT))))


def last_call(q0, q1, keys, values, *state):
    message = jax.ShapeDtypeStruct((2, HALF + EXTRA, WIDTH), jnp.bfloat16)
    *state, message = pl.pallas_call(
        last_kernel,
        in_specs=[FULL] * 7,
        out_specs=[FULL] * 4,
        out_shape=state_shapes(COUNT) + [message],
        compiler_params=params(24),
        cost_estimate=attend_cost(2),
    )(q0, q1, keys, values, *state)
    return state, message


def merge_kernel(place, *refs):
    swap = jnp.bitwise_and(coordinate(place, 1), 1) == 1
    for block in range(2):
        state, message = refs[4 * block : 4 * block + 3], refs[4 * block + 3]
        mine, other = refs[8 + 2 * block : 10 + 2 * block]
        for c in HEADS:
            halves = []
            for n in range(2):
                part = load_state(state, c, slice(n * HALF, (n + 1) * HALF))
                both_cores = merge(part, unpack(message[n, :, c]))
                halves.append(pack(*both_cores).astype(jnp.float32))
            mine[:, c] = jnp.where(swap, halves[1], halves[0]).astype(jnp.bfloat16)
            other[:, c] = jnp.where(swap, halves[0], halves[1]).astype(jnp.bfloat16)


def merge_call(place, *args):
    return pl.pallas_call(
        merge_kernel,
        in_specs=[FULL] * 9,
        out_specs=[FULL] * 4,
        out_shape=[jax.ShapeDtypeStruct((HALF + EXTRA, WIDTH), jnp.bfloat16)] * 4,
        compiler_params=params(24),
        cost_estimate=cost(0, 4 * MIB),
    )(place, *args)


QUARTERS = ((0, 0), (1, 1), (1, 0), (0, 1))


def project_kernel(place, *refs):
    messages, (w, w_pair, w_core) = refs[:4], refs[4:7]
    outs, attn, full = refs[7:11], refs[11], refs[12]
    x, first = coordinate(place, 0), coordinate(place, 2) == 0
    high_y = lax.shift_right_logical(coordinate(place, 1), 1)
    for n in range(2):
        for head in range(LOCAL_HEADS):
            c = head_of(head)
            num, _, den = merge(*[unpack(m[:, c]) for m in messages[2 * n : 2 * n + 2]])
            attn[:, head_of(LOCAL_HEADS * n + head)] = (num * (1.0 / den)).astype(jnp.bfloat16)
    low = attn[:, WIDTH : WIDTH + SPLIT].astype(jnp.float32)
    high = attn[:, WIDTH + SPLIT :].astype(jnp.float32)
    by_x = jnp.where(first, low, high).astype(jnp.bfloat16)
    by_core = jnp.where(first, high, low).astype(jnp.bfloat16)
    for at in range(0, MODEL, 768):
        cols = slice(at, at + 768)
        total = jnp.dot(attn[:, :WIDTH], w[:, cols], preferred_element_type=jnp.float32)
        total += jnp.dot(by_x, w_pair[:, cols], preferred_element_type=jnp.float32)
        total += jnp.dot(by_core, w_core[:, cols], preferred_element_type=jnp.float32)
        full[:, cols] = total.astype(jnp.bfloat16)
    for out, (dy, dx) in zip(outs, QUARTERS):
        to = jnp.bitwise_xor(high_y, dy) * 2 + jnp.bitwise_xor(x, dx)
        out[...] = full[pl.ds(pl.multiple_of(to * ROWS, ROWS), ROWS), :]


def project_call(place, messages, weights):
    return pl.pallas_call(
        project_kernel,
        in_specs=[FULL] * 8,
        out_specs=[FULL] * 4,
        out_shape=[jax.ShapeDtypeStruct((ROWS, MODEL), jnp.bfloat16)] * 4,
        scratch_shapes=[
            pltpu.VMEM((HALF, 2 * WIDTH), jnp.bfloat16),
            pltpu.VMEM((HALF, MODEL), jnp.bfloat16),
        ],
        compiler_params=params(24),
        cost_estimate=cost(2 * COUNT * WIDTH * MODEL, 5 * MIB),
    )(place, *messages, *weights)


def put_kernel(offsets, place, *refs):
    out, sems = refs[-2:]
    x, y = coordinate(place, 0), coordinate(place, 1)
    copies = []
    for n, (flip, step) in enumerate(offsets):
        from_y = lax.rem(y + 4 - step, 4)
        quarter = lax.shift_right_logical(from_y, 1) * 2 + (1 - x if flip else x)
        at = jnp.bitwise_and(from_y, 1) * HALF + quarter * ROWS
        rows = pl.ds(pl.multiple_of(at, ROWS), ROWS)
        copies.append(pltpu.make_async_copy(refs[n], out.at[rows], sems.at[n]))
    for copy in copies:
        copy.start()
    for copy in copies:
        copy.wait()


def put_call(place, offsets, pieces, out=None):
    anywhere = pl.BlockSpec(memory_space=pl.ANY)
    count = len(pieces)
    more = [] if out is None else [out]
    return pl.pallas_call(
        functools.partial(put_kernel, offsets),
        in_specs=[FULL] * (count + 1) + [anywhere] * len(more),
        out_specs=anywhere,
        out_shape=jax.ShapeDtypeStruct((COUNT, MODEL), jnp.bfloat16),
        input_output_aliases={count + 1: 0} if more else {},
        scratch_shapes=[pltpu.SemaphoreType.DMA((count,))],
        compiler_params=params(24),
        cost_estimate=cost(0, 4 * MIB),
    )(place, *pieces, *more)


def ring(value, axis, step):
    size = SIZES[AXES.index(axis)]
    return lax.ppermute(value, axis, [(i, (i + step) % size) for i in range(size)])


def beside_y(value):
    return lax.ppermute(value, "y", [(i, i ^ 1) for i in range(4)])


def crossed(value, axes):
    return lax.ppermute(value, axes, [(i, 3 - i) for i in range(4)])


def shards(
    latents,
    token_rows,
    mod_shift,
    mod_scale,
    mod_gate,
    w_qkv,
    q_gain,
    k_gain,
    stale_kv,
    text_kv,
    w_out,
    b_out,
):
    after = lax.optimization_barrier
    x, y = lax.axis_index("x_hi"), lax.axis_index("y")
    place = jnp.stack([x, y, lax.axis_index("core")] + [0] * 5).astype(jnp.float32)
    place = jnp.broadcast_to(place[:, None], (8, HEAD))
    own = jnp.transpose(stale_kv, (1, 0, 2))
    r1, l1 = ring(own, "z", 1), ring(own, "z", -1)

    w = jnp.transpose(w_qkv, (1, 0, 2))
    q, k, v, w_half = qkv_call(
        place, latents, w, token_rows, mod_shift, mod_scale, q_gain, k_gain, w_out
    )
    w_pair = beside_y(w_half)
    q_core, q_x = ring(q, "core", 1), ring(q, "x_lo", 1)

    r1, l1, q = after((r1, l1, q))
    r2, l2 = ring(r1, "z", 1), ring(l1, "z", -1)
    text = jnp.transpose(text_kv, (1, 0, 2))
    near = attend_call(near_kernel, 8, q, q_core, k, v, text, own, r1, l1)

    q_x, near[2] = after((q_x, near[2]))
    q_both = ring(q_x, "core", 1)
    r2, near[0] = after((r2, near[0]))
    r3 = ring(r2, "z", 1)
    l2, near[1] = after((l2, near[1]))
    l3 = ring(l2, "z", -1)
    near = attend_call(next_kernel, 4, q, q_core, r2, l2, *near)
    far = attend_call(far_kernel, 10, q_x, q_both, own, r1, l1, r2, l2)

    r3, near[0], far[0] = after((r3, near[0], far[0]))
    far_k = ring(r3[0], "z", 1)
    l3, near[1], far[1] = after((l3, near[1], far[1]))
    far_v = ring(l3[1], "z", -1)
    far = attend_call(next_kernel, 4, q_x, q_both, r3, l3, *far)
    near = attend_call(next_kernel, 4, q, q_core, r3, l3, *near)

    far_k, far_v, near[0], far[0] = after((far_k, far_v, near[0], far[0]))
    x_state, x_msg = last_call(q_x, q_both, far_k, far_v, *far)
    x_msg = ring(x_msg, "core", 1)
    o_state, o_msg = last_call(q, q_core, far_k, far_v, *near)
    w_pair, o_msg = after((w_pair, o_msg))
    o_msg = ring(o_msg, "core", 1)
    w_core = ring(w_pair, "core", 1)
    x_mine, x_other, o_mine, o_other = merge_call(place, *x_state, x_msg, *o_state, o_msg)
    from_y, from_x = beside_y(o_other), ring(x_mine, "x_lo", 1)
    from_both = lax.ppermute(
        x_other, ("x_lo", "y"), [(i, (1 - i // 4) * 4 + (i % 4 ^ 1)) for i in range(8)]
    )

    mine, both_ways, along_y, along_x = project_call(
        place, (o_mine, from_x, from_y, from_both), (w_out, w_pair, w_core)
    )
    parts = [
        lax.ppermute(both_ways, TENSOR, [(i, (i // 2 + 2) % 4 * 2 + (1 - i % 2)) for i in range(8)]),
        ring(along_y, "y", 2),
        ring(along_x, "x_hi", 1),
    ]
    start = y % 2 * HALF + (y // 2 * 2 + x) * ROWS
    rows = lax.dynamic_slice_in_dim(latents, start, ROWS, 0).astype(jnp.float32)
    total = mine.astype(jnp.float32)
    for part in parts:
        total = total + part.astype(jnp.float32)
    piece = (rows + mod_gate * (total + b_out)).astype(jnp.bfloat16)

    beside, two = ring(piece, "x_hi", 1), ring(piece, "y", 2)
    plus, minus = ring(piece, "y", 1), ring(piece, "y", -1)
    early = [
        ((0, 0), piece),
        ((1, 0), beside),
        ((0, 1), plus),
        ((0, -1), minus),
        ((0, 2), two),
    ]
    late = [
        ((1, 1), ring(beside, "y", 1)),
        ((1, -1), ring(beside, "y", -1)),
        ((1, 2), ring(two, "x_hi", 1)),
    ]
    out = put_call(place, [e[0] for e in early], [e[1] for e in early])
    out = put_call(place, [e[0] for e in late], [e[1] for e in late], out)
    return (out, jnp.stack([k, v], axis=1))


def solution(mesh):
    fine = Mesh(mesh.devices.reshape(SIZES), AXES)
    return jax.shard_map(
        shards,
        mesh=fine,
        in_specs=(
            P(PATCH, None),
            P(PATCH),
            P(),
            P(),
            P(),
            P(None, None, TENSOR),
            P(),
            P(),
            P(PATCH, None, TENSOR),
            P(None, None, TENSOR),
            P(TENSOR, None),
            P(),
        ),
        out_specs=(P(PATCH, None), P(PATCH, None, TENSOR)),
        check_vma=False,
    )
```

```python
import functools

import jax
import jax.numpy as jnp
import numpy as np
from jax import lax
from jax.experimental import pallas as pl
from jax.experimental.pallas import tpu as pltpu
from jax.sharding import Mesh
from jax.sharding import PartitionSpec as P

WIDTH_TOK = 256
ROW_POS = 8192 // WIDTH_TOK
HEAD = 128
LOCAL_HEADS = 3
WIDTH = HEAD * LOCAL_HEADS
COUNT = 256
TEXT = 512
MODEL = 3072
ROWS = COUNT // 8
AXES = ("x_lo", "z", "core", "y", "x_hi")
SIZES = (2, 8, 2, 4, 2)
PATCH = ("x_lo", "z", "core")
TENSOR = ("y", "x_hi")
SCALE = float(np.log2(np.e) / np.sqrt(128.0))
MIB = 1024 * 1024
EXTRA = 16
HALF = COUNT // 2
SPLIT = WIDTH // 2
FULL = pl.BlockSpec(memory_space=pltpu.VMEM)


def params(mib=48):
    return pltpu.CompilerParams(vmem_limit_bytes=mib * MIB)


def cost(flops, nbytes, exps=0):
    del flops, nbytes, exps
    return pl.CostEstimate(flops=1024, bytes_accessed=1024, transcendentals=0)


def coordinate(place, n):
    return jnp.max(place[n : n + 1, :]).astype(jnp.int32)


def head_of(head):
    return slice(head * HEAD, (head + 1) * HEAD)


HEADS = [head_of(n) for n in range(LOCAL_HEADS)]


def whole_spec(shape):
    return pl.BlockSpec(shape, lambda i: (0,) * len(shape))


def trig_parts():
    omega = 10000.0 ** (-2.0 * np.arange(28) / 56.0)
    by_row = np.repeat(np.concatenate([np.zeros(8), omega, np.zeros(28)]), 2).astype(np.float32)
    by_col = np.repeat(np.concatenate([np.zeros(36), omega]), 2).astype(np.float32)
    lanes = np.arange(HEAD)
    sign = np.where(lanes % 2 == 0, -1.0, 1.0)
    blocks = []
    for omegas, count, mine in ((by_row, ROW_POS, lanes < 72), (by_col, WIDTH_TOK, lanes >= 72)):
        angle = (np.arange(count, dtype=np.float32)[:, None] * omegas[None, :]).astype(np.float64)
        blocks.append(np.concatenate([np.cos(angle) * mine, np.sin(angle) * sign * mine], axis=1))
    rest = np.concatenate(blocks).astype(np.float32)
    parts = []
    for _ in range(3):
        parts.append(rest.astype(jnp.bfloat16))
        rest = rest - parts[-1].astype(np.float32)
    return np.concatenate(parts, axis=1)


def qkv_kernel(place, *refs):
    given, (q, k, v, w_half), buffers, sems = refs[:9], refs[9:13], refs[13:-1], refs[-1]
    lat, w, trig, rows, shift, scale, q_gain, k_gain, half = buffers
    copy = lambda n, source, target: pltpu.make_async_copy(source, target, sems.at[n])
    weights = [copy(n, given[1].at[n], w.at[n]) for n in range(3)]
    small = [copy(n + 1, given[n], buffers[n]) for n in range(2, 8)]
    latents, half_out = copy(9, given[0], lat), copy(11, half, w_half)
    latents.start()
    for c in small:
        c.start()
    weights[0].start()

    for c in small:
        c.wait()
    at = lax.broadcasted_iota(jnp.int32, (ROW_POS + WIDTH_TOK, COUNT), 0)
    row_pos = lax.shift_right_logical(rows[...], 8)
    col_pos = jnp.bitwise_and(rows[...], WIDTH_TOK - 1) + ROW_POS
    hot = jnp.where((at == row_pos) | (at == col_pos), 1.0, 0.0).astype(jnp.bfloat16)
    turn = lax.dot_general(hot, trig[...], (((0,), (0,)), ((), ())), preferred_element_type=jnp.float32)
    turn = turn[:, : 2 * HEAD] + (turn[:, 2 * HEAD : 4 * HEAD] + turn[:, 4 * HEAD :])
    cosine, sine = turn[:, :HEAD], turn[:, HEAD:]
    even = lax.broadcasted_iota(jnp.int32, (COUNT, HEAD), 1) % 2 == 0

    latents.wait()
    weights[1].start()
    x = lat[...].astype(jnp.float32)
    centred = x - jnp.mean(x, axis=-1, keepdims=True)
    spread = jnp.mean(centred * centred, axis=-1, keepdims=True)
    y = centred * lax.rsqrt(spread + 1e-06) * (1.0 + scale[...]) + shift[...]
    normed = y.astype(jnp.bfloat16)

    def rotated(x, gain, factor):
        x = x * lax.rsqrt(jnp.mean(x * x, axis=-1, keepdims=True) + 1e-06) * gain[...]
        other = jnp.where(even, pltpu.roll(x, HEAD - 1, 1), pltpu.roll(x, 1, 1))
        x = x * cosine + other * sine
        return (x * factor if factor else x).astype(jnp.bfloat16)

    for n, (ref, gain, factor) in enumerate(((q, q_gain, SCALE), (k, k_gain, None), (v, None, None))):
        weights[n].wait()
        if n == 0:
            weights[2].start()
            part = pl.ds(pl.multiple_of(coordinate(place, 2) * SPLIT, SPLIT), SPLIT)
            half_in = copy(10, given[8].at[part], half)
            half_in.start()
        out = jnp.dot(normed, w[n], preferred_element_type=jnp.float32)
        for c in HEADS:
            x = out[:, c]
            ref[:, c] = x.astype(jnp.bfloat16) if gain is None else rotated(x, gain, factor)
        if n == 1:
            half_in.wait()
            half_out.start()
    half_out.wait()


def qkv_call(place, latents, w, rows, shift, scale, q_gain, k_gain, w_out):
    anywhere = pl.BlockSpec(memory_space=pl.ANY)
    row = lambda a: a.reshape(1, a.shape[0])
    args = [latents, w, jnp.asarray(trig_parts())]
    args += [row(a) for a in (rows, shift, scale, q_gain, k_gain)]
    half = (SPLIT, MODEL)
    return pl.pallas_call(
        qkv_kernel,
        in_specs=[FULL] + [anywhere] * 9,
        out_specs=[FULL] * 3 + [anywhere],
        out_shape=[jax.ShapeDtypeStruct((COUNT, WIDTH), jnp.bfloat16)] * 3
        + [jax.ShapeDtypeStruct(half, jnp.bfloat16)],
        scratch_shapes=[pltpu.VMEM(a.shape, a.dtype) for a in args]
        + [pltpu.VMEM(half, jnp.bfloat16), pltpu.SemaphoreType.DMA((12,))],
        compiler_params=params(60),
        cost_estimate=cost(2 * COUNT * MODEL * WIDTH * 3, 10 * MIB),
    )(place, *args, w_out)


def attend(q, pairs, state=None):
    scores = []
    for k, _ in pairs:
        s = lax.dot_general(q, k, (((1,), (1,)), ((), ())), preferred_element_type=jnp.float32)
        scores.append([s[:, at : at + HEAD] for at in range(0, s.shape[1], HEAD)])
    top = None
    for piece in sum(scores, []):
        top = piece if top is None else jnp.maximum(top, piece)
    top = jnp.broadcast_to(jnp.max(top, axis=1, keepdims=True), top.shape)
    if state is not None:
        top = jnp.maximum(top, state[1])
    total = None
    for pieces, (_, v) in zip(scores, pairs):
        p = [jnp.exp2(s - top).astype(jnp.bfloat16) for s in pieces]
        wide = jnp.concatenate([v, jnp.ones_like(v)], axis=1)
        part = jnp.dot(jnp.concatenate(p, axis=1), wide, preferred_element_type=jnp.float32)
        total = part if total is None else total + part
    num, den = total[:, :HEAD], total[:, HEAD:]
    if state is not None:
        keep = jnp.exp2(state[1] - top)
        num, den = num + keep * state[0], den + keep * state[2]
    return num, top, den


def store_state(refs, cols, result, rows=slice(None)):
    for ref, value in zip(refs, result):
        ref[rows, cols] = value


def load_state(refs, cols, rows=slice(None)):
    return [ref[rows, cols] for ref in refs]


def both(pair, cols):
    return [(ref[0, :, cols], ref[1, :, cols]) for ref in pair]


def near_kernel(q0, q1, k, v, text, own, right, left, *state):
    for c in HEADS:
        ring_pairs = both((right, left), c)
        first = [(k[:, c], v[:, c]), (text[0, :, c], text[1, :, c])]
        store_state(state, c, attend(q0[:, c], first + ring_pairs), slice(0, COUNT))
        second = both((own,), c) + ring_pairs
        store_state(state, c, attend(q1[:, c], second), slice(COUNT, 2 * COUNT))


def far_kernel(q0, q1, *refs):
    blocks, state = refs[:-3], refs[-3:]
    for c in HEADS:
        q = jnp.concatenate([q0[:, c], q1[:, c]], axis=0)
        store_state(state, c, attend(q, both(blocks, c)))


def next_kernel(q0, q1, *refs):
    blocks, given, state = refs[:-6], refs[-6:-3], refs[-3:]
    for c in HEADS:
        q = jnp.concatenate([q0[:, c], q1[:, c]], axis=0)
        store_state(state, c, attend(q, both(blocks, c), load_state(given, c)))


def state_shapes(rows):
    return [jax.ShapeDtypeStruct((rows, WIDTH), jnp.float32)] * 3


def attend_cost(blocks):
    return cost(blocks * COUNT * COUNT * WIDTH * 4, 6 * MIB, blocks * COUNT * COUNT * LOCAL_HEADS)


def attend_call(kernel, blocks, *args):
    call = pl.pallas_call(
        kernel,
        in_specs=[FULL] * len(args),
        out_specs=[FULL] * 3,
        out_shape=state_shapes(2 * COUNT),
        compiler_params=params(24),
        cost_estimate=attend_cost(blocks),
    )
    return list(call(*args))


def pack(num, top, den):
    log = (top + jnp.log2(den)).T[:EXTRA, :]
    row = lax.broadcasted_iota(jnp.int32, log.shape, 0)
    parts = jnp.zeros_like(log)
    for n in range(3):
        rounded = log.astype(jnp.bfloat16).astype(jnp.float32)
        parts = jnp.where(row == n, rounded, parts)
        log = log - rounded
    return jnp.concatenate([num * (1.0 / den), parts], axis=0).astype(jnp.bfloat16)


def unpack(message):
    value = message[:HALF, :].astype(jnp.float32)
    stats = message[HALF:, :].astype(jnp.float32)
    log = stats[0:1, :] + (stats[1:2, :] + stats[2:3, :])
    return value, jnp.broadcast_to(log, (HALF, HEAD)).T, 1.0


def merge(*states):
    top = states[0][1]
    for s in states[1:]:
        top = jnp.maximum(top, s[1])
    num, den = 0.0, 0.0
    for n, m, d in states:
        keep = jnp.exp2(m - top)
        num, den = num + keep * n, den + keep * d
    return num, top, den


def last_kernel(x0, x1, o0, o1, keys, values, *refs):
    message = refs[12]
    for block, (kept, sent) in enumerate(((x0, x1), (o0, o1))):
        given, state = refs[3 * block : 3 * block + 3], refs[6 + 3 * block : 9 + 3 * block]
        for c in HEADS:
            pairs = [(keys[:, c], values[:, c])]
            result = attend(sent[:, c], pairs, load_state(given, c, slice(COUNT, 2 * COUNT)))
            for n in range(2):
                part = pack(*[a[n * HALF : (n + 1) * HALF] for a in result])
                message[2 * block + n, :, c] = part
            store_state(state, c, attend(kept[:, c], pairs, load_state(given, c, slice(0, COUNT))))


def last_call(x0, x1, o0, o1, keys, values, far, near):
    message = jax.ShapeDtypeStruct((4, HALF + EXTRA, WIDTH), jnp.bfloat16)
    return pl.pallas_call(
        last_kernel,
        in_specs=[FULL] * 12,
        out_specs=[FULL] * 7,
        out_shape=state_shapes(COUNT) * 2 + [message],
        compiler_params=params(24),
        cost_estimate=attend_cost(4),
    )(x0, x1, o0, o1, keys, values, *far, *near)


def merge_kernel(place, *refs):
    message = refs[6]
    swap = jnp.bitwise_and(coordinate(place, 1), 1) == 1
    for block in range(2):
        state = refs[3 * block : 3 * block + 3]
        mine, other = refs[7 + 2 * block : 9 + 2 * block]
        for c in HEADS:
            halves = []
            for n in range(2):
                part = load_state(state, c, slice(n * HALF, (n + 1) * HALF))
                both_cores = merge(part, unpack(message[2 * block + n, :, c]))
                halves.append(pack(*both_cores).astype(jnp.float32))
            mine[:, c] = jnp.where(swap, halves[1], halves[0]).astype(jnp.bfloat16)
            other[:, c] = jnp.where(swap, halves[0], halves[1]).astype(jnp.bfloat16)


def merge_call(place, *args):
    return pl.pallas_call(
        merge_kernel,
        in_specs=[FULL] * 8,
        out_specs=[FULL] * 4,
        out_shape=[jax.ShapeDtypeStruct((HALF + EXTRA, WIDTH), jnp.bfloat16)] * 4,
        compiler_params=params(24),
        cost_estimate=cost(0, 4 * MIB),
    )(place, *args)


QUARTERS = ((0, 0), (1, 1), (1, 0), (0, 1))


def project_kernel(place, *refs):
    messages, (w, w_pair, w_core) = refs[:4], refs[4:7]
    outs, attn, full = refs[7:11], refs[11], refs[12]
    x, first = coordinate(place, 0), coordinate(place, 2) == 0
    high_y = lax.shift_right_logical(coordinate(place, 1), 1)
    for n in range(2):
        for head in range(LOCAL_HEADS):
            c = head_of(head)
            num, _, den = merge(*[unpack(m[:, c]) for m in messages[2 * n : 2 * n + 2]])
            attn[:, head_of(LOCAL_HEADS * n + head)] = (num * (1.0 / den)).astype(jnp.bfloat16)
    low = attn[:, WIDTH : WIDTH + SPLIT].astype(jnp.float32)
    high = attn[:, WIDTH + SPLIT :].astype(jnp.float32)
    by_x = jnp.where(first, low, high).astype(jnp.bfloat16)
    by_core = jnp.where(first, high, low).astype(jnp.bfloat16)
    for at in range(0, MODEL, 768):
        cols = slice(at, at + 768)
        total = jnp.dot(attn[:, :WIDTH], w[:, cols], preferred_element_type=jnp.float32)
        total += jnp.dot(by_x, w_pair[:, cols], preferred_element_type=jnp.float32)
        total += jnp.dot(by_core, w_core[:, cols], preferred_element_type=jnp.float32)
        full[:, cols] = total.astype(jnp.bfloat16)
    for out, (dy, dx) in zip(outs, QUARTERS):
        to = jnp.bitwise_xor(high_y, dy) * 2 + jnp.bitwise_xor(x, dx)
        out[...] = full[pl.ds(pl.multiple_of(to * ROWS, ROWS), ROWS), :]


def project_call(place, messages, weights):
    return pl.pallas_call(
        project_kernel,
        in_specs=[FULL] * 8,
        out_specs=[FULL] * 4,
        out_shape=[jax.ShapeDtypeStruct((ROWS, MODEL), jnp.bfloat16)] * 4,
        scratch_shapes=[
            pltpu.VMEM((HALF, 2 * WIDTH), jnp.bfloat16),
            pltpu.VMEM((HALF, MODEL), jnp.bfloat16),
        ],
        compiler_params=params(24),
        cost_estimate=cost(2 * COUNT * WIDTH * MODEL, 5 * MIB),
    )(place, *messages, *weights)


def put_kernel(offsets, place, *refs):
    out, sems = refs[-2:]
    x, y = coordinate(place, 0), coordinate(place, 1)
    copies = []
    for n, (flip, step) in enumerate(offsets):
        from_y = lax.rem(y + 4 - step, 4)
        quarter = lax.shift_right_logical(from_y, 1) * 2 + (1 - x if flip else x)
        at = jnp.bitwise_and(from_y, 1) * HALF + quarter * ROWS
        rows = pl.ds(pl.multiple_of(at, ROWS), ROWS)
        copies.append(pltpu.make_async_copy(refs[n], out.at[rows], sems.at[n]))
    for copy in copies:
        copy.start()
    for copy in copies:
        copy.wait()


def put_call(place, offsets, pieces, out=None):
    anywhere = pl.BlockSpec(memory_space=pl.ANY)
    count = len(pieces)
    more = [] if out is None else [out]
    return pl.pallas_call(
        functools.partial(put_kernel, offsets),
        in_specs=[FULL] * (count + 1) + [anywhere] * len(more),
        out_specs=anywhere,
        out_shape=jax.ShapeDtypeStruct((COUNT, MODEL), jnp.bfloat16),
        input_output_aliases={count + 1: 0} if more else {},
        scratch_shapes=[pltpu.SemaphoreType.DMA((count,))],
        compiler_params=params(24),
        cost_estimate=cost(0, 4 * MIB),
    )(place, *pieces, *more)


def ring(value, axis, step):
    size = SIZES[AXES.index(axis)]
    return lax.ppermute(value, axis, [(i, (i + step) % size) for i in range(size)])


def beside_y(value):
    return lax.ppermute(value, "y", [(i, i ^ 1) for i in range(4)])


def crossed(value, axes):
    return lax.ppermute(value, axes, [(i, 3 - i) for i in range(4)])


def shards(
    latents,
    token_rows,
    mod_shift,
    mod_scale,
    mod_gate,
    w_qkv,
    q_gain,
    k_gain,
    stale_kv,
    text_kv,
    w_out,
    b_out,
):
    after = lax.optimization_barrier
    x, y = lax.axis_index("x_hi"), lax.axis_index("y")
    place = jnp.stack([x, y, lax.axis_index("core")] + [0] * 5).astype(jnp.float32)
    place = jnp.broadcast_to(place[:, None], (8, HEAD))
    own = jnp.transpose(stale_kv, (1, 0, 2))
    r1, l1 = ring(own, "z", 1), ring(own, "z", -1)

    w = jnp.transpose(w_qkv, (1, 0, 2))
    q, k, v, w_half = qkv_call(
        place, latents, w, token_rows, mod_shift, mod_scale, q_gain, k_gain, w_out
    )
    w_pair = beside_y(w_half)
    q_core, q_x = ring(q, "core", 1), ring(q, "x_lo", 1)

    r1, l1, q = after((r1, l1, q))
    r2, l2 = ring(r1, "z", 1), ring(l1, "z", -1)
    text = jnp.transpose(text_kv, (1, 0, 2))
    near = attend_call(near_kernel, 8, q, q_core, k, v, text, own, r1, l1)

    q_x, near[2] = after((q_x, near[2]))
    q_both = ring(q_x, "core", 1)
    r2, near[0] = after((r2, near[0]))
    r3 = ring(r2, "z", 1)
    l2, near[1] = after((l2, near[1]))
    l3 = ring(l2, "z", -1)
    near = attend_call(next_kernel, 4, q, q_core, r2, l2, *near)
    far = attend_call(far_kernel, 10, q_x, q_both, own, r1, l1, r2, l2)

    r3, near[0], far[0] = after((r3, near[0], far[0]))
    far_k = ring(r3[0], "z", 1)
    l3, near[1], far[1] = after((l3, near[1], far[1]))
    far_v = ring(l3[1], "z", -1)
    far = attend_call(next_kernel, 4, q_x, q_both, r3, l3, *far)
    near = attend_call(next_kernel, 4, q, q_core, r3, l3, *near)

    far_k, far_v, near[0], far[0] = after((far_k, far_v, near[0], far[0]))
    *states, message = last_call(q_x, q_both, q, q_core, far_k, far_v, far, near)
    w_pair, message = after((w_pair, message))
    message = ring(message, "core", 1)
    x_mine, x_other, o_mine, o_other = merge_call(place, *states, message)
    from_both = lax.ppermute(
        x_other, ("x_lo", "y"), [(i, (1 - i // 4) * 4 + (i % 4 ^ 1)) for i in range(8)]
    )
    from_y, from_x = beside_y(o_other), ring(x_mine, "x_lo", 1)
    w_pair, o_mine = after((w_pair, o_mine))
    w_core = ring(w_pair, "core", 1)

    mine, both_ways, along_y, along_x = project_call(
        place, (o_mine, from_x, from_y, from_both), (w_out, w_pair, w_core)
    )
    parts = [
        lax.ppermute(both_ways, TENSOR, [(i, (i // 2 + 2) % 4 * 2 + (1 - i % 2)) for i in range(8)]),
        ring(along_y, "y", 2),
        ring(along_x, "x_hi", 1),
    ]
    start = y % 2 * HALF + (y // 2 * 2 + x) * ROWS
    rows = lax.dynamic_slice_in_dim(latents, start, ROWS, 0).astype(jnp.float32)
    total = mine.astype(jnp.float32)
    for part in parts:
        total = total + part.astype(jnp.float32)
    piece = (rows + mod_gate * (total + b_out)).astype(jnp.bfloat16)

    beside, two = ring(piece, "x_hi", 1), ring(piece, "y", 2)
    plus, minus = ring(piece, "y", 1), ring(piece, "y", -1)
    early = [
        ((0, 0), piece),
        ((1, 0), beside),
        ((0, 1), plus),
        ((0, -1), minus),
        ((0, 2), two),
    ]
    late = [
        ((1, 1), ring(beside, "y", 1)),
        ((1, -1), ring(beside, "y", -1)),
        ((1, 2), ring(two, "x_hi", 1)),
    ]
    out = put_call(place, [e[0] for e in early], [e[1] for e in early])
    out = put_call(place, [e[0] for e in late], [e[1] for e in late], out)
    return (out, jnp.stack([k, v], axis=1))


def solution(mesh):
    fine = Mesh(mesh.devices.reshape(SIZES), AXES)
    return jax.shard_map(
        shards,
        mesh=fine,
        in_specs=(
            P(PATCH, None),
            P(PATCH),
            P(),
            P(),
            P(),
            P(None, None, TENSOR),
            P(),
            P(),
            P(PATCH, None, TENSOR),
            P(None, None, TENSOR),
            P(TENSOR, None),
            P(),
        ),
        out_specs=(P(PATCH, None), P(PATCH, None, TENSOR)),
        check_vma=False,
    )
```

```python
import functools

import jax
import jax.numpy as jnp
import numpy as np
from jax import lax
from jax.experimental import pallas as pl
from jax.experimental.pallas import tpu as pltpu
from jax.sharding import Mesh
from jax.sharding import PartitionSpec as P

WIDTH_TOK = 256
ROW_POS = 8192 // WIDTH_TOK
HEAD = 128
LOCAL_HEADS = 3
WIDTH = HEAD * LOCAL_HEADS
COUNT = 256
TEXT = 512
MODEL = 3072
ROWS = COUNT // 8
AXES = ("x_lo", "z", "core", "y", "x_hi")
SIZES = (2, 8, 2, 4, 2)
PATCH = ("x_lo", "z", "core")
TENSOR = ("y", "x_hi")
SCALE = float(np.log2(np.e) / np.sqrt(128.0))
MIB = 1024 * 1024
EXTRA = 16
HALF = COUNT // 2
SPLIT = WIDTH // 2
FULL = pl.BlockSpec(memory_space=pltpu.VMEM)


def params(mib=48):
    return pltpu.CompilerParams(vmem_limit_bytes=mib * MIB)


def cost(flops, nbytes, exps=0):
    del flops, nbytes, exps
    return pl.CostEstimate(flops=1024, bytes_accessed=1024, transcendentals=0)


def coordinate(place, n):
    return jnp.max(place[n : n + 1, :]).astype(jnp.int32)


def head_of(head):
    return slice(head * HEAD, (head + 1) * HEAD)


HEADS = [head_of(n) for n in range(LOCAL_HEADS)]


def whole_spec(shape):
    return pl.BlockSpec(shape, lambda i: (0,) * len(shape))


def trig_parts():
    omega = 10000.0 ** (-2.0 * np.arange(28) / 56.0)
    by_row = np.repeat(np.concatenate([np.zeros(8), omega, np.zeros(28)]), 2).astype(np.float32)
    by_col = np.repeat(np.concatenate([np.zeros(36), omega]), 2).astype(np.float32)
    lanes = np.arange(HEAD)
    sign = np.where(lanes % 2 == 0, -1.0, 1.0)
    blocks = []
    for omegas, count, mine in ((by_row, ROW_POS, lanes < 72), (by_col, WIDTH_TOK, lanes >= 72)):
        angle = (np.arange(count, dtype=np.float32)[:, None] * omegas[None, :]).astype(np.float64)
        blocks.append(np.concatenate([np.cos(angle) * mine, np.sin(angle) * sign * mine], axis=1))
    rest = np.concatenate(blocks).astype(np.float32)
    parts = []
    for _ in range(3):
        parts.append(rest.astype(jnp.bfloat16))
        rest = rest - parts[-1].astype(np.float32)
    return np.concatenate(parts, axis=1)


def qkv_kernel(place, *refs):
    given, (q, k, v, w_half), buffers, sems = refs[:9], refs[9:13], refs[13:-1], refs[-1]
    lat, w, trig, rows, shift, scale, q_gain, k_gain, half = buffers
    copy = lambda n, source, target: pltpu.make_async_copy(source, target, sems.at[n])
    weights = [copy(n, given[1].at[n], w.at[n]) for n in range(3)]
    small = [copy(n + 1, given[n], buffers[n]) for n in range(2, 8)]
    latents, half_out = copy(9, given[0], lat), copy(11, half, w_half)
    latents.start()
    for c in small:
        c.start()
    weights[0].start()

    for c in small:
        c.wait()
    at = lax.broadcasted_iota(jnp.int32, (ROW_POS + WIDTH_TOK, COUNT), 0)
    row_pos = lax.shift_right_logical(rows[...], 8)
    col_pos = jnp.bitwise_and(rows[...], WIDTH_TOK - 1) + ROW_POS
    hot = jnp.where((at == row_pos) | (at == col_pos), 1.0, 0.0).astype(jnp.bfloat16)
    turn = lax.dot_general(hot, trig[...], (((0,), (0,)), ((), ())), preferred_element_type=jnp.float32)
    turn = turn[:, : 2 * HEAD] + (turn[:, 2 * HEAD : 4 * HEAD] + turn[:, 4 * HEAD :])
    cosine, sine = turn[:, :HEAD], turn[:, HEAD:]
    even = lax.broadcasted_iota(jnp.int32, (COUNT, HEAD), 1) % 2 == 0

    latents.wait()
    weights[1].start()
    x = lat[...].astype(jnp.float32)
    centred = x - jnp.mean(x, axis=-1, keepdims=True)
    spread = jnp.mean(centred * centred, axis=-1, keepdims=True)
    y = centred * lax.rsqrt(spread + 1e-06) * (1.0 + scale[...]) + shift[...]
    normed = y.astype(jnp.bfloat16)

    def rotated(x, gain, factor):
        x = x * lax.rsqrt(jnp.mean(x * x, axis=-1, keepdims=True) + 1e-06) * gain[...]
        other = jnp.where(even, pltpu.roll(x, HEAD - 1, 1), pltpu.roll(x, 1, 1))
        x = x * cosine + other * sine
        return (x * factor if factor else x).astype(jnp.bfloat16)

    for n, (ref, gain, factor) in enumerate(((q, q_gain, SCALE), (k, k_gain, None), (v, None, None))):
        weights[n].wait()
        if n == 0:
            weights[2].start()
            part = pl.ds(pl.multiple_of(coordinate(place, 2) * SPLIT, SPLIT), SPLIT)
            half_in = copy(10, given[8].at[part], half)
            half_in.start()
        out = jnp.dot(normed, w[n], preferred_element_type=jnp.float32)
        for c in HEADS:
            x = out[:, c]
            ref[:, c] = x.astype(jnp.bfloat16) if gain is None else rotated(x, gain, factor)
        if n == 1:
            half_in.wait()
            half_out.start()
    half_out.wait()


def qkv_call(place, latents, w, rows, shift, scale, q_gain, k_gain, w_out):
    anywhere = pl.BlockSpec(memory_space=pl.ANY)
    row = lambda a: a.reshape(1, a.shape[0])
    args = [latents, w, jnp.asarray(trig_parts())]
    args += [row(a) for a in (rows, shift, scale, q_gain, k_gain)]
    half = (SPLIT, MODEL)
    return pl.pallas_call(
        qkv_kernel,
        in_specs=[FULL] + [anywhere] * 9,
        out_specs=[FULL] * 3 + [anywhere],
        out_shape=[jax.ShapeDtypeStruct((COUNT, WIDTH), jnp.bfloat16)] * 3
        + [jax.ShapeDtypeStruct(half, jnp.bfloat16)],
        scratch_shapes=[pltpu.VMEM(a.shape, a.dtype) for a in args]
        + [pltpu.VMEM(half, jnp.bfloat16), pltpu.SemaphoreType.DMA((12,))],
        compiler_params=params(60),
        cost_estimate=cost(2 * COUNT * MODEL * WIDTH * 3, 10 * MIB),
    )(place, *args, w_out)


def attend(q, pairs, state=None):
    scores = []
    for k, _ in pairs:
        s = lax.dot_general(q, k, (((1,), (1,)), ((), ())), preferred_element_type=jnp.float32)
        scores.append([s[:, at : at + HEAD] for at in range(0, s.shape[1], HEAD)])
    top = None
    for piece in sum(scores, []):
        top = piece if top is None else jnp.maximum(top, piece)
    top = jnp.broadcast_to(jnp.max(top, axis=1, keepdims=True), top.shape)
    if state is not None:
        top = jnp.maximum(top, state[1])
    total = None
    for pieces, (_, v) in zip(scores, pairs):
        p = [jnp.exp2(s - top).astype(jnp.bfloat16) for s in pieces]
        wide = jnp.concatenate([v, jnp.ones_like(v)], axis=1)
        part = jnp.dot(jnp.concatenate(p, axis=1), wide, preferred_element_type=jnp.float32)
        total = part if total is None else total + part
    num, den = total[:, :HEAD], total[:, HEAD:]
    if state is not None:
        keep = jnp.exp2(state[1] - top)
        num, den = num + keep * state[0], den + keep * state[2]
    return num, top, den


def store_state(refs, cols, result, rows=slice(None)):
    for ref, value in zip(refs, result):
        ref[rows, cols] = value


def load_state(refs, cols, rows=slice(None)):
    return [ref[rows, cols] for ref in refs]


def both(pair, cols):
    return [(ref[0, :, cols], ref[1, :, cols]) for ref in pair]


def near_kernel(q0, q1, k, v, text, own, right, left, *state):
    for c in HEADS:
        ring_pairs = both((right, left), c)
        first = [(k[:, c], v[:, c]), (text[0, :, c], text[1, :, c])]
        store_state(state, c, attend(q0[:, c], first + ring_pairs), slice(0, COUNT))
        second = both((own,), c) + ring_pairs
        store_state(state, c, attend(q1[:, c], second), slice(COUNT, 2 * COUNT))


def far_kernel(q0, q1, *refs):
    blocks, state = refs[:-3], refs[-3:]
    for c in HEADS:
        q = jnp.concatenate([q0[:, c], q1[:, c]], axis=0)
        store_state(state, c, attend(q, both(blocks, c)))


def next_kernel(q0, q1, *refs):
    blocks, given, state = refs[:-6], refs[-6:-3], refs[-3:]
    for c in HEADS:
        q = jnp.concatenate([q0[:, c], q1[:, c]], axis=0)
        store_state(state, c, attend(q, both(blocks, c), load_state(given, c)))


def state_shapes(rows):
    return [jax.ShapeDtypeStruct((rows, WIDTH), jnp.float32)] * 3


def attend_cost(blocks):
    return cost(blocks * COUNT * COUNT * WIDTH * 4, 6 * MIB, blocks * COUNT * COUNT * LOCAL_HEADS)


def attend_call(kernel, blocks, *args):
    call = pl.pallas_call(
        kernel,
        in_specs=[FULL] * len(args),
        out_specs=[FULL] * 3,
        out_shape=state_shapes(2 * COUNT),
        compiler_params=params(24),
        cost_estimate=attend_cost(blocks),
    )
    return list(call(*args))


def pack(num, top, den):
    log = (top + jnp.log2(den)).T[:EXTRA, :]
    row = lax.broadcasted_iota(jnp.int32, log.shape, 0)
    parts = jnp.zeros_like(log)
    for n in range(3):
        rounded = log.astype(jnp.bfloat16).astype(jnp.float32)
        parts = jnp.where(row == n, rounded, parts)
        log = log - rounded
    return jnp.concatenate([num * (1.0 / den), parts], axis=0).astype(jnp.bfloat16)


def unpack(message):
    value = message[:HALF, :].astype(jnp.float32)
    stats = message[HALF:, :].astype(jnp.float32)
    log = stats[0:1, :] + (stats[1:2, :] + stats[2:3, :])
    return value, jnp.broadcast_to(log, (HALF, HEAD)).T, 1.0


def merge(*states):
    top = states[0][1]
    for s in states[1:]:
        top = jnp.maximum(top, s[1])
    num, den = 0.0, 0.0
    for n, m, d in states:
        keep = jnp.exp2(m - top)
        num, den = num + keep * n, den + keep * d
    return num, top, den


def last_kernel(x0, x1, o0, o1, keys, values, *refs):
    message = refs[12]
    for block, (kept, sent) in enumerate(((x0, x1), (o0, o1))):
        given, state = refs[3 * block : 3 * block + 3], refs[6 + 3 * block : 9 + 3 * block]
        for c in HEADS:
            pairs = [(keys[:, c], values[:, c])]
            result = attend(sent[:, c], pairs, load_state(given, c, slice(COUNT, 2 * COUNT)))
            for n in range(2):
                part = pack(*[a[n * HALF : (n + 1) * HALF] for a in result])
                message[2 * block + n, :, c] = part
            store_state(state, c, attend(kept[:, c], pairs, load_state(given, c, slice(0, COUNT))))


def last_call(x0, x1, o0, o1, keys, values, far, near):
    message = jax.ShapeDtypeStruct((4, HALF + EXTRA, WIDTH), jnp.bfloat16)
    return pl.pallas_call(
        last_kernel,
        in_specs=[FULL] * 12,
        out_specs=[FULL] * 7,
        out_shape=state_shapes(COUNT) * 2 + [message],
        compiler_params=params(24),
        cost_estimate=attend_cost(4),
    )(x0, x1, o0, o1, keys, values, *far, *near)


def merge_kernel(place, *refs):
    message = refs[6]
    swap = jnp.bitwise_and(coordinate(place, 1), 1) == 1
    for block in range(2):
        state = refs[3 * block : 3 * block + 3]
        mine, other = refs[7 + 2 * block : 9 + 2 * block]
        for c in HEADS:
            halves = []
            for n in range(2):
                part = load_state(state, c, slice(n * HALF, (n + 1) * HALF))
                both_cores = merge(part, unpack(message[2 * block + n, :, c]))
                halves.append(pack(*both_cores).astype(jnp.float32))
            mine[:, c] = jnp.where(swap, halves[1], halves[0]).astype(jnp.bfloat16)
            other[:, c] = jnp.where(swap, halves[0], halves[1]).astype(jnp.bfloat16)


def merge_call(place, *args):
    return pl.pallas_call(
        merge_kernel,
        in_specs=[FULL] * 8,
        out_specs=[FULL] * 4,
        out_shape=[jax.ShapeDtypeStruct((HALF + EXTRA, WIDTH), jnp.bfloat16)] * 4,
        compiler_params=params(24),
        cost_estimate=cost(0, 4 * MIB),
    )(place, *args)


QUARTERS = ((0, 0), (1, 1), (1, 0), (0, 1))


def project_kernel(place, *refs):
    messages, (w, w_pair, w_core) = refs[:4], refs[4:7]
    outs, attn, full = refs[7:11], refs[11], refs[12]
    x, first = coordinate(place, 0), coordinate(place, 2) == 0
    high_y = lax.shift_right_logical(coordinate(place, 1), 1)
    for n in range(2):
        for head in range(LOCAL_HEADS):
            c = head_of(head)
            num, _, den = merge(*[unpack(m[:, c]) for m in messages[2 * n : 2 * n + 2]])
            attn[:, head_of(LOCAL_HEADS * n + head)] = (num * (1.0 / den)).astype(jnp.bfloat16)
    low = attn[:, WIDTH : WIDTH + SPLIT].astype(jnp.float32)
    high = attn[:, WIDTH + SPLIT :].astype(jnp.float32)
    by_x = jnp.where(first, low, high).astype(jnp.bfloat16)
    by_core = jnp.where(first, high, low).astype(jnp.bfloat16)
    for at in range(0, MODEL, 768):
        cols = slice(at, at + 768)
        total = jnp.dot(attn[:, :WIDTH], w[:, cols], preferred_element_type=jnp.float32)
        total += jnp.dot(by_x, w_pair[:, cols], preferred_element_type=jnp.float32)
        total += jnp.dot(by_core, w_core[:, cols], preferred_element_type=jnp.float32)
        full[:, cols] = total.astype(jnp.bfloat16)
    for out, (dy, dx) in zip(outs, QUARTERS):
        to = jnp.bitwise_xor(high_y, dy) * 2 + jnp.bitwise_xor(x, dx)
        out[...] = full[pl.ds(pl.multiple_of(to * ROWS, ROWS), ROWS), :]


def project_call(place, messages, weights):
    return pl.pallas_call(
        project_kernel,
        in_specs=[FULL] * 8,
        out_specs=[FULL] * 4,
        out_shape=[jax.ShapeDtypeStruct((ROWS, MODEL), jnp.bfloat16)] * 4,
        scratch_shapes=[
            pltpu.VMEM((HALF, 2 * WIDTH), jnp.bfloat16),
            pltpu.VMEM((HALF, MODEL), jnp.bfloat16),
        ],
        compiler_params=params(24),
        cost_estimate=cost(2 * COUNT * WIDTH * MODEL, 5 * MIB),
    )(place, *messages, *weights)


def sum_kernel(mine, a, b, c, rows, gate, bias, out):
    total = mine[...].astype(jnp.float32) + a[...].astype(jnp.float32)
    total += b[...].astype(jnp.float32) + c[...].astype(jnp.float32)
    out[...] = (rows[...].astype(jnp.float32) + gate[...] * (total + bias[...])).astype(jnp.bfloat16)


def sum_call(mine, parts, rows, gate, bias):
    return pl.pallas_call(
        sum_kernel,
        in_specs=[FULL] * 7,
        out_specs=FULL,
        out_shape=jax.ShapeDtypeStruct((ROWS, MODEL), jnp.bfloat16),
        compiler_params=params(24),
        cost_estimate=cost(0, 2 * MIB),
    )(mine, *parts, rows, gate.reshape(1, MODEL), bias.reshape(1, MODEL))


def put_kernel(offsets, place, *refs):
    out, sems = refs[-2:]
    x, y = coordinate(place, 0), coordinate(place, 1)
    copies = []
    for n, (flip, step) in enumerate(offsets):
        from_y = lax.rem(y + 4 - step, 4)
        quarter = lax.shift_right_logical(from_y, 1) * 2 + (1 - x if flip else x)
        at = jnp.bitwise_and(from_y, 1) * HALF + quarter * ROWS
        rows = pl.ds(pl.multiple_of(at, ROWS), ROWS)
        copies.append(pltpu.make_async_copy(refs[n], out.at[rows], sems.at[n]))
    for copy in copies:
        copy.start()
    for copy in copies:
        copy.wait()


def put_call(place, offsets, pieces, out=None):
    anywhere = pl.BlockSpec(memory_space=pl.ANY)
    count = len(pieces)
    more = [] if out is None else [out]
    return pl.pallas_call(
        functools.partial(put_kernel, offsets),
        in_specs=[FULL] * (count + 1) + [anywhere] * len(more),
        out_specs=anywhere,
        out_shape=jax.ShapeDtypeStruct((COUNT, MODEL), jnp.bfloat16),
        input_output_aliases={count + 1: 0} if more else {},
        scratch_shapes=[pltpu.SemaphoreType.DMA((count,))],
        compiler_params=params(24),
        cost_estimate=cost(0, 4 * MIB),
    )(place, *pieces, *more)


def ring(value, axis, step):
    size = SIZES[AXES.index(axis)]
    return lax.ppermute(value, axis, [(i, (i + step) % size) for i in range(size)])


def beside_y(value):
    return lax.ppermute(value, "y", [(i, i ^ 1) for i in range(4)])


def crossed(value, axes):
    return lax.ppermute(value, axes, [(i, 3 - i) for i in range(4)])


def shards(
    latents,
    token_rows,
    mod_shift,
    mod_scale,
    mod_gate,
    w_qkv,
    q_gain,
    k_gain,
    stale_kv,
    text_kv,
    w_out,
    b_out,
):
    after = lax.optimization_barrier
    x, y = lax.axis_index("x_hi"), lax.axis_index("y")
    place = jnp.stack([x, y, lax.axis_index("core")] + [0] * 5).astype(jnp.float32)
    place = jnp.broadcast_to(place[:, None], (8, HEAD))
    own = jnp.transpose(stale_kv, (1, 0, 2))
    r1, l1 = ring(own, "z", 1), ring(own, "z", -1)

    w = jnp.transpose(w_qkv, (1, 0, 2))
    q, k, v, w_half = qkv_call(
        place, latents, w, token_rows, mod_shift, mod_scale, q_gain, k_gain, w_out
    )
    w_pair = beside_y(w_half)
    q_core, q_x = ring(q, "core", 1), ring(q, "x_lo", 1)

    r1, l1, q = after((r1, l1, q))
    r2, l2 = ring(r1, "z", 1), ring(l1, "z", -1)
    text = jnp.transpose(text_kv, (1, 0, 2))
    near = attend_call(near_kernel, 8, q, q_core, k, v, text, own, r1, l1)

    q_x, near[2] = after((q_x, near[2]))
    q_both = ring(q_x, "core", 1)
    r2, near[0] = after((r2, near[0]))
    r3 = ring(r2, "z", 1)
    l2, near[1] = after((l2, near[1]))
    l3 = ring(l2, "z", -1)
    near = attend_call(next_kernel, 4, q, q_core, r2, l2, *near)
    far = attend_call(far_kernel, 10, q_x, q_both, own, r1, l1, r2, l2)

    r3, near[0], far[0] = after((r3, near[0], far[0]))
    far_k = ring(r3[0], "z", 1)
    l3, near[1], far[1] = after((l3, near[1], far[1]))
    far_v = ring(l3[1], "z", -1)
    far = attend_call(next_kernel, 4, q_x, q_both, r3, l3, *far)
    near = attend_call(next_kernel, 4, q, q_core, r3, l3, *near)

    far_k, far_v, near[0], far[0] = after((far_k, far_v, near[0], far[0]))
    *states, message = last_call(q_x, q_both, q, q_core, far_k, far_v, far, near)
    w_pair, message = after((w_pair, message))
    message = ring(message, "core", 1)
    x_mine, x_other, o_mine, o_other = merge_call(place, *states, message)
    from_both = lax.ppermute(
        x_other, ("x_lo", "y"), [(i, (1 - i // 4) * 4 + (i % 4 ^ 1)) for i in range(8)]
    )
    from_y, from_x = beside_y(o_other), ring(x_mine, "x_lo", 1)
    w_pair, o_mine = after((w_pair, o_mine))
    w_core = ring(w_pair, "core", 1)

    mine, both_ways, along_y, along_x = project_call(
        place, (o_mine, from_x, from_y, from_both), (w_out, w_pair, w_core)
    )
    parts = [
        lax.ppermute(both_ways, TENSOR, [(i, (i // 2 + 2) % 4 * 2 + (1 - i % 2)) for i in range(8)]),
        ring(along_y, "y", 2),
        ring(along_x, "x_hi", 1),
    ]
    start = y % 2 * HALF + (y // 2 * 2 + x) * ROWS
    rows = lax.dynamic_slice_in_dim(latents, start, ROWS, 0)
    piece = sum_call(mine, parts, rows, mod_gate, b_out)

    beside, two = ring(piece, "x_hi", 1), ring(piece, "y", 2)
    plus, minus = ring(piece, "y", 1), ring(piece, "y", -1)
    early = [
        ((0, 0), piece),
        ((1, 0), beside),
        ((0, 1), plus),
        ((0, -1), minus),
        ((0, 2), two),
    ]
    late = [
        ((1, 1), ring(beside, "y", 1)),
        ((1, -1), ring(beside, "y", -1)),
        ((1, 2), ring(two, "x_hi", 1)),
    ]
    out = put_call(place, [e[0] for e in early], [e[1] for e in early])
    out = put_call(place, [e[0] for e in late], [e[1] for e in late], out)
    return (out, jnp.stack([k, v], axis=1))


def solution(mesh):
    fine = Mesh(mesh.devices.reshape(SIZES), AXES)
    return jax.shard_map(
        shards,
        mesh=fine,
        in_specs=(
            P(PATCH, None),
            P(PATCH),
            P(),
            P(),
            P(),
            P(None, None, TENSOR),
            P(),
            P(),
            P(PATCH, None, TENSOR),
            P(None, None, TENSOR),
            P(TENSOR, None),
            P(),
        ),
        out_specs=(P(PATCH, None), P(PATCH, None, TENSOR)),
        check_vma=False,
    )
```
